256 devices in a mesh: section: 4 (over x_hi, core), seq: 8 (over z), fsdp: 8 (over y, x_lo).
Axes of the slice: x: 4 (x_hi: 2, x_lo: 2; x = x_hi * 2 + x_lo), y: 4, z: 8, core: 2. Of those that a mesh axis runs over, the one named last changes fastest.
Arguments:
- student_input: bfloat16 [2048, 64], P('seq'), may hold values from -6 to 6
- previous_latent: bfloat16 [2048, 64], P('seq'), may hold values from -6 to 6
- score_noise: bfloat16 [2048, 64], P('seq'), may hold values from -6 to 6
- timesteps: int32 [3], replicated, may hold values from 50 to 949
- modulation: float32 [4, 5, 5120], P('section'), may hold values from -3 to 3
- in_weight: bfloat16 [3, 64, 5120], replicated, may hold values from -4 to 4
- qkv_weight: bfloat16 [3, 5120, 3, 3072], P(None, 'seq', None, 'fsdp'), may hold values from -1 to 1
- out_weight: bfloat16 [3, 5120, 3072], P(None, 'seq', 'fsdp'), may hold values from -0.109375 to 0.109375
- head_weight: bfloat16 [3, 5120, 64], replicated, may hold values from -0.078125 to 0.078125
- kv_cache: bfloat16 [4, 2048, 2, 3072], P('section', 'seq', None, 'fsdp'), may hold values from -60 to 60
- saved_features: bfloat16 [2048, 5120], P(('seq', 'fsdp')), may hold values from -6 to 6
Outputs:
- student_group: float32 [2048, 64], P(('seq', 'fsdp'))
- dmd_grad: float32 [2048, 64], P(('seq', 'fsdp'))
- head_grad: float32 [5120, 64], P(('seq', 'fsdp'))
The draws below stay inside these ranges and needn't reach their ends.
All inputs are finite; a program needn't handle non-finite values.
Results may differ from the reference program's by a relative error of at most 0.015.
Values may be sent and summed in bfloat16 or wider, within the bound.
No kernel may reach another device: no remote copies, remote signals or barrier semaphores. Data moves between devices by JAX's collectives and lax.ppermute only.
A program may use at most 128 MiB of HBM per device.

```python
import jax
import jax.numpy as jnp
from jax import lax

D = 5120
HEAD_DIM = 128
HEADS = 24
LATENT = 64
GROUP = 2048
FEAT = 3072


def draw_in_weight(key, part):
    key = jax.random.fold_in(key, 11)
    values = jax.random.truncated_normal(key, -6.0, 6.0, (3, LATENT, D), jnp.float32) * LATENT ** (-0.5)
    return values.astype(jnp.bfloat16)


def draw_qkv_weight(key, part):
    key = jax.random.fold_in(key, 13)
    values = jax.random.truncated_normal(key, -6.0, 6.0, (3, D, 3, FEAT), jnp.float32)
    return (values * D ** (-0.5)).astype(jnp.bfloat16)


def draw_kv_cache(key, part):
    key = jax.random.fold_in(key, 17)
    first = jax.random.fold_in(key, 0)
    values = jax.random.truncated_normal(first, -6.0, 6.0, (4, GROUP, 2, HEADS, HEAD_DIM), jnp.float32)
    return values.reshape(4, GROUP, 2, FEAT).astype(jnp.bfloat16)


def block_scale(key, shape, shards, low, largest):
    loudness = 1.0
    for dim, shards_of in shards:
        heights = jax.random.uniform(jax.random.fold_in(jax.random.fold_in(key, 6), dim), (shards_of,), jnp.float32, low / len(shards), largest / len(shards))
        loudness = loudness * jnp.repeat(jnp.exp(heights), shape[dim] // shards_of).reshape((-1,) + (1,) * (len(shape) - 1 - dim))
    return loudness


def gaussian(rng, dims, scale, most, cuts=(), held_as=jnp.bfloat16):
    array = scale * jax.random.normal(rng, dims, jnp.float32)
    if cuts:
        array = array * block_scale(rng, dims, cuts, -0.22, 0.18)
    return jnp.clip(array, -most, most).astype(held_as)


def setup_inputs(seed: int = 0) -> dict:
    arg_keys = jax.random.split(jax.random.key(seed), 12)
    student_input = gaussian(arg_keys[0], (GROUP, LATENT), 1.0, 6.0, ((0, 8),))
    previous_latent = gaussian(arg_keys[1], (GROUP, LATENT), 1.0, 6.0, ((0, 8),))
    score_noise = gaussian(arg_keys[2], (GROUP, LATENT), 1.0, 6.0, ((0, 8),))
    timesteps = jax.random.randint(arg_keys[3], (3,), 50, 950).astype(jnp.int32)
    modulation = gaussian(arg_keys[4], (4, 5, D), 0.5, 3.0, ((0, 4),), jnp.float32)
    in_weight = draw_in_weight(jax.random.fold_in(arg_keys[11], 71), 0)
    qkv_weight = draw_qkv_weight(jax.random.fold_in(arg_keys[11], 71), 0)
    out_weight = gaussian(arg_keys[7], (3, D, FEAT), FEAT ** -0.5, 0.109375, ((1, 8), (2, 8)))
    head_weight = gaussian(arg_keys[8], (3, D, LATENT), D ** -0.5, 0.078125)
    kv_cache = draw_kv_cache(jax.random.fold_in(arg_keys[11], 71), 0)
    saved_features = gaussian(arg_keys[10], (GROUP, D), 1.0, 6.0, ((0, 64),))
    return dict(student_input=student_input, previous_latent=previous_latent, score_noise=score_noise, timesteps=timesteps, modulation=modulation, in_weight=in_weight, qkv_weight=qkv_weight, out_weight=out_weight, head_weight=head_weight, kv_cache=kv_cache, saved_features=saved_features)


guidance_scale = 5.0

def noise_levels(steps):
    remain = 1.0 - steps.astype(jnp.float32) / 1000.0
    return 5.0 * remain / (1.0 + 4.0 * remain)

def normalize(values):
    centre = values - lax.optimization_barrier(jnp.mean(values, axis=-1, keepdims=True))
    spread = lax.optimization_barrier(jnp.mean(centre * centre, axis=-1, keepdims=True))
    return centre * lax.rsqrt(spread + 1e-06)

def head_attention(operands):
    queries, key_rows, value_rows = operands
    scores = jnp.dot(queries, key_rows.T, preferred_element_type=jnp.float32) * HEAD_DIM ** (-0.5)
    weights = jnp.exp(scores - lax.optimization_barrier(jnp.max(scores, axis=1, keepdims=True)))
    totals = lax.optimization_barrier(jnp.sum(weights, axis=1))
    weighted = jnp.dot(weights.astype(jnp.bfloat16), value_rows, preferred_element_type=jnp.float32)
    return weighted / totals[:, None]

def heads_first(values):
    return values.reshape(-1, HEADS, HEAD_DIM).transpose(1, 0, 2)

def section_output(latent, noise_level, shifts, embed_weight, attn_weight, output_weight, final_weight, context):
    hidden = jnp.dot(latent, embed_weight, preferred_element_type=jnp.float32)
    normed = (normalize(hidden) * (1.0 + shifts[1]) + shifts[0]).astype(jnp.bfloat16)
    projected = jnp.dot(normed, attn_weight.reshape(D, 3 * FEAT), preferred_element_type=jnp.float32)
    projected = projected.reshape(GROUP, 3, FEAT).astype(jnp.bfloat16)
    queries = heads_first(projected[:, 0])
    key_rows = heads_first(jnp.concatenate([context[:, 0], projected[:, 1]], axis=0))
    value_rows = heads_first(jnp.concatenate([context[:, 1], projected[:, 2]], axis=0))
    attended = lax.map(head_attention, (queries, key_rows, value_rows))
    attended = attended.transpose(1, 0, 2).reshape(GROUP, FEAT).astype(jnp.bfloat16)
    mixed_sum = jnp.dot(attended, output_weight.T, preferred_element_type=jnp.float32)
    residual = hidden + shifts[2] * mixed_sum
    head_in = (normalize(residual) * (1.0 + shifts[4]) + shifts[3]).astype(jnp.bfloat16)
    velocity = jnp.dot(head_in, final_weight, preferred_element_type=jnp.float32)
    return latent.astype(jnp.float32) - noise_level * velocity

def reference(student_input, previous_latent, score_noise, timesteps, modulation, in_weight, qkv_weight, out_weight, head_weight, kv_cache, saved_features):
    levels = noise_levels(timesteps)
    noised = ((1.0 - levels[1]) * previous_latent.astype(jnp.float32) + levels[1] * score_noise.astype(jnp.float32)).astype(jnp.bfloat16)
    results = []
    for section in range(4):
        model_index = (0, 1, 1, 2)[section]
        latent = student_input if section == 0 else noised
        noise_level = levels[0] if section == 0 else levels[1]
        results.append(section_output(latent, noise_level, modulation[section], in_weight[model_index], qkv_weight[model_index], out_weight[model_index], head_weight[model_index], kv_cache[section]))
    student_group = results[0]
    teacher_estimate = results[2] + guidance_scale * (results[1] - results[2])
    dmd_grad = results[3] - teacher_estimate
    velocity_grad = (-levels[2] * dmd_grad).astype(jnp.bfloat16)
    head_grad = jnp.dot(saved_features.T, velocity_grad, preferred_element_type=jnp.float32)
    return (student_group, dmd_grad, head_grad)
```

```python
import functools

import jax
import jax.numpy as jnp
from jax import lax
from jax.experimental import pallas as pl
from jax.experimental.pallas import tpu as pltpu
from jax.sharding import PartitionSpec as P

HEAD_DIM = 128
LOG2E = 1.4426950408889634
guidance_scale = 5.0
bf16 = jnp.bfloat16
f32 = jnp.float32


def noise_levels(steps):
    remain = 1.0 - steps.astype(f32) / 1000.0
    return 5.0 * remain / (1.0 + 4.0 * remain)


def select_model(stacked, model_index):
    return lax.dynamic_index_in_dim(stacked, model_index, 0, keepdims=False)


def exchange(blocks, axis):
    return lax.all_to_all(blocks, axis, 0, 0, tiled=True)


def share(block, axis, count):
    return exchange(jnp.broadcast_to(block[None], (count,) + block.shape), axis)


def ring(block, axis, count, split):
    half = count // 2
    up = [(i, (i + 1) % count) for i in range(count)]
    down = [(i, (i - 1) % count) for i in range(count)]
    behind, ahead = [block], [block]
    for _ in range(half - 1):
        behind.append(lax.ppermute(behind[-1], axis, up))
        ahead.append(lax.ppermute(ahead[-1], axis, down))
    size = block.shape[split] // 2
    first = lax.ppermute(lax.slice_in_dim(behind[-1], 0, size, axis=split), axis, up)
    second = lax.ppermute(lax.slice_in_dim(ahead[-1], size, 2 * size, axis=split), axis, down)
    return behind, ahead[1:], first, second


def attention_kernel(heads, where_ref, lat_ref, a_ref, *refs):
    context_refs, out_ref = refs[:-1], refs[-1]
    feat = heads * HEAD_DIM
    factors = a_ref[...].astype(f32)
    count, _, width = factors.shape
    table = factors[:, :8].reshape(count * 8, width).astype(bf16)
    shift = factors[0, 8:9]
    queries_here = out_ref.shape[0]

    def project(block, first, last):
        latents = block[: count * 8]
        scale = jnp.sum(block[count * 8 :].astype(f32).T, axis=1, keepdims=True)
        plain = lax.dot_general(
            latents, table[:, first:last], (((0,), (0,)), ((), ())), preferred_element_type=f32
        )
        return plain * scale + shift[:, first:last]

    queries = (project(lat_ref[where_ref[0]], 0, feat) * (HEAD_DIM ** (-0.5) * LOG2E)).astype(bf16)

    def update(carry, keys, values):
        new = []
        for h in range(heads):
            top, total, weighted = carry[h]
            cols = slice(h * HEAD_DIM, (h + 1) * HEAD_DIM)
            scores = lax.dot_general(
                keys[:, cols], queries[:, cols], (((1,), (1,)), ((), ())), preferred_element_type=f32
            )
            new_top = jnp.maximum(top, jnp.max(scores, axis=0, keepdims=True))
            weights = jnp.exp2(scores - new_top)
            keep = jnp.exp2(top - new_top)
            total = total * keep + jnp.sum(weights, axis=0, keepdims=True)
            weighted = weighted * keep + lax.dot_general(
                values[:, cols], weights.astype(bf16), (((0,), (0,)), ((), ())), preferred_element_type=f32
            )
            new.append((new_top, total, weighted))
        return tuple(new)

    def current_step(i, carry):
        both = project(lat_ref[i], feat, 3 * feat).astype(bf16)
        return update(carry, both[:, :feat], both[:, feat:])

    carry = tuple(
        (
            jnp.full((1, queries_here), -1e30, f32),
            jnp.zeros((1, queries_here), f32),
            jnp.zeros((HEAD_DIM, queries_here), f32),
        )
        for _ in range(heads)
    )
    carry = lax.fori_loop(0, lat_ref.shape[0], current_step, carry)
    for ref in context_refs:
        carry = update(carry, ref[0], ref[1])
    for h in range(heads):
        _, total, weighted = carry[h]
        out_ref[:, h * HEAD_DIM : (h + 1) * HEAD_DIM] = (weighted / total).T.astype(bf16)


def head_kernel(count, where_ref, lat_ref, embed_ref, gate_ref, head_ref, aux_ref, *refs):
    out_ref = refs[-1]
    weight_refs = refs[: count]
    att_refs = refs[count:-1]
    me_seq, me_fsdp = where_ref[0], where_ref[1]
    half = count // 2
    def block_rows(f):
        rows = [att_refs[i][f] for i in range(half)]
        rows += [att_refs[half][f], att_refs[half + 1][f]]
        rows += [att_refs[half + 2 + i][f] for i in range(half - 1)]
        return jnp.concatenate(rows, axis=0)

    distance = list(range(half)) + [half] + [-(i + 1) for i in range(half - 1)]
    owners = [lax.rem(me_seq - d + 2 * count, count) for d in distance]
    mixed = None
    for k in range(count):
        f = lax.rem(me_fsdp - k + count, count)
        part = lax.dot_general(
            block_rows(f), weight_refs[k][...], (((1,), (1,)), ((), ())), preferred_element_type=f32
        )
        mixed = part if mixed is None else mixed + part
    latents = jnp.concatenate([lat_ref[o] for o in owners], axis=0)
    hidden = jnp.dot(latents, embed_ref[...], preferred_element_type=f32)
    residual = hidden + gate_ref[...] * mixed
    centre = jnp.mean(residual, axis=1, keepdims=True)
    residual = residual - centre
    spread = jnp.sum(residual * residual, axis=1, keepdims=True)
    values = lax.dot_general(
        residual.astype(bf16), head_ref[...], (((1,), (1,)), ((), ())), preferred_element_type=f32
    )
    lanes = lax.broadcasted_iota(jnp.int32, values.shape, 1)
    values = jnp.where(lanes == 64, centre, jnp.where(lanes == 65, spread, values))
    size = lat_ref.shape[1]
    for n, o in enumerate(owners):
        out_ref[o, :size] = values[n * size : (n + 1) * size]
        out_ref[o, size:] = aux_ref[...]


def per_device(
    student_input,
    previous_latent,
    score_noise,
    timesteps,
    modulation,
    in_weight,
    qkv_weight,
    out_weight,
    head_weight,
    kv_cache,
    saved_features,
):
    section, me_seq, me_fsdp = (lax.axis_index(a) for a in ("section", "seq", "fsdp"))
    sections, n_seq, n_fsdp = (lax.axis_size(a) for a in ("section", "seq", "fsdp"))
    where = jnp.stack([me_seq, me_fsdp]).astype(jnp.int32)
    model_index = section - (section >= 2).astype(jnp.int32)
    levels = noise_levels(timesteps)
    is_student = section == 0
    noised = (
        (1.0 - levels[1]) * previous_latent.astype(f32) + levels[1] * score_noise.astype(f32)
    ).astype(bf16)
    latent = jnp.where(is_student, student_input, noised)
    rows, latent_dim = latent.shape
    width = in_weight.shape[2]
    shifts = modulation[0]
    part = qkv_weight.shape[1]
    feat = qkv_weight.shape[3]
    heads = feat // HEAD_DIM
    piece = rows // n_fsdp

    context = kv_cache[0].transpose(1, 0, 2)
    ctx_behind, ctx_ahead, ctx_first, ctx_second = ring(context, "seq", n_seq, 1)
    output_weight = select_model(out_weight, model_index)
    output_weights = [output_weight] + [
        lax.ppermute(output_weight, "fsdp", [(i, (i + k) % n_fsdp) for i in range(n_fsdp)])
        for k in range(1, n_fsdp)
    ]

    embed_weight = select_model(in_weight, model_index)
    embed = embed_weight.astype(f32)
    row_mean = jnp.mean(embed, axis=1, keepdims=True)
    embed_here = lax.dynamic_slice_in_dim(embed_weight, me_seq * part, part, 1)
    shifts_here = lax.dynamic_slice_in_dim(shifts, me_seq * part, part, 1)
    centred = ((embed_here.astype(f32) - row_mean) * (1.0 + shifts_here[1])).astype(bf16)
    group = latent_dim // n_seq
    folded = jnp.concatenate(
        [
            centred.reshape(n_seq, group, part),
            jnp.broadcast_to(shifts_here[0].astype(bf16), (n_seq, 1, part)),
            jnp.zeros((n_seq, 15 - group, part), bf16),
        ],
        axis=1,
    ).reshape(n_seq * 16, part)
    attn_weight = select_model(qkv_weight, model_index).transpose(1, 0, 2)
    table = jnp.concatenate(
        [jnp.dot(folded, attn_weight[i], preferred_element_type=f32) for i in range(3)], axis=1
    )
    table = exchange(table.astype(bf16).reshape(n_seq, 16, 3 * feat), "seq")
    table = jnp.sum(table.astype(f32), axis=0).astype(bf16)
    table = share(table, "seq", n_seq)

    hidden = jnp.dot(latent, embed_weight, preferred_element_type=f32)
    hidden = hidden - jnp.mean(hidden, axis=1, keepdims=True)
    inverse = lax.rsqrt(jnp.mean(hidden * hidden, axis=1) + 1e-06)
    inverse_hi = lax.reduce_precision(inverse, 8, 7)
    inverse_mid = lax.reduce_precision(inverse - inverse_hi, 8, 7)
    inverse_lo = inverse - inverse_hi - inverse_mid
    packed = jnp.concatenate(
        [
            latent.T,
            jnp.stack([inverse_hi, inverse_mid, inverse_lo]).astype(bf16),
            jnp.zeros((13, rows), bf16),
        ],
        axis=0,
    )
    latents = share(packed, "seq", n_seq)

    vmem = pl.BlockSpec(memory_space=pltpu.VMEM)
    smem = pl.BlockSpec(memory_space=pltpu.SMEM)
    context_blocks = ctx_behind + [ctx_first, ctx_second] + ctx_ahead
    attended = pl.pallas_call(
        functools.partial(attention_kernel, heads),
        out_shape=jax.ShapeDtypeStruct((rows, feat), bf16),
        in_specs=[smem] + [vmem] * (2 + len(context_blocks)),
        out_specs=vmem,
        compiler_params=pltpu.CompilerParams(vmem_limit_bytes=48 * 1024 * 1024),
    )(where, latents, table, *context_blocks)

    attended = exchange(attended.reshape(n_fsdp, piece, feat), "fsdp")
    att_behind, att_ahead, att_first, att_second = ring(attended, "seq", n_seq, 1)
    att_blocks = att_behind + [att_first, att_second] + att_ahead

    head = select_model(head_weight, model_index)
    head_here = lax.dynamic_slice_in_dim(head, me_seq * part, part, 0).T
    scaled_head = (head_here.astype(f32) * (1.0 + shifts_here[4])).astype(bf16)
    head_sum = jnp.sum(scaled_head.astype(f32), axis=1)
    head_shift = jnp.sum(head_here.astype(f32) * shifts_here[3], axis=1)
    aux = jnp.zeros((8, 128), f32).at[0, :latent_dim].set(head_sum).at[1, :latent_dim].set(head_shift)
    padded_head = jnp.concatenate([scaled_head, jnp.zeros((128 - latent_dim, part), bf16)], axis=0)
    group_latents = lax.dynamic_slice_in_dim(latents, me_fsdp * piece, piece, 2)[
        :, :latent_dim
    ].transpose(0, 2, 1)
    partials = pl.pallas_call(
        functools.partial(head_kernel, n_seq),
        out_shape=jax.ShapeDtypeStruct((n_seq, piece + 8, 128), f32),
        in_specs=[smem] + [vmem] * (5 + n_fsdp + len(att_blocks)),
        out_specs=vmem,
        compiler_params=pltpu.CompilerParams(vmem_limit_bytes=48 * 1024 * 1024),
    )(
        where,
        group_latents,
        embed_here,
        shifts_here[2:3],
        padded_head,
        aux,
        *output_weights,
        *att_blocks,
    )
    partials = jnp.broadcast_to(partials[None], (sections,) + partials.shape)
    partials = exchange(partials.reshape((sections * n_seq,) + partials.shape[2:]), ("section", "seq"))
    partials = partials.reshape(sections, n_seq, piece + 8, 128)
    values = partials[:, :, :piece, :latent_dim]
    means = partials[:, :, :piece, latent_dim]
    spreads = partials[:, :, :piece, latent_dim + 1]
    sums = partials[:, :, piece, :latent_dim]
    consts = jnp.sum(partials[:, :, piece + 1, :latent_dim], axis=1)
    offsets = means - jnp.mean(means, axis=1, keepdims=True)
    linear = jnp.sum(values + offsets[..., None] * sums[:, :, None, :], axis=1)
    variance = (jnp.sum(spreads, axis=1) + part * jnp.sum(offsets * offsets, axis=1)) / width
    velocity = linear * lax.rsqrt(variance + 1e-06)[..., None] + consts[:, None, :]
    own_student = lax.dynamic_slice_in_dim(student_input, me_fsdp * piece, piece, 0).astype(f32)
    own_noised = lax.dynamic_slice_in_dim(noised, me_fsdp * piece, piece, 0).astype(f32)
    student_group = own_student - levels[0] * velocity[0]
    scored = own_noised[None] - levels[1] * velocity[1:]
    teacher_estimate = scored[1] + guidance_scale * (scored[0] - scored[1])
    dmd_grad = scored[2] - teacher_estimate
    velocity_grad = (-levels[2] * dmd_grad).astype(bf16)

    share_width = width // (n_seq * n_fsdp)
    features = saved_features.reshape(piece, n_seq, n_fsdp, share_width).transpose(2, 1, 0, 3)
    features = exchange(features, "fsdp")
    features = features.transpose(1, 0, 2, 3).reshape(n_seq, rows, share_width)
    grads = share(velocity_grad, "fsdp", n_fsdp).reshape(rows, latent_dim)
    partial_grad = lax.dot_general(
        jnp.broadcast_to(grads[None], (n_seq, rows, latent_dim)),
        features,
        (((1,), (1,)), ((0,), (0,))),
        preferred_element_type=f32,
    )
    head_grad = jnp.sum(exchange(partial_grad, "seq"), axis=0).T
    return (student_group, dmd_grad, head_grad)


def solution(mesh):
    placed = (
        P("seq", None),
        P("seq", None),
        P("seq", None),
        P(),
        P("section", None, None),
        P(),
        P(None, "seq", None, "fsdp"),
        P(None, "seq", "fsdp"),
        P(),
        P("section", "seq", None, "fsdp"),
        P(("seq", "fsdp"), None),
    )
    return jax.shard_map(
        per_device,
        mesh=mesh,
        in_specs=placed,
        out_specs=(P(("seq", "fsdp"), None), P(("seq", "fsdp"), None), P(("seq", "fsdp"), None)),
        check_vma=False,
    )
```

```python
import functools

import jax
import jax.numpy as jnp
from jax import lax
from jax.experimental import pallas as pl
from jax.experimental.pallas import tpu as pltpu
from jax.sharding import PartitionSpec as P

HEAD_DIM = 128
LOG2E = 1.4426950408889634
guidance_scale = 5.0
bf16 = jnp.bfloat16
f32 = jnp.float32
VMEM = pl.BlockSpec(memory_space=pltpu.VMEM)
SMEM = pl.BlockSpec(memory_space=pltpu.SMEM)
ROOM = pltpu.CompilerParams(vmem_limit_bytes=48 * 1024 * 1024)


def noise_levels(steps):
    remain = 1.0 - steps.astype(f32) / 1000.0
    return 5.0 * remain / (1.0 + 4.0 * remain)


def select_model(stacked, model_index):
    return lax.dynamic_index_in_dim(stacked, model_index, 0, keepdims=False)


def exchange(blocks, axis):
    return lax.all_to_all(blocks, axis, 0, 0, tiled=True)


def ring(block, axis, count, split):
    up = [(i, (i + 1) % count) for i in range(count)]
    down = [(i, (i - 1) % count) for i in range(count)]
    behind, ahead = [block], [block]
    for _ in range(count // 2 - 1):
        behind.append(lax.ppermute(behind[-1], axis, up))
        ahead.append(lax.ppermute(ahead[-1], axis, down))
    size = block.shape[split] // 2
    first = lax.ppermute(lax.slice_in_dim(behind[-1], 0, size, axis=split), axis, up)
    second = lax.ppermute(lax.slice_in_dim(ahead[-1], size, 2 * size, axis=split), axis, down)
    return behind + ahead[1:] + [first, second]


def dot(a, b, over):
    return lax.dot_general(a, b, ((over[0], over[1]), ((), ())), preferred_element_type=f32)


def prepare_kernel(
    where_ref, levels_ref, embed_ref, weight_ref, shifts_ref, student_ref, previous_ref, noise_ref, out_ref
):
    pieces, size, _ = out_ref.shape
    latent_dim, width = embed_ref.shape[1:]
    parts, depth, feat = weight_ref.shape[1:]
    rows = student_ref.shape[1]
    level = levels_ref[1]
    noised = (1.0 - level) * previous_ref[...].astype(f32) + level * noise_ref[...].astype(f32)
    latents = jnp.where(where_ref[3] == 0, student_ref[...].astype(f32), noised.astype(bf16).astype(f32))

    step = 1024
    row_sum = jnp.zeros((latent_dim, 1), f32)
    for first in range(0, width, step):
        row_sum += jnp.sum(embed_ref[0, :, first : first + step].astype(f32), axis=1, keepdims=True)
    row_mean = row_sum / width

    here = pl.ds(pl.multiple_of(where_ref[1] * depth, 128), depth)
    centred = (embed_ref[0, :, here].astype(f32) - row_mean) * (1.0 + shifts_ref[1:2, here])
    group = latent_dim // pieces
    filler = jnp.concatenate(
        [shifts_ref[0:1, here], jnp.zeros((size - group - 1, depth), f32)], axis=0
    )
    folded = jnp.concatenate(
        [
            x
            for i in range(pieces)
            for x in (centred[i * group : (i + 1) * group], filler)
        ],
        axis=0,
    ).astype(bf16)
    for i in range(parts):
        table = dot(folded, weight_ref[0, i], ((1,), (0,))).astype(bf16)
        out_ref[:, :, i * feat : (i + 1) * feat] = table.reshape(pieces, size, feat)

    mean = jnp.sum(row_mean * latents, axis=0, keepdims=True)
    plain = latents.astype(bf16)
    spread = jnp.zeros((1, rows), f32)
    for first in range(0, width, step):
        hidden = dot(embed_ref[0, :, first : first + step], plain, ((0,), (0,))) - mean
        spread += jnp.sum(hidden * hidden, axis=0, keepdims=True)
    inverse = lax.rsqrt(spread / width + 1e-06)
    high = inverse.astype(bf16).astype(f32)
    middle = (inverse - high).astype(bf16).astype(f32)
    low = inverse - high - middle
    line = lax.broadcasted_iota(jnp.int32, (size, rows), 0)
    tail = jnp.where(line == 0, high, jnp.where(line == 1, middle, jnp.where(line == 2, low, 0.0)))
    blocks = [plain[i * size : (i + 1) * size] for i in range(latent_dim // size)] + [tail.astype(bf16)]
    for n, block in enumerate(blocks):
        first = parts * feat + n * rows
        out_ref[:, :, first : first + rows] = jnp.broadcast_to(block[None], (pieces, size, rows))


def total_kernel(in_ref, out_ref):
    total = jnp.sum(in_ref[:, :, : out_ref.shape[2]].astype(f32), axis=0).astype(bf16)
    out_ref[...] = jnp.broadcast_to(total[None], out_ref.shape)


def fold_keys(heads, carry, queries, keys, values):
    scores = [dot(keys(h), queries[:, h * HEAD_DIM : (h + 1) * HEAD_DIM], ((1,), (1,))) for h in range(heads)]
    new = []
    for h in range(heads):
        top, total, weighted = carry[h]
        new_top = jnp.maximum(top, jnp.max(scores[h], axis=0, keepdims=True))
        weights = jnp.exp2(scores[h] - new_top)
        keep = jnp.exp2(top - new_top)
        total = total * keep + jnp.sum(weights, axis=0, keepdims=True)
        weighted = weighted * keep + dot(values(h), weights.astype(bf16), ((0,), (0,)))
        new.append((new_top, total, weighted))
    return tuple(new)


def current_kernel(heads, where_ref, packed_ref, table_ref, query_ref, state_ref, held_ref):
    feat = heads * HEAD_DIM
    count, size, width = table_ref.shape
    rows = query_ref.shape[0]
    group = 8
    factors = table_ref[...].astype(f32)
    table = factors[:, :group].reshape(count * group, width).astype(bf16)
    shift = factors[0, group : group + 1]
    lines = count * group // size

    def project(i, first, last):
        latents = jnp.concatenate(
            [packed_ref[i, :, width + n * rows : width + (n + 1) * rows] for n in range(lines)], axis=0
        )
        scale = packed_ref[i, :, width + lines * rows : width + (lines + 1) * rows].astype(f32)
        scale = jnp.sum(scale.T, axis=1, keepdims=True)
        return dot(latents, table[:, first:last], ((0,), (0,))) * scale + shift[:, first:last]

    queries = (project(where_ref[1], 0, feat) * (HEAD_DIM ** (-0.5) * LOG2E)).astype(bf16)
    query_ref[...] = queries

    def fill(i, _):
        at = pl.ds(pl.multiple_of(i * rows, rows), rows)
        held_ref[at, :] = project(i, feat, 3 * feat).astype(bf16)
        return 0

    lax.fori_loop(0, count, fill, 0)
    carry = tuple(
        (jnp.full((1, rows), -1e30, f32), jnp.zeros((1, rows), f32), jnp.zeros((HEAD_DIM, rows), f32))
        for _ in range(heads)
    )
    step = 2 * rows

    def current(i, carry):
        at = pl.ds(pl.multiple_of(i * step, step), step)
        return fold_keys(
            heads,
            carry,
            queries,
            lambda h: held_ref[at, h * HEAD_DIM : (h + 1) * HEAD_DIM],
            lambda h: held_ref[at, feat + h * HEAD_DIM : feat + (h + 1) * HEAD_DIM],
        )

    carry = lax.fori_loop(0, count * rows // step, current, carry)
    for h in range(heads):
        state_ref[h, :HEAD_DIM] = carry[h][2]
        state_ref[h, HEAD_DIM : HEAD_DIM + 8] = jnp.broadcast_to(carry[h][0], (8, rows))
        state_ref[h, HEAD_DIM + 8 : HEAD_DIM + 16] = jnp.broadcast_to(carry[h][1], (8, rows))


def context_kernel(heads, query_ref, state_ref, *refs):
    context_refs, out_ref = refs[:-1], refs[-1]
    rows = query_ref.shape[0]
    queries = query_ref[...]
    carry = tuple(
        (
            state_ref[h, HEAD_DIM : HEAD_DIM + 1],
            state_ref[h, HEAD_DIM + 8 : HEAD_DIM + 9],
            state_ref[h, :HEAD_DIM],
        )
        for h in range(heads)
    )
    taken, held = [], 0
    for ref in context_refs:
        taken.append(ref)
        held += ref.shape[1]
        if held == 2 * rows:
            carry = fold_keys(
                heads,
                carry,
                queries,
                lambda h: jnp.concatenate([r[0, :, h * HEAD_DIM : (h + 1) * HEAD_DIM] for r in taken], axis=0),
                lambda h: jnp.concatenate([r[1, :, h * HEAD_DIM : (h + 1) * HEAD_DIM] for r in taken], axis=0),
            )
            taken, held = [], 0
    for h in range(heads):
        _, total, weighted = carry[h]
        attended = (weighted / total).T.astype(bf16)
        out_ref[:, :, h * HEAD_DIM : (h + 1) * HEAD_DIM] = jnp.broadcast_to(
            attended[None], (out_ref.shape[0], rows, HEAD_DIM)
        )


def halves(value):
    high = value.astype(bf16).astype(f32)
    return high, value - high


def head_kernel(sections, where_ref, packed_ref, embed_ref, shifts_ref, head_ref, att_ref, *refs):
    weight_refs, out_ref = refs[:-1], refs[-1]
    n_fsdp, rows = att_ref.shape[:2]
    latent_dim = embed_ref.shape[0]
    size = packed_ref.shape[1]
    width = packed_ref.shape[2] - rows * (latent_dim // size + 1)
    mixed = None
    for f in range(n_fsdp):
        whole = [ref[f] for ref in weight_refs[:-2]]
        whole.append(weight_refs[-2][f] if f < n_fsdp // 2 else weight_refs[-1][f - n_fsdp // 2])
        part = dot(att_ref[f], jnp.concatenate(whole, axis=0), ((1,), (1,)))
        mixed = part if mixed is None else mixed + part
    latents = jnp.concatenate(
        [
            packed_ref[where_ref[1], :, width + n * rows : width + (n + 1) * rows]
            for n in range(latent_dim // size)
        ],
        axis=0,
    )
    residual = dot(latents, embed_ref[...], ((0,), (0,))) + shifts_ref[2:3] * mixed
    centre = jnp.mean(residual, axis=1, keepdims=True)
    residual = residual - centre
    spread = jnp.sum(residual * residual, axis=1, keepdims=True)
    plain_head = head_ref[...].astype(f32)
    head = (plain_head * (1.0 + shifts_ref[4:5])).astype(bf16)
    padded = jnp.concatenate([head, jnp.zeros_like(head)], axis=0)
    values = dot(residual.astype(bf16), padded, ((1,), (1,)))
    lanes = lax.broadcasted_iota(jnp.int32, values.shape, 1)
    for n, column in enumerate(halves(centre) + halves(spread)):
        values = jnp.where(lanes == latent_dim + n, column, values)
    values = values.astype(bf16)
    sums = jnp.sum(head.astype(f32), axis=1, keepdims=True)
    consts = jnp.sum(plain_head * shifts_ref[3:4], axis=1, keepdims=True)
    place = lax.broadcasted_iota(jnp.int32, (latent_dim, 128), 1)
    extra = jnp.zeros((latent_dim, 128), f32)
    for n, column in enumerate(halves(sums) + halves(consts)):
        extra = jnp.where(place == n, column, extra)
    extra = jnp.concatenate([extra, jnp.zeros_like(extra)], axis=0).T[:16].astype(bf16)
    piece = rows // n_fsdp
    for f in range(n_fsdp):
        for s in range(sections):
            out_ref[s * n_fsdp + f, :piece] = values[f * piece : (f + 1) * piece]
            out_ref[s * n_fsdp + f, piece:] = extra


def estimate_kernel(sections, width, levels_ref, partial_ref, student_ref, noised_ref, group_ref, grad_ref, out_ref):
    piece, latent_dim = student_ref.shape
    count = partial_ref.shape[0] // sections
    estimates = []
    for p in range(sections):
        blocks = [partial_ref[p * count + i].astype(f32) for i in range(count)]

        def column(b, n):
            at = latent_dim + n
            return b[:piece, at : at + 1] + b[:piece, at + 1 : at + 2]

        def line(b, n):
            at = piece + n
            return b[at : at + 1, :latent_dim] + b[at + 1 : at + 2, :latent_dim]

        means = [column(b, 0) for b in blocks]
        mean = sum(means) / count
        linear, spread, shift = 0.0, 0.0, 0.0
        for b, m in zip(blocks, means):
            offset = m - mean
            linear += b[:piece, :latent_dim] + offset * line(b, 0)
            spread += column(b, 2) + (width // count) * (offset * offset)
            shift += line(b, 2)
        velocity = linear * lax.rsqrt(spread / width + 1e-06) + shift
        latent = (student_ref if p == 0 else noised_ref)[...].astype(f32)
        estimates.append(latent - levels_ref[0 if p == 0 else 1] * velocity)
    group_ref[...] = estimates[0]
    teacher = estimates[2] + guidance_scale * (estimates[1] - estimates[2])
    grad = estimates[3] - teacher
    grad_ref[...] = grad
    velocity_grad = -levels_ref[2] * grad
    padded = jnp.concatenate([velocity_grad, jnp.zeros_like(velocity_grad)], axis=1).astype(bf16)
    out_ref[...] = jnp.broadcast_to(padded[None], out_ref.shape)


def gradient_kernel(grad_ref, feature_ref, out_ref):
    count, latent_dim, width = out_ref.shape
    grads = grad_ref[...].reshape(-1, grad_ref.shape[2])
    for first, last in ((0, feature_ref.shape[2]), (feature_ref.shape[2], count * width)):
        rows = feature_ref.shape[1] // 2
        part = feature_ref[:, :rows] if first == 0 else feature_ref[:, rows:]
        part = part.reshape(-1, feature_ref.shape[2])
        product = dot(grads, part, ((0,), (0,)))[:latent_dim]
        if first == 0:
            joined = product
        else:
            joined = jnp.concatenate([joined, product], axis=1)
    for i in range(count):
        out_ref[i] = joined[:, i * width : (i + 1) * width]


def per_device(
    student_input,
    previous_latent,
    score_noise,
    timesteps,
    modulation,
    in_weight,
    qkv_weight,
    out_weight,
    head_weight,
    kv_cache,
    saved_features,
):
    section, me_seq, me_fsdp = (lax.axis_index(a) for a in ("section", "seq", "fsdp"))
    sections, n_seq, n_fsdp = (lax.axis_size(a) for a in ("section", "seq", "fsdp"))
    model_index = section - (section >= 2).astype(jnp.int32)
    where = jnp.stack([model_index, me_seq, me_fsdp, section]).astype(jnp.int32)
    levels = noise_levels(timesteps)
    rows, latent_dim = student_input.shape
    width = in_weight.shape[2]
    depth, feat = qkv_weight.shape[1], qkv_weight.shape[3]
    heads = feat // HEAD_DIM
    piece = rows // n_fsdp
    shifts = modulation[0]
    slot = depth // n_fsdp

    context_blocks = ring(kv_cache[0].transpose(1, 0, 2), "seq", n_seq, 1)

    packed_width = 3 * feat + (latent_dim // 16 + 1) * rows
    packed = pl.pallas_call(
        prepare_kernel,
        grid_spec=pltpu.PrefetchScalarGridSpec(
            num_scalar_prefetch=1,
            grid=(1,),
            in_specs=[
                SMEM,
                pl.BlockSpec((1, latent_dim, width), lambda i, w: (w[0], 0, 0)),
                pl.BlockSpec((1, 3, depth, feat), lambda i, w: (w[0], 0, 0, 0)),
                VMEM,
                VMEM,
                VMEM,
                VMEM,
            ],
            out_specs=VMEM,
        ),
        out_shape=jax.ShapeDtypeStruct((n_seq, 16, packed_width), bf16),
        compiler_params=ROOM,
    )(
        where,
        levels,
        in_weight,
        qkv_weight.transpose(0, 2, 1, 3),
        shifts,
        student_input.T,
        previous_latent.T,
        score_noise.T,
    )
    weight_blocks = select_model(out_weight, model_index).reshape(n_fsdp, slot, feat)
    feature_blocks = saved_features.reshape(piece, n_seq, n_fsdp, slot).transpose(2, 0, 1, 3)
    feature_blocks = feature_blocks.reshape(n_fsdp, piece, n_seq * slot)
    spare = jnp.zeros((n_fsdp, piece, 2 * feat - n_seq * slot), bf16)
    aside = jnp.concatenate(
        [
            weight_blocks,
            feature_blocks[:, :, :feat],
            jnp.concatenate([feature_blocks[:, :, feat:], spare], axis=2),
        ],
        axis=1,
    )
    aside, packed = lax.optimization_barrier((aside, packed))
    aside = exchange(aside, "fsdp")
    features = aside[:, slot:]
    weight_ring = ring(aside[:, :slot], "seq", n_seq, 0)
    packed = exchange(packed, "seq")
    table = pl.pallas_call(
        total_kernel,
        in_specs=[VMEM],
        out_specs=VMEM,
        out_shape=jax.ShapeDtypeStruct((n_seq, 16, 3 * feat), bf16),
        compiler_params=ROOM,
    )(packed)
    table = exchange(table, "seq")
    queries, state = pl.pallas_call(
        functools.partial(current_kernel, heads),
        out_shape=(
            jax.ShapeDtypeStruct((rows, feat), bf16),
            jax.ShapeDtypeStruct((heads, HEAD_DIM + 16, rows), f32),
        ),
        in_specs=[SMEM] + [VMEM] * 2,
        out_specs=(VMEM, VMEM),
        scratch_shapes=[pltpu.VMEM((n_seq * rows, 2 * feat), bf16)],
        compiler_params=ROOM,
    )(where, packed, table)
    attended = pl.pallas_call(
        functools.partial(context_kernel, heads),
        out_shape=jax.ShapeDtypeStruct((n_fsdp, rows, feat), bf16),
        in_specs=[VMEM] * (2 + len(context_blocks)),
        out_specs=VMEM,
        compiler_params=ROOM,
    )(queries, state, *context_blocks)
    attended = exchange(attended, "fsdp")

    def columns(array):
        cut = array.reshape(array.shape[0], n_seq, n_fsdp, slot)
        cut = lax.dynamic_index_in_dim(cut, me_fsdp, 2, keepdims=False)
        cut = lax.dynamic_slice_in_dim(jnp.concatenate([cut, cut], axis=1), me_seq, n_seq, 1)
        half = n_seq // 2
        order = [0] + [n_seq - d for d in range(1, half)] + list(range(1, half + 1))
        return jnp.concatenate([cut[:, d] for d in order], axis=1)

    embed_here = columns(select_model(in_weight, model_index))
    head_here = columns(select_model(head_weight.transpose(0, 2, 1), model_index))
    shifts_here = columns(shifts)
    partials = pl.pallas_call(
        functools.partial(head_kernel, sections),
        out_shape=jax.ShapeDtypeStruct((sections * n_fsdp, piece + 16, 128), bf16),
        in_specs=[SMEM] + [VMEM] * (5 + len(weight_ring)),
        out_specs=VMEM,
        compiler_params=ROOM,
    )(where, packed, embed_here, shifts_here, head_here, attended, *weight_ring)
    partials = exchange(partials, ("section", "fsdp"))

    noised = (
        (1.0 - levels[1]) * previous_latent.astype(f32) + levels[1] * score_noise.astype(f32)
    ).astype(bf16)
    own_student = lax.dynamic_slice_in_dim(student_input, me_fsdp * piece, piece, 0)
    own_noised = lax.dynamic_slice_in_dim(noised, me_fsdp * piece, piece, 0)
    student_group, dmd_grad, grads = pl.pallas_call(
        functools.partial(estimate_kernel, sections, width),
        out_shape=(
            jax.ShapeDtypeStruct((piece, latent_dim), f32),
            jax.ShapeDtypeStruct((piece, latent_dim), f32),
            jax.ShapeDtypeStruct((n_fsdp, piece, 2 * latent_dim), bf16),
        ),
        in_specs=[SMEM] + [VMEM] * 3,
        out_specs=(VMEM, VMEM, VMEM),
    )(levels, partials, own_student, own_noised)
    grads = exchange(grads, "fsdp")
    partial_grad = pl.pallas_call(
        gradient_kernel,
        out_shape=jax.ShapeDtypeStruct((n_seq, latent_dim, slot), f32),
        in_specs=[VMEM] * 2,
        out_specs=VMEM,
    )(grads, features)
    head_grad = jnp.sum(exchange(partial_grad, "seq"), axis=0).T
    return (student_group, dmd_grad, head_grad)


def solution(mesh):
    placed = (
        P("seq", None),
        P("seq", None),
        P("seq", None),
        P(),
        P("section", None, None),
        P(),
        P(None, "seq", None, "fsdp"),
        P(None, "seq", "fsdp"),
        P(),
        P("section", "seq", None, "fsdp"),
        P(("seq", "fsdp"), None),
    )
    return jax.shard_map(
        per_device,
        mesh=mesh,
        in_specs=placed,
        out_specs=(P(("seq", "fsdp"), None), P(("seq", "fsdp"), None), P(("seq", "fsdp"), None)),
        check_vma=False,
    )
```

```python
import functools

import jax
import jax.numpy as jnp
from jax import lax
from jax.experimental import pallas as pl
from jax.experimental.pallas import tpu as pltpu
from jax.sharding import PartitionSpec as P

HEAD_DIM = 128
LOG2E = 1.4426950408889634
guidance_scale = 5.0
bf16 = jnp.bfloat16
f32 = jnp.float32


def run(kernel, where, outs, *operands, picked=(), scratch=(), raw=False):
    def spec(shape, pick=False):
        zeros = (0,) * (len(shape) - 1)
        if pick:
            return pl.BlockSpec((1,) + tuple(shape[1:]), lambda i, w: (w[0],) + zeros)
        return pl.BlockSpec(tuple(shape), lambda i, w: (0,) + zeros)

    in_specs = [
        pl.BlockSpec(memory_space=pltpu.SMEM)
        if x.ndim == 1
        else pl.BlockSpec(memory_space=pl.ANY)
        if raw
        else spec(x.shape, n in picked)
        for n, x in enumerate(operands)
    ]
    result = pl.pallas_call(
        kernel,
        grid_spec=pltpu.PrefetchScalarGridSpec(
            num_scalar_prefetch=1,
            grid=(1,),
            in_specs=in_specs,
            out_specs=tuple(spec(shape) for shape, _ in outs),
            scratch_shapes=list(scratch),
        ),
        out_shape=tuple(jax.ShapeDtypeStruct(shape, dtype) for shape, dtype in outs),
        compiler_params=pltpu.CompilerParams(vmem_limit_bytes=52 * 1024 * 1024),
    )(where, *operands)
    return result[0] if len(outs) == 1 else result


def together(value, *others):
    return lax.optimization_barrier((value,) + others)[0]


def noise_levels(steps):
    remain = 1.0 - steps.astype(f32) / 1000.0
    return 5.0 * remain / (1.0 + 4.0 * remain)


def select_model(stacked, model_index):
    return lax.dynamic_index_in_dim(stacked, model_index, 0, keepdims=False)


def exchange(blocks, axis):
    return lax.all_to_all(blocks, axis, 0, 0, tiled=True)


class Ring:
    def __init__(self, block, axis, count, split, split_at=None):
        self.split_at = split_at
        self.axis, self.split, self.half = axis, split, count // 2
        self.up = [(i, (i + 1) % count) for i in range(count)]
        self.down = [(i, (i - 1) % count) for i in range(count)]
        self.behind, self.ahead, self.last = [block], [block], []

    def step(self):
        self.behind.append(lax.ppermute(self.behind[-1], self.axis, self.up))
        self.ahead.append(lax.ppermute(self.ahead[-1], self.axis, self.down))

    def ends(self):
        return self.behind[-1], self.ahead[-1]

    def finish(self):
        while len(self.behind) < self.half:
            self.step()
        total = self.behind[0].shape[self.split]
        size = total // 2 if self.split_at is None else self.split_at
        first = lax.slice_in_dim(self.behind[-1], 0, size, axis=self.split)
        second = lax.slice_in_dim(self.ahead[-1], size, total, axis=self.split)
        self.last = [lax.ppermute(first, self.axis, self.up), lax.ppermute(second, self.axis, self.down)]

    def blocks(self):
        return self.behind + self.ahead[1:] + self.last


def dot(a, b, over):
    return lax.dot_general(a, b, ((over[0], over[1]), ((), ())), preferred_element_type=f32)


def prepare_kernel(
    where_ref, steps_ref, embed_ref, weight_ref, shifts_ref, student_ref, previous_ref, noise_ref, context_ref, out_ref
):
    latent_dim, width = embed_ref.shape[1:]
    parts, depth, feat = weight_ref.shape[1:]
    rows = student_ref.shape[1]
    out_ref[: 2 * rows] = context_ref[...].reshape(2 * rows, feat)
    level = noise_levels(jnp.full((1, rows), steps_ref[1], jnp.int32))
    noised = (1.0 - level) * previous_ref[...].astype(f32) + level * noise_ref[...].astype(f32)
    latents = jnp.where(where_ref[3] == 0, student_ref[...].astype(f32), noised.astype(bf16).astype(f32))

    step = 1024
    row_sum = jnp.zeros((latent_dim, 1), f32)
    for first in range(0, width, step):
        row_sum += jnp.sum(embed_ref[0, :, first : first + step].astype(f32), axis=1, keepdims=True)
    row_mean = row_sum / width

    here = pl.ds(pl.multiple_of(where_ref[1] * depth, 128), depth)
    centred = (embed_ref[0, :, here].astype(f32) - row_mean) * (1.0 + shifts_ref[1, :, here])
    shift = jnp.broadcast_to(shifts_ref[0, :, here], (16, depth))
    folded = jnp.concatenate([centred, shift], axis=0).astype(bf16)
    tail = 2 * rows + parts * latent_dim
    lines = []
    for i in range(parts):
        table = dot(folded, weight_ref[0, i], ((1,), (0,)))
        at = 2 * rows + i * latent_dim
        out_ref[at : at + latent_dim] = table[:latent_dim].astype(bf16)
        lines += [table[latent_dim : latent_dim + 1, n : n + 128] for n in range(0, feat, 128)]

    mean = jnp.sum(row_mean * latents, axis=0, keepdims=True)
    plain = latents.astype(bf16)
    spread = jnp.zeros((1, rows), f32)
    for first in range(0, width, step):
        hidden = dot(embed_ref[0, :, first : first + step], plain, ((0,), (0,))) - mean
        spread += jnp.sum(hidden * hidden, axis=0, keepdims=True)
    inverse = lax.rsqrt(spread / width + 1e-06)
    high = inverse.astype(bf16).astype(f32)
    middle = (inverse - high).astype(bf16).astype(f32)
    low = inverse - high - middle
    line = lax.broadcasted_iota(jnp.int32, (16, rows), 0)
    scales = jnp.where(line == 0, high, jnp.where(line == 1, middle, jnp.where(line == 2, low, 0.0)))
    out_ref[tail : tail + latent_dim, :rows] = plain
    out_ref[tail + latent_dim :, :rows] = scales.astype(bf16)
    spare = jnp.zeros((latent_dim + 16 - len(lines), 128), f32)
    out_ref[tail:, rows:] = jnp.concatenate(lines + [spare], axis=0).astype(bf16)


def aside_kernel(where_ref, weight_ref, feature_ref, out_ref):
    count, lines, feat = out_ref.shape
    rows, width = feature_ref.shape
    slot = weight_ref.shape[1] // count
    part = width // count
    out_ref[:, :slot] = weight_ref[0].reshape(count, slot, feat)
    spare = jnp.zeros((rows, 2 * feat - part), bf16)
    for j in range(count):
        pieces = [feature_ref[:, s * part + j * slot : s * part + (j + 1) * slot] for s in range(count)]
        joined = jnp.concatenate(pieces + [spare], axis=1)
        out_ref[j, slot : slot + rows] = joined[:, :feat]
        out_ref[j, slot + rows :] = joined[:, feat:]


def columns_kernel(where_ref, embed_ref, head_ref, shifts_ref, embed_out, head_out, shifts_out):
    count = 8
    part = embed_ref.shape[2] // count
    slot = part // count
    half = count // 2
    order = [0] + [count - d for d in range(1, half)] + list(range(1, half + 1))
    for f in range(count):

        @pl.when(where_ref[2] == f)
        def _(f=f):
            sources = [(embed_ref.at[0], embed_out), (head_ref.at[0], head_out)]
            sources += [(shifts_ref.at[i], shifts_out.at[i]) for i in range(shifts_ref.shape[0])]
            for source, target in sources:
                pieces = []
                for d in order:
                    owner = lax.rem(where_ref[1] + d, count)
                    block = source[:, pl.ds(pl.multiple_of(owner * part, 128), part)]
                    pieces.append(block[:, f * slot : (f + 1) * slot])
                target[...] = jnp.concatenate(pieces, axis=1)


def fold_keys(heads, carry, queries, keys, values):
    scores = [dot(keys(h), queries[:, h * HEAD_DIM : (h + 1) * HEAD_DIM], ((1,), (1,))) for h in range(heads)]
    new = []
    for h in range(heads):
        top, total, weighted = carry[h]
        new_top = jnp.maximum(top, jnp.max(scores[h], axis=0, keepdims=True))
        weights = jnp.exp2(scores[h] - new_top)
        keep = jnp.exp2(top - new_top)
        total = total * keep + jnp.sum(weights, axis=0, keepdims=True)
        weighted = weighted * keep + dot(values(h), weights.astype(bf16), ((0,), (0,)))
        new.append((new_top, total, weighted))
    return tuple(new)


def attention_kernel(heads, latent_dim, where_ref, *refs):
    n_blocks = len(refs) - 4
    block_refs, (out_ref, all_ref, held_ref, sems) = refs[:n_blocks], refs[n_blocks:]
    count, lines, feat = all_ref.shape
    rows = out_ref.shape[1]
    copies = []
    for n, ref in enumerate(block_refs):
        if n < count:
            target = all_ref.at[n, pl.ds(0, ref.shape[0])]
        else:
            target = all_ref.at[count - 1, pl.ds(lines - ref.shape[0], ref.shape[0])]
        copies.append(pltpu.make_async_copy(ref, target, sems.at[n]))
    for copy in copies:
        copy.start()
    for copy in copies:
        copy.wait()

    tail = 2 * rows + 3 * latent_dim
    parts = [slice(2 * rows + i * latent_dim, 2 * rows + (i + 1) * latent_dim) for i in range(3)]
    tables = [sum(all_ref[n, at].astype(f32) for n in range(count)).astype(bf16) for at in parts]
    shift = sum(all_ref[n, tail : tail + 16, rows:].astype(f32) for n in range(count))
    shifts = [
        jnp.concatenate([shift[i * heads + h : i * heads + h + 1] for h in range(heads)], axis=1) for i in range(3)
    ]

    def project(n, which):
        latents = all_ref[n, tail : tail + latent_dim, :rows]
        scale = all_ref[n, tail + latent_dim :, :rows].astype(f32)
        scale = jnp.sum(scale.T, axis=1, keepdims=True)
        return [dot(latents, tables[i], ((0,), (0,))) * scale + shifts[i] for i in which]

    queries = (project(0, (0,))[0] * (HEAD_DIM ** (-0.5) * LOG2E)).astype(bf16)

    def fill(n, _):
        keys, values = project(n, (1, 2))
        held_ref[n, :rows] = keys.astype(bf16)
        held_ref[n, rows:] = values.astype(bf16)
        return 0

    lax.fori_loop(0, count, fill, 0)
    carry = tuple(
        (jnp.full((1, rows), -1e30, f32), jnp.zeros((1, rows), f32), jnp.zeros((HEAD_DIM, rows), f32))
        for _ in range(heads)
    )

    def pair(ref, i, carry):
        def both(first, h):
            cols = slice(h * HEAD_DIM, (h + 1) * HEAD_DIM)
            return jnp.concatenate([ref[2 * i + n, first : first + rows, cols] for n in range(2)], axis=0)

        return fold_keys(heads, carry, queries, lambda h: both(0, h), lambda h: both(rows, h))

    carry = lax.fori_loop(0, count // 2, lambda i, c: pair(held_ref, i, c), carry)
    carry = lax.fori_loop(0, count // 2, lambda i, c: pair(all_ref, i, c), carry)
    for h in range(heads):
        _, total, weighted = carry[h]
        attended = (weighted / total).T.astype(bf16)
        out_ref[:, :, h * HEAD_DIM : (h + 1) * HEAD_DIM] = jnp.broadcast_to(
            attended[None], (out_ref.shape[0], rows, HEAD_DIM)
        )


def halves(value):
    high = value.astype(bf16).astype(f32)
    return high, value - high


def head_kernel(sections, where_ref, own_ref, embed_ref, shifts_ref, head_ref, att_ref, *refs):
    weight_refs, out_ref = refs[:-1], refs[-1]
    n_fsdp, rows = att_ref.shape[:2]
    latent_dim = embed_ref.shape[0]
    mixed = None
    for f in range(n_fsdp):
        whole = [ref[f] for ref in weight_refs[:-2]]
        whole.append(weight_refs[-2][f] if f < n_fsdp // 2 else weight_refs[-1][f - n_fsdp // 2])
        part = dot(att_ref[f], jnp.concatenate(whole, axis=0), ((1,), (1,)))
        mixed = part if mixed is None else mixed + part
    latents = own_ref[own_ref.shape[0] - latent_dim - 16 : own_ref.shape[0] - 16, :rows]
    residual = dot(latents, embed_ref[...], ((0,), (0,))) + shifts_ref[2] * mixed
    centre = jnp.mean(residual, axis=1, keepdims=True)
    residual = residual - centre
    spread = jnp.sum(residual * residual, axis=1, keepdims=True)
    plain_head = head_ref[...].astype(f32)
    head = (plain_head * (1.0 + shifts_ref[4])).astype(bf16)
    padded = jnp.concatenate([head, jnp.zeros_like(head)], axis=0)
    values = dot(residual.astype(bf16), padded, ((1,), (1,)))
    lanes = lax.broadcasted_iota(jnp.int32, values.shape, 1)
    for n, column in enumerate(halves(centre) + halves(spread)):
        values = jnp.where(lanes == latent_dim + n, column, values)
    values = values.astype(bf16)
    sums = jnp.sum(head.astype(f32), axis=1, keepdims=True)
    consts = jnp.sum(plain_head * shifts_ref[3], axis=1, keepdims=True)
    place = lax.broadcasted_iota(jnp.int32, (latent_dim, 128), 1)
    extra = jnp.zeros((latent_dim, 128), f32)
    for n, column in enumerate(halves(sums) + halves(consts)):
        extra = jnp.where(place == n, column, extra)
    extra = jnp.concatenate([extra, jnp.zeros_like(extra)], axis=0).T[:16].astype(bf16)
    piece = rows // n_fsdp
    for f in range(n_fsdp):
        for s in range(sections):
            out_ref[s * n_fsdp + f, :piece] = values[f * piece : (f + 1) * piece]
            out_ref[s * n_fsdp + f, piece:] = extra


def estimate_kernel(sections, width, where_ref, levels_ref, partial_ref, student_ref, noised_ref, group_ref, grad_ref, out_ref):
    piece, latent_dim = student_ref.shape
    count = partial_ref.shape[0] // sections
    estimates = []
    for p in range(sections):
        blocks = [partial_ref[p * count + i].astype(f32) for i in range(count)]

        def column(b, n):
            at = latent_dim + n
            return b[:piece, at : at + 1] + b[:piece, at + 1 : at + 2]

        def line(b, n):
            at = piece + n
            return b[at : at + 1, :latent_dim] + b[at + 1 : at + 2, :latent_dim]

        means = [column(b, 0) for b in blocks]
        mean = sum(means) / count
        linear, spread, shift = 0.0, 0.0, 0.0
        for b, m in zip(blocks, means):
            offset = m - mean
            linear += b[:piece, :latent_dim] + offset * line(b, 0)
            spread += column(b, 2) + (width // count) * (offset * offset)
            shift += line(b, 2)
        velocity = linear * lax.rsqrt(spread / width + 1e-06) + shift
        latent = (student_ref if p == 0 else noised_ref)[...].astype(f32)
        estimates.append(latent - levels_ref[0 if p == 0 else 1] * velocity)
    group_ref[...] = estimates[0]
    teacher = estimates[2] + guidance_scale * (estimates[1] - estimates[2])
    grad = estimates[3] - teacher
    grad_ref[...] = grad
    velocity_grad = -levels_ref[2] * grad
    padded = jnp.concatenate([velocity_grad, jnp.zeros_like(velocity_grad)], axis=1).astype(bf16)
    out_ref[...] = jnp.broadcast_to(padded[None], out_ref.shape)


def gradient_kernel(where_ref, grad_ref, feature_ref, out_ref):
    count, latent_dim, width = out_ref.shape
    rows = grad_ref.shape[1]
    grads = grad_ref[...].reshape(-1, grad_ref.shape[2])
    first, second = (
        dot(grads, feature_ref[:, at : at + rows].reshape(count * rows, -1), ((0,), (0,)))[:latent_dim]
        for at in (width, width + rows)
    )
    joined = jnp.concatenate([first, second], axis=1)
    for i in range(count):
        out_ref[i] = joined[:, i * width : (i + 1) * width]


def per_device(
    student_input,
    previous_latent,
    score_noise,
    timesteps,
    modulation,
    in_weight,
    qkv_weight,
    out_weight,
    head_weight,
    kv_cache,
    saved_features,
):
    section, me_seq, me_fsdp = (lax.axis_index(a) for a in ("section", "seq", "fsdp"))
    sections, n_seq, n_fsdp = (lax.axis_size(a) for a in ("section", "seq", "fsdp"))
    model_index = section - (section >= 2).astype(jnp.int32)
    where = jnp.stack([model_index, me_seq, me_fsdp, section]).astype(jnp.int32)
    levels = noise_levels(timesteps)
    rows, latent_dim = student_input.shape
    width = in_weight.shape[2]
    depth, feat = qkv_weight.shape[1], qkv_weight.shape[3]
    heads = feat // HEAD_DIM
    piece = rows // n_fsdp
    shifts = modulation.transpose(1, 0, 2)
    slot = depth // n_fsdp

    cut = run(aside_kernel, where, [((n_fsdp, slot + 2 * piece, feat), bf16)], out_weight, saved_features, picked=(0,))
    lines = 2 * rows + 3 * latent_dim + latent_dim + 16
    own = run(
        prepare_kernel,
        where,
        [((lines, feat), bf16)],
        timesteps,
        in_weight,
        qkv_weight.transpose(0, 2, 1, 3),
        shifts,
        student_input.T,
        previous_latent.T,
        score_noise.T,
        kv_cache[0].transpose(1, 0, 2),
        picked=(1, 2),
    )
    aside = exchange(cut, "fsdp")
    around = Ring(own, "seq", n_seq, 0, lines // 32 * 16)
    around.step()
    around.step()
    block, *_ = lax.optimization_barrier((aside[:, :slot],) + around.ends())
    weights = Ring(block, "seq", n_seq, 0)
    weights.step()
    around.finish()
    blocks = around.blocks()
    attended = run(
        functools.partial(attention_kernel, heads, latent_dim),
        together(where, *weights.ends()),
        [((n_fsdp, rows, feat), bf16)],
        *blocks,
        scratch=[
            pltpu.VMEM((n_seq, lines, feat), bf16),
            pltpu.VMEM((n_seq, 2 * rows, feat), bf16),
            pltpu.SemaphoreType.DMA((n_seq + 1,)),
        ],
        raw=True,
    )
    weights.step()
    attended = exchange(together(attended, *weights.ends()), "fsdp")
    weights.step()
    weights.finish()
    embed_here, head_here, shifts_here = run(
        columns_kernel,
        together(where, own),
        [((latent_dim, depth), bf16), ((latent_dim, depth), bf16), ((shifts.shape[0], 1, depth), f32)],
        in_weight,
        head_weight.transpose(0, 2, 1),
        shifts,
        picked=(0, 1),
    )
    partials = run(
        functools.partial(head_kernel, sections),
        where,
        [((sections * n_fsdp, piece + 16, 128), bf16)],
        own,
        embed_here,
        shifts_here,
        head_here,
        attended,
        *weights.blocks(),
    )
    partials = exchange(partials, ("section", "fsdp"))

    noised = (
        (1.0 - levels[1]) * previous_latent.astype(f32) + levels[1] * score_noise.astype(f32)
    ).astype(bf16)
    own_student = lax.dynamic_slice_in_dim(student_input, me_fsdp * piece, piece, 0)
    own_noised = lax.dynamic_slice_in_dim(noised, me_fsdp * piece, piece, 0)
    student_group, dmd_grad, grads = run(
        functools.partial(estimate_kernel, sections, width),
        where,
        [((piece, latent_dim), f32), ((piece, latent_dim), f32), ((n_fsdp, piece, 2 * latent_dim), bf16)],
        levels,
        partials,
        own_student,
        own_noised,
    )
    grads = exchange(grads, "fsdp")
    partial_grad = run(gradient_kernel, where, [((n_seq, latent_dim, slot), f32)], grads, aside)
    head_grad = jnp.sum(exchange(partial_grad, "seq"), axis=0).T
    return (student_group, dmd_grad, head_grad)


def solution(mesh):
    placed = (
        P("seq", None),
        P("seq", None),
        P("seq", None),
        P(),
        P("section", None, None),
        P(),
        P(None, "seq", None, "fsdp"),
        P(None, "seq", "fsdp"),
        P(),
        P("section", "seq", None, "fsdp"),
        P(("seq", "fsdp"), None),
    )
    return jax.shard_map(
        per_device,
        mesh=mesh,
        in_specs=placed,
        out_specs=(P(("seq", "fsdp"), None), P(("seq", "fsdp"), None), P(("seq", "fsdp"), None)),
        check_vma=False,
    )
```

```python
import functools

import jax
import jax.numpy as jnp
from jax import lax
from jax.experimental import pallas as pl
from jax.experimental.pallas import tpu as pltpu
from jax.sharding import PartitionSpec as P

HEAD_DIM = 128
LOG2E = 1.4426950408889634
guidance_scale = 5.0
bf16 = jnp.bfloat16
f32 = jnp.float32


def run(kernel, where, outs, *operands, picked=(), scratch=(), raw=(), cost=None):
    def spec(shape, pick=False):
        zeros = (0,) * (len(shape) - 1)
        if pick:
            return pl.BlockSpec((1,) + tuple(shape[1:]), lambda i, w: (w[0],) + zeros)
        return pl.BlockSpec(tuple(shape), lambda i, w: (0,) + zeros)

    in_specs = [
        pl.BlockSpec(memory_space=pltpu.SMEM)
        if x.ndim == 1
        else pl.BlockSpec(memory_space=pltpu.HBM)
        if n in raw
        else spec(x.shape, n in picked)
        for n, x in enumerate(operands)
    ]
    result = pl.pallas_call(
        kernel,
        grid_spec=pltpu.PrefetchScalarGridSpec(
            num_scalar_prefetch=1,
            grid=(1,),
            in_specs=in_specs,
            out_specs=tuple(spec(shape) for shape, _ in outs),
            scratch_shapes=list(scratch),
        ),
        out_shape=tuple(jax.ShapeDtypeStruct(shape, dtype) for shape, dtype in outs),
        compiler_params=pltpu.CompilerParams(vmem_limit_bytes=52 * 1024 * 1024),
        cost_estimate=cost,
    )(where, *operands)
    return result[0] if len(outs) == 1 else result


def together(value, *others):
    return lax.optimization_barrier((value,) + others)[0]


def noise_levels(steps):
    remain = 1.0 - steps.astype(f32) / 1000.0
    return 5.0 * remain / (1.0 + 4.0 * remain)


def select_model(stacked, model_index):
    return lax.dynamic_index_in_dim(stacked, model_index, 0, keepdims=False)


def exchange(blocks, axis):
    return lax.all_to_all(blocks, axis, 0, 0, tiled=True)


class Ring:
    def __init__(self, block, axis, count, split, split_at=None):
        self.split_at = split_at
        self.axis, self.split, self.half = axis, split, count // 2
        self.up = [(i, (i + 1) % count) for i in range(count)]
        self.down = [(i, (i - 1) % count) for i in range(count)]
        self.behind, self.ahead, self.last = [block], [block], []

    def step(self):
        self.behind.append(lax.ppermute(self.behind[-1], self.axis, self.up))
        self.ahead.append(lax.ppermute(self.ahead[-1], self.axis, self.down))

    def ends(self):
        return self.behind[-1], self.ahead[-1]

    def finish(self):
        while len(self.behind) < self.half:
            self.step()
        total = self.behind[0].shape[self.split]
        size = total // 2 if self.split_at is None else self.split_at
        first = lax.slice_in_dim(self.behind[-1], 0, size, axis=self.split)
        second = lax.slice_in_dim(self.ahead[-1], size, total, axis=self.split)
        self.last = [lax.ppermute(first, self.axis, self.up), lax.ppermute(second, self.axis, self.down)]

    def blocks(self):
        return self.behind + self.ahead[1:] + self.last


def dot(a, b, over):
    return lax.dot_general(a, b, ((over[0], over[1]), ((), ())), preferred_element_type=f32)


def prepare_kernel(
    where_ref, embed_ref, weight_ref, shifts_hbm, student_hbm, previous_hbm, noise_hbm, context_hbm, *refs
):
    first_ref, second_ref, shifts_ref, student_ref, previous_ref, noise_ref, out_ref, sems = refs
    latent_dim, width = embed_ref.shape[1:]
    parts, depth, feat = weight_ref.shape[1:]
    rows = student_ref.shape[1]
    sources = (shifts_hbm, student_hbm, previous_hbm, noise_hbm, context_hbm)
    targets = (shifts_ref, student_ref, previous_ref, noise_ref, out_ref.at[pl.ds(0, 2 * rows)])
    copies = [pltpu.make_async_copy(a, b, sems.at[n]) for n, (a, b) in enumerate(zip(sources, targets))]
    for copy in copies:
        copy.start()
    for copy in copies:
        copy.wait()
    level = noise_levels(jnp.full((1, rows), where_ref[5], jnp.int32))
    noised = (1.0 - level) * previous_ref[...].astype(f32) + level * noise_ref[...].astype(f32)
    latents = jnp.where(where_ref[3] == 0, student_ref[...].astype(f32), noised.astype(bf16).astype(f32))

    step = 1024
    row_sum = jnp.zeros((latent_dim, 1), f32)
    for first in range(0, width, step):
        row_sum += jnp.sum(embed_ref[0, :, first : first + step].astype(f32), axis=1, keepdims=True)
    row_mean = row_sum / width

    here = pl.ds(pl.multiple_of(where_ref[1] * depth, 128), depth)
    centred = (embed_ref[0, :, here].astype(f32) - row_mean) * (1.0 + shifts_ref[1, :, here])
    shift = jnp.broadcast_to(shifts_ref[0, :, here], (16, depth))
    folded = jnp.concatenate([centred, shift], axis=0).astype(bf16)
    tail = 2 * rows + parts * latent_dim
    lines = []
    for i in range(parts):
        table = dot(folded, weight_ref[0, i], ((1,), (0,)))
        at = 2 * rows + i * latent_dim
        out_ref[at : at + latent_dim] = table[:latent_dim].astype(bf16)
        lines += [table[latent_dim : latent_dim + 1, n : n + 128] for n in range(0, feat, 128)]

    mean = jnp.sum(row_mean * latents, axis=0, keepdims=True)
    plain = latents.astype(bf16)
    spread = jnp.zeros((1, rows), f32)
    for first in range(0, width, step):
        hidden = dot(embed_ref[0, :, first : first + step], plain, ((0,), (0,))) - mean
        spread += jnp.sum(hidden * hidden, axis=0, keepdims=True)
    inverse = lax.rsqrt(spread / width + 1e-06)
    high = inverse.astype(bf16).astype(f32)
    middle = (inverse - high).astype(bf16).astype(f32)
    low = inverse - high - middle
    line = lax.broadcasted_iota(jnp.int32, (16, rows), 0)
    scales = jnp.where(line == 0, high, jnp.where(line == 1, middle, jnp.where(line == 2, low, 0.0)))
    out_ref[tail : tail + latent_dim, :rows] = plain
    out_ref[tail + latent_dim :, :rows] = scales.astype(bf16)
    spare = jnp.zeros((latent_dim + 16 - len(lines), 128), f32)
    out_ref[tail:, rows:] = jnp.concatenate(lines + [spare], axis=0).astype(bf16)
    cut = first_ref.shape[0]
    first_ref[...] = out_ref[:cut]
    second_ref[...] = out_ref[cut:]


def aside_kernel(where_ref, weight_ref, feature_ref, out_ref):
    count, lines, feat = out_ref.shape
    rows, width = feature_ref.shape
    slot = weight_ref.shape[1] // count
    part = width // count
    out_ref[:, :slot] = weight_ref[0].reshape(count, slot, feat)
    spare = jnp.zeros((rows, 2 * feat - part), bf16)
    for j in range(count):
        pieces = [feature_ref[:, s * part + j * slot : s * part + (j + 1) * slot] for s in range(count)]
        joined = jnp.concatenate(pieces + [spare], axis=1)
        out_ref[j, slot : slot + rows] = joined[:, :feat]
        out_ref[j, slot + rows :] = joined[:, feat:]


def columns_kernel(where_ref, embed_ref, head_ref, shifts_ref, embed_out, head_out, shifts_out):
    count = 8
    part = embed_ref.shape[2] // count
    slot = part // count
    half = count // 2
    order = [0] + [count - d for d in range(1, half)] + list(range(1, half + 1))
    for f in range(count):

        @pl.when(where_ref[2] == f)
        def _(f=f):
            sources = [(embed_ref.at[0], embed_out), (head_ref.at[0], head_out)]
            sources += [(shifts_ref.at[i], shifts_out.at[i]) for i in range(shifts_ref.shape[0])]
            for source, target in sources:
                pieces = []
                for d in order:
                    owner = lax.rem(where_ref[1] + d, count)
                    block = source[:, pl.ds(pl.multiple_of(owner * part, 128), part)]
                    pieces.append(block[:, f * slot : (f + 1) * slot])
                target[...] = jnp.concatenate(pieces, axis=1)


def fold_keys(heads, carry, queries, keys, values):
    scores = [dot(keys(h), queries[:, h * HEAD_DIM : (h + 1) * HEAD_DIM], ((1,), (1,))) for h in range(heads)]
    new = []
    for h in range(heads):
        top, total, weighted = carry[h]
        new_top = jnp.maximum(top, jnp.max(scores[h], axis=0, keepdims=True))
        weights = jnp.exp2(scores[h] - new_top)
        keep = jnp.exp2(top - new_top)
        total = total * keep + jnp.sum(weights, axis=0, keepdims=True)
        weighted = weighted * keep + dot(values(h), weights.astype(bf16), ((0,), (0,)))
        new.append((new_top, total, weighted))
    return tuple(new)


def attention_kernel(heads, latent_dim, group_start, where_ref, *refs):
    n_blocks = len(refs) - 4
    block_refs, (out_ref, all_ref, held_ref, sems) = refs[:n_blocks], refs[n_blocks:]
    count, lines, feat = all_ref.shape
    rows = out_ref.shape[1]
    half = n_blocks // 2
    copies = []
    for start, group in ((0, block_refs[:half]), (group_start, block_refs[half:])):
        at = [(n, start) for n in range(count)] + [(count - 1, start + group[count - 1].shape[0])]
        copies.append(
            [
                pltpu.make_async_copy(
                    ref, all_ref.at[n, pl.ds(place, ref.shape[0])], sems.at[(half if start else 0) + i]
                )
                for i, ((n, place), ref) in enumerate(zip(at, group))
            ]
        )
    early, late = copies[1], copies[0]
    for copy in early + late:
        copy.start()
    for copy in early:
        copy.wait()

    tail = 2 * rows + 3 * latent_dim
    parts = [slice(2 * rows + i * latent_dim, 2 * rows + (i + 1) * latent_dim) for i in range(3)]
    tables = [sum(all_ref[n, at].astype(f32) for n in range(count)).astype(bf16) for at in parts]
    shift = sum(all_ref[n, tail : tail + 16, rows:].astype(f32) for n in range(count))
    shifts = [
        jnp.concatenate([shift[i * heads + h : i * heads + h + 1] for h in range(heads)], axis=1) for i in range(3)
    ]

    def project(n, which):
        latents = all_ref[n, tail : tail + latent_dim, :rows]
        scale = all_ref[n, tail + latent_dim :, :rows].astype(f32)
        scale = jnp.sum(scale.T, axis=1, keepdims=True)
        return [dot(latents, tables[i], ((0,), (0,))) * scale + shifts[i] for i in which]

    queries = (project(0, (0,))[0] * (HEAD_DIM ** (-0.5) * LOG2E)).astype(bf16)

    def fill(n, _):
        keys, values = project(n, (1, 2))
        held_ref[n, :rows] = keys.astype(bf16)
        held_ref[n, rows:] = values.astype(bf16)
        return 0

    lax.fori_loop(0, count, fill, 0)
    carry = tuple(
        (jnp.full((1, rows), -1e30, f32), jnp.zeros((1, rows), f32), jnp.zeros((HEAD_DIM, rows), f32))
        for _ in range(heads)
    )

    def pair(ref, i, carry):
        def both(first, h):
            cols = slice(h * HEAD_DIM, (h + 1) * HEAD_DIM)
            return jnp.concatenate([ref[2 * i + n, first : first + rows, cols] for n in range(2)], axis=0)

        return fold_keys(heads, carry, queries, lambda h: both(0, h), lambda h: both(rows, h))

    carry = lax.fori_loop(0, count // 2, lambda i, c: pair(held_ref, i, c), carry, unroll=2)
    for copy in late:
        copy.wait()
    carry = lax.fori_loop(0, count // 2, lambda i, c: pair(all_ref, i, c), carry, unroll=2)
    for h in range(heads):
        _, total, weighted = carry[h]
        attended = (weighted / total).T.astype(bf16)
        out_ref[:, :, h * HEAD_DIM : (h + 1) * HEAD_DIM] = jnp.broadcast_to(
            attended[None], (out_ref.shape[0], rows, HEAD_DIM)
        )


def halves(value):
    high = value.astype(bf16).astype(f32)
    return high, value - high


def head_kernel(sections, where_ref, own_ref, embed_ref, shifts_ref, head_ref, att_ref, *refs):
    weight_refs, out_ref = refs[:-1], refs[-1]
    n_fsdp, rows = att_ref.shape[:2]
    latent_dim = embed_ref.shape[0]
    mixed = None
    middle = len(weight_refs) // 2
    for f in range(n_fsdp):
        group = weight_refs[:middle] if f < n_fsdp // 2 else weight_refs[middle:]
        g = f % (n_fsdp // 2)
        whole = [ref[g] for ref in group[:-2]]
        whole.append(group[-2][g] if g < n_fsdp // 4 else group[-1][g - n_fsdp // 4])
        part = dot(att_ref[f], jnp.concatenate(whole, axis=0), ((1,), (1,)))
        mixed = part if mixed is None else mixed + part
    latents = own_ref[own_ref.shape[0] - latent_dim - 16 : own_ref.shape[0] - 16, :rows]
    residual = dot(latents, embed_ref[...], ((0,), (0,))) + shifts_ref[2] * mixed
    centre = jnp.mean(residual, axis=1, keepdims=True)
    residual = residual - centre
    spread = jnp.sum(residual * residual, axis=1, keepdims=True)
    plain_head = head_ref[...].astype(f32)
    head = (plain_head * (1.0 + shifts_ref[4])).astype(bf16)
    padded = jnp.concatenate([head, jnp.zeros_like(head)], axis=0)
    values = dot(residual.astype(bf16), padded, ((1,), (1,)))
    lanes = lax.broadcasted_iota(jnp.int32, values.shape, 1)
    for n, column in enumerate(halves(centre) + halves(spread)):
        values = jnp.where(lanes == latent_dim + n, column, values)
    values = values.astype(bf16)
    sums = jnp.sum(head.astype(f32), axis=1, keepdims=True)
    consts = jnp.sum(plain_head * shifts_ref[3], axis=1, keepdims=True)
    place = lax.broadcasted_iota(jnp.int32, (latent_dim, 128), 1)
    extra = jnp.zeros((latent_dim, 128), f32)
    for n, column in enumerate(halves(sums) + halves(consts)):
        extra = jnp.where(place == n, column, extra)
    extra = jnp.concatenate([extra, jnp.zeros_like(extra)], axis=0).T[:16].astype(bf16)
    piece = rows // n_fsdp
    for f in range(n_fsdp):
        for s in range(sections):
            out_ref[s * n_fsdp + f, :piece] = values[f * piece : (f + 1) * piece]
            out_ref[s * n_fsdp + f, piece:] = extra


def estimate_kernel(sections, width, where_ref, levels_ref, partial_ref, student_ref, noised_ref, group_ref, grad_ref, out_ref):
    piece, latent_dim = student_ref.shape
    count = partial_ref.shape[0] // sections
    estimates = []
    for p in range(sections):
        blocks = [partial_ref[p * count + i].astype(f32) for i in range(count)]

        def column(b, n):
            at = latent_dim + n
            return b[:piece, at : at + 1] + b[:piece, at + 1 : at + 2]

        def line(b, n):
            at = piece + n
            return b[at : at + 1, :latent_dim] + b[at + 1 : at + 2, :latent_dim]

        means = [column(b, 0) for b in blocks]
        mean = sum(means) / count
        linear, spread, shift = 0.0, 0.0, 0.0
        for b, m in zip(blocks, means):
            offset = m - mean
            linear += b[:piece, :latent_dim] + offset * line(b, 0)
            spread += column(b, 2) + (width // count) * (offset * offset)
            shift += line(b, 2)
        velocity = linear * lax.rsqrt(spread / width + 1e-06) + shift
        latent = (student_ref if p == 0 else noised_ref)[...].astype(f32)
        estimates.append(latent - levels_ref[0 if p == 0 else 1] * velocity)
    group_ref[...] = estimates[0]
    teacher = estimates[2] + guidance_scale * (estimates[1] - estimates[2])
    grad = estimates[3] - teacher
    grad_ref[...] = grad
    velocity_grad = -levels_ref[2] * grad
    padded = jnp.concatenate([velocity_grad, jnp.zeros_like(velocity_grad)], axis=1).astype(bf16)
    out_ref[...] = jnp.broadcast_to(padded[None], out_ref.shape)


def gradient_kernel(where_ref, grad_ref, feature_ref, out_ref):
    count, latent_dim, width = out_ref.shape
    rows = grad_ref.shape[1]
    grads = grad_ref[...].reshape(-1, grad_ref.shape[2])
    first, second = (
        dot(grads, feature_ref[:, at : at + rows].reshape(count * rows, -1), ((0,), (0,)))[:latent_dim]
        for at in (width, width + rows)
    )
    joined = jnp.concatenate([first, second], axis=1)
    for i in range(count):
        out_ref[i] = joined[:, i * width : (i + 1) * width]


def per_device(
    student_input,
    previous_latent,
    score_noise,
    timesteps,
    modulation,
    in_weight,
    qkv_weight,
    out_weight,
    head_weight,
    kv_cache,
    saved_features,
):
    section, me_seq, me_fsdp = (lax.axis_index(a) for a in ("section", "seq", "fsdp"))
    sections, n_seq, n_fsdp = (lax.axis_size(a) for a in ("section", "seq", "fsdp"))
    model_index = section - (section >= 2).astype(jnp.int32)
    where = jnp.concatenate([jnp.stack([model_index, me_seq, me_fsdp, section]).astype(jnp.int32), timesteps])
    levels = noise_levels(timesteps)
    rows, latent_dim = student_input.shape
    width = in_weight.shape[2]
    depth, feat = qkv_weight.shape[1], qkv_weight.shape[3]
    heads = feat // HEAD_DIM
    piece = rows // n_fsdp
    shifts = modulation.transpose(1, 0, 2)
    slot = depth // n_fsdp

    cut = run(aside_kernel, where, [((n_fsdp, slot + 2 * piece, feat), bf16)], out_weight, saved_features, picked=(0,))
    lines = 2 * rows + 3 * latent_dim + latent_dim + 16
    first = lines // 32 * 16
    own, second = run(
        prepare_kernel,
        where,
        [((first, feat), bf16), ((lines - first, feat), bf16)],
        in_weight,
        qkv_weight.transpose(0, 2, 1, 3),
        shifts,
        student_input.T,
        previous_latent.T,
        score_noise.T,
        kv_cache[0].transpose(1, 0, 2).reshape(2 * rows, feat),
        picked=(0, 1),
        raw=(2, 3, 4, 5, 6),
        scratch=[
            pltpu.VMEM(shifts.shape, f32),
            pltpu.VMEM((latent_dim, rows), bf16),
            pltpu.VMEM((latent_dim, rows), bf16),
            pltpu.VMEM((latent_dim, rows), bf16),
            pltpu.VMEM((lines, feat), bf16),
            pltpu.SemaphoreType.DMA((5,)),
        ],
    )
    aside = exchange(cut, "fsdp")
    around = [Ring(x, "seq", n_seq, 0, x.shape[0] // 32 * 16) for x in (own, second)]
    for _ in range(n_seq // 2 - 1):
        for r in around:
            r.step()
    ends = around[0].ends() + around[1].ends()
    block, *_ = lax.optimization_barrier((aside[:, :slot],) + ends)
    weights = [Ring(block[i : i + n_fsdp // 2], "seq", n_seq, 0) for i in (0, n_fsdp // 2)]
    for r in around:
        r.finish()
    for r in weights:
        r.step()
    blocks = around[0].blocks() + around[1].blocks()
    attended = run(
        functools.partial(attention_kernel, heads, latent_dim, first),
        where,
        [((n_fsdp, rows, feat), bf16)],
        *blocks,
        scratch=[
            pltpu.VMEM((n_seq, lines, feat), bf16),
            pltpu.VMEM((n_seq, 2 * rows, feat), bf16),
            pltpu.SemaphoreType.DMA((len(blocks),)),
        ],
        raw=range(len(blocks)),
        cost=pl.CostEstimate(flops=11 * 10**9, bytes_accessed=20 * 10**6, transcendentals=3 * 10**6),
    )
    attended = exchange(together(attended, *weights[0].ends(), *weights[1].ends()), "fsdp")
    for _ in range(n_seq // 2 - 2):
        for r in weights:
            r.step()
    for r in weights:
        r.finish()
    embed_here, head_here, shifts_here = run(
        columns_kernel,
        together(where, own),
        [((latent_dim, depth), bf16), ((latent_dim, depth), bf16), ((shifts.shape[0], 1, depth), f32)],
        in_weight,
        head_weight.transpose(0, 2, 1),
        shifts,
        picked=(0, 1),
    )
    partials = run(
        functools.partial(head_kernel, sections),
        where,
        [((sections * n_fsdp, piece + 16, 128), bf16)],
        second,
        embed_here,
        shifts_here,
        head_here,
        attended,
        *weights[0].blocks(),
        *weights[1].blocks(),
    )
    partials = exchange(partials, ("section", "fsdp"))

    noised = (
        (1.0 - levels[1]) * previous_latent.astype(f32) + levels[1] * score_noise.astype(f32)
    ).astype(bf16)
    own_student = lax.dynamic_slice_in_dim(student_input, me_fsdp * piece, piece, 0)
    own_noised = lax.dynamic_slice_in_dim(noised, me_fsdp * piece, piece, 0)
    student_group, dmd_grad, grads = run(
        functools.partial(estimate_kernel, sections, width),
        where,
        [((piece, latent_dim), f32), ((piece, latent_dim), f32), ((n_fsdp, piece, 2 * latent_dim), bf16)],
        levels,
        partials,
        own_student,
        own_noised,
    )
    grads = exchange(grads, "fsdp")
    partial_grad = run(gradient_kernel, where, [((n_seq, latent_dim, slot), f32)], grads, aside)
    head_grad = jnp.sum(exchange(partial_grad, "seq"), axis=0).T
    return (student_group, dmd_grad, head_grad)


def solution(mesh):
    placed = (
        P("seq", None),
        P("seq", None),
        P("seq", None),
        P(),
        P("section", None, None),
        P(),
        P(None, "seq", None, "fsdp"),
        P(None, "seq", "fsdp"),
        P(),
        P("section", "seq", None, "fsdp"),
        P(("seq", "fsdp"), None),
    )
    return jax.shard_map(
        per_device,
        mesh=mesh,
        in_specs=placed,
        out_specs=(P(("seq", "fsdp"), None), P(("seq", "fsdp"), None), P(("seq", "fsdp"), None)),
        check_vma=False,
    )
```

```python
import functools

import jax
import jax.numpy as jnp
from jax import lax
from jax.experimental import pallas as pl
from jax.experimental.pallas import tpu as pltpu
from jax.sharding import PartitionSpec as P

HEAD_DIM = 128
LOG2E = 1.4426950408889634
guidance_scale = 5.0
bf16 = jnp.bfloat16
f32 = jnp.float32


def run(kernel, where, outs, *operands, picked=(), scratch=(), raw=(), cost=None):
    def spec(shape, pick=False):
        zeros = (0,) * (len(shape) - 1)
        if pick:
            return pl.BlockSpec((1,) + tuple(shape[1:]), lambda i, w: (w[0],) + zeros)
        return pl.BlockSpec(tuple(shape), lambda i, w: (0,) + zeros)

    in_specs = [
        pl.BlockSpec(memory_space=pltpu.SMEM)
        if x.ndim == 1
        else pl.BlockSpec(memory_space=pltpu.HBM)
        if n in raw
        else spec(x.shape, n in picked)
        for n, x in enumerate(operands)
    ]
    result = pl.pallas_call(
        kernel,
        grid_spec=pltpu.PrefetchScalarGridSpec(
            num_scalar_prefetch=1,
            grid=(1,),
            in_specs=in_specs,
            out_specs=tuple(spec(shape) for shape, _ in outs),
            scratch_shapes=list(scratch),
        ),
        out_shape=tuple(jax.ShapeDtypeStruct(shape, dtype) for shape, dtype in outs),
        compiler_params=pltpu.CompilerParams(vmem_limit_bytes=52 * 1024 * 1024),
        cost_estimate=cost,
    )(where, *operands)
    return result[0] if len(outs) == 1 else result


def together(value, *others):
    return lax.optimization_barrier((value,) + others)[0]


def noise_levels(steps):
    remain = 1.0 - steps.astype(f32) / 1000.0
    return 5.0 * remain / (1.0 + 4.0 * remain)


def select_model(stacked, model_index):
    return lax.dynamic_index_in_dim(stacked, model_index, 0, keepdims=False)


def exchange(blocks, axis):
    return lax.all_to_all(blocks, axis, 0, 0, tiled=True)


class Ring:
    def __init__(self, block, axis, count, split, split_at=None):
        self.split_at = split_at
        self.axis, self.split, self.half = axis, split, count // 2
        self.up = [(i, (i + 1) % count) for i in range(count)]
        self.down = [(i, (i - 1) % count) for i in range(count)]
        self.behind, self.ahead, self.last = [block], [block], []

    def step(self):
        self.behind.append(lax.ppermute(self.behind[-1], self.axis, self.up))
        self.ahead.append(lax.ppermute(self.ahead[-1], self.axis, self.down))

    def ends(self):
        return self.behind[-1], self.ahead[-1]

    def finish(self):
        while len(self.behind) < self.half:
            self.step()
        total = self.behind[0].shape[self.split]
        size = total // 2 if self.split_at is None else self.split_at
        first = lax.slice_in_dim(self.behind[-1], 0, size, axis=self.split)
        second = lax.slice_in_dim(self.ahead[-1], size, total, axis=self.split)
        self.last = [lax.ppermute(first, self.axis, self.up), lax.ppermute(second, self.axis, self.down)]

    def blocks(self):
        return self.behind + self.ahead[1:] + self.last


def dot(a, b, over):
    return lax.dot_general(a, b, ((over[0], over[1]), ((), ())), preferred_element_type=f32)


def prepare_kernel(
    where_ref, embed_ref, weight_ref, shifts_hbm, student_hbm, previous_hbm, noise_hbm, context_hbm, *refs
):
    out_ref, plain_ref, shifts_ref, student_ref, previous_ref, noise_ref, sems = refs
    latent_dim, width = embed_ref.shape[1:]
    parts, depth, feat = weight_ref.shape[1:]
    rows = student_ref.shape[1]
    sources = (shifts_hbm, student_hbm, previous_hbm, noise_hbm, context_hbm)
    targets = (shifts_ref, student_ref, previous_ref, noise_ref, out_ref.at[pl.ds(0, 2 * rows)])
    copies = [pltpu.make_async_copy(a, b, sems.at[n]) for n, (a, b) in enumerate(zip(sources, targets))]
    for copy in copies:
        copy.start()
    for copy in copies:
        copy.wait()
    level = noise_levels(jnp.full((1, rows), where_ref[5], jnp.int32))
    noised = (1.0 - level) * previous_ref[...].astype(f32) + level * noise_ref[...].astype(f32)
    latents = jnp.where(where_ref[3] == 0, student_ref[...].astype(f32), noised.astype(bf16).astype(f32))

    step = 1024
    row_sum = jnp.zeros((latent_dim, 1), f32)
    for first in range(0, width, step):
        row_sum += jnp.sum(embed_ref[0, :, first : first + step].astype(f32), axis=1, keepdims=True)
    row_mean = row_sum / width

    here = pl.ds(pl.multiple_of(where_ref[1] * depth, 128), depth)
    centred = (embed_ref[0, :, here].astype(f32) - row_mean) * (1.0 + shifts_ref[1, :, here])
    shift = jnp.broadcast_to(shifts_ref[0, :, here], (16, depth))
    folded = jnp.concatenate([centred, shift], axis=0).astype(bf16)
    tail = 2 * rows + parts * latent_dim
    lines = []
    for i in range(parts):
        table = dot(folded, weight_ref[0, i], ((1,), (0,)))
        at = 2 * rows + i * latent_dim
        out_ref[at : at + latent_dim] = table[:latent_dim].astype(bf16)
        lines += [table[latent_dim : latent_dim + 1, n : n + 128] for n in range(0, feat, 128)]

    mean = jnp.sum(row_mean * latents, axis=0, keepdims=True)
    plain = latents.astype(bf16)
    spread = jnp.zeros((1, rows), f32)
    for first in range(0, width, step):
        hidden = dot(embed_ref[0, :, first : first + step], plain, ((0,), (0,))) - mean
        spread += jnp.sum(hidden * hidden, axis=0, keepdims=True)
    inverse = lax.rsqrt(spread / width + 1e-06)
    out_ref[tail:, :rows] = (latents * inverse).astype(bf16)
    plain_ref[...] = plain
    spare = jnp.zeros((latent_dim - len(lines), 128), f32)
    out_ref[tail:, rows:] = jnp.concatenate(lines + [spare], axis=0).astype(bf16)


def aside_kernel(where_ref, weight_ref, feature_ref, out_ref):
    count, lines, feat = out_ref.shape
    rows, width = feature_ref.shape
    slot = weight_ref.shape[1] // count
    part = width // count
    out_ref[:, :slot] = weight_ref[0].reshape(count, slot, feat)
    spare = jnp.zeros((rows, 2 * feat - part), bf16)
    for j in range(count):
        pieces = [feature_ref[:, s * part + j * slot : s * part + (j + 1) * slot] for s in range(count)]
        joined = jnp.concatenate(pieces + [spare], axis=1)
        out_ref[j, slot : slot + rows] = joined[:, :feat]
        out_ref[j, slot + rows :] = joined[:, feat:]


def columns_kernel(where_ref, embed_ref, head_ref, shifts_ref, embed_out, head_out, shifts_out):
    count = 8
    part = embed_ref.shape[2] // count
    slot = part // count
    half = count // 2
    order = [0] + [count - d for d in range(1, half)] + list(range(1, half + 1))
    for f in range(count):

        @pl.when(where_ref[2] == f)
        def _(f=f):
            sources = [(embed_ref.at[0], embed_out), (head_ref.at[0], head_out)]
            sources += [(shifts_ref.at[i], shifts_out.at[i]) for i in range(shifts_ref.shape[0])]
            for source, target in sources:
                pieces = []
                for d in order:
                    owner = lax.rem(where_ref[1] + d, count)
                    block = source[:, pl.ds(pl.multiple_of(owner * part, 128), part)]
                    pieces.append(block[:, f * slot : (f + 1) * slot])
                target[...] = jnp.concatenate(pieces, axis=1)


def fold_keys(heads, carry, queries, keys, values):
    scores = [dot(keys(h), queries[:, h * HEAD_DIM : (h + 1) * HEAD_DIM], ((1,), (1,))) for h in range(heads)]
    new = []
    for h in range(heads):
        top, total, weighted = carry[h]
        new_top = jnp.maximum(top, jnp.max(scores[h], axis=0, keepdims=True))
        weights = jnp.exp2(scores[h] - new_top)
        keep = jnp.exp2(top - new_top)
        total = total * keep + jnp.sum(weights, axis=0, keepdims=True)
        weighted = weighted * keep + dot(values(h), weights.astype(bf16), ((0,), (0,)))
        new.append((new_top, total, weighted))
    return tuple(new)


def attention_kernel(heads, latent_dim, where_ref, *refs):
    n_blocks = len(refs) - 4
    block_refs, (out_ref, all_ref, held_ref, sems) = refs[:n_blocks], refs[n_blocks:]
    count, lines, feat = all_ref.shape
    rows = out_ref.shape[1]
    at = [(n, 0, ref.shape[0]) for n, ref in enumerate(block_refs[:-1])]
    at.append((count - 1, block_refs[-2].shape[0], block_refs[-1].shape[0]))
    early, late = [], []
    for ref, (n, place, size) in zip(block_refs, at):
        for first, last, group in ((0, 2 * rows, late), (2 * rows, lines, early)):
            first, last = max(first, place), min(last, place + size)
            if first < last:
                copies = len(early) + len(late)
                group.append(
                    pltpu.make_async_copy(
                        ref.at[pl.ds(first - place, last - first)],
                        all_ref.at[n, pl.ds(first, last - first)],
                        sems.at[copies],
                    )
                )
    for copy in early + late:
        copy.start()
    for copy in early:
        copy.wait()

    tail = 2 * rows + 3 * latent_dim
    parts = [slice(2 * rows + i * latent_dim, 2 * rows + (i + 1) * latent_dim) for i in range(3)]
    tables = [sum(all_ref[n, at].astype(f32) for n in range(count)).astype(bf16) for at in parts]
    shift = sum(all_ref[n, tail : tail + 16, rows:].astype(f32) for n in range(count))
    shifts = [
        jnp.concatenate([shift[i * heads + h : i * heads + h + 1] for h in range(heads)], axis=1) for i in range(3)
    ]

    def project(n, which):
        latents = all_ref[n, tail : tail + latent_dim, :rows]
        return [dot(latents, tables[i], ((0,), (0,))) + shifts[i] for i in which]

    queries = (project(0, (0,))[0] * (HEAD_DIM ** (-0.5) * LOG2E)).astype(bf16)

    def fill(n, _):
        keys, values = project(n, (1, 2))
        held_ref[n, :rows] = keys.astype(bf16)
        held_ref[n, rows:] = values.astype(bf16)
        return 0

    lax.fori_loop(0, count, fill, 0, unroll=4)
    carry = tuple(
        (jnp.full((1, rows), -1e30, f32), jnp.zeros((1, rows), f32), jnp.zeros((HEAD_DIM, rows), f32))
        for _ in range(heads)
    )

    def four(ref, i, carry):
        def both(first, h):
            cols = slice(h * HEAD_DIM, (h + 1) * HEAD_DIM)
            return jnp.concatenate([ref[4 * i + n, first : first + rows, cols] for n in range(4)], axis=0)

        return fold_keys(heads, carry, queries, lambda h: both(0, h), lambda h: both(rows, h))

    carry = lax.fori_loop(0, count // 4, lambda i, c: four(held_ref, i, c), carry, unroll=2)
    for copy in late:
        copy.wait()
    carry = lax.fori_loop(0, count // 4, lambda i, c: four(all_ref, i, c), carry, unroll=2)
    for h in range(heads):
        _, total, weighted = carry[h]
        attended = (weighted / total).T.astype(bf16)
        out_ref[:, :, h * HEAD_DIM : (h + 1) * HEAD_DIM] = jnp.broadcast_to(
            attended[None], (out_ref.shape[0], rows, HEAD_DIM)
        )


def halves(value):
    high = value.astype(bf16).astype(f32)
    return high, value - high


def head_kernel(sections, where_ref, own_ref, embed_ref, shifts_ref, head_ref, att_ref, *refs):
    weight_refs, out_ref = refs[:-1], refs[-1]
    n_fsdp, rows = att_ref.shape[:2]
    latent_dim = embed_ref.shape[0]
    mixed = None
    for f in range(n_fsdp):
        whole = [ref[f] for ref in weight_refs[:-2]]
        whole.append(weight_refs[-2][f] if f < n_fsdp // 2 else weight_refs[-1][f - n_fsdp // 2])
        part = dot(att_ref[f], jnp.concatenate(whole, axis=0), ((1,), (1,)))
        mixed = part if mixed is None else mixed + part
    residual = dot(own_ref[...], embed_ref[...], ((0,), (0,))) + shifts_ref[2] * mixed
    centre = jnp.mean(residual, axis=1, keepdims=True)
    residual = residual - centre
    spread = jnp.sum(residual * residual, axis=1, keepdims=True)
    plain_head = head_ref[...].astype(f32)
    head = (plain_head * (1.0 + shifts_ref[4])).astype(bf16)
    padded = jnp.concatenate([head, jnp.zeros_like(head)], axis=0)
    values = dot(residual.astype(bf16), padded, ((1,), (1,)))
    lanes = lax.broadcasted_iota(jnp.int32, values.shape, 1)
    for n, column in enumerate(halves(centre) + halves(spread)):
        values = jnp.where(lanes == latent_dim + n, column, values)
    values = values.astype(bf16)
    sums = jnp.sum(head.astype(f32), axis=1, keepdims=True)
    consts = jnp.sum(plain_head * shifts_ref[3], axis=1, keepdims=True)
    place = lax.broadcasted_iota(jnp.int32, (latent_dim, 128), 1)
    extra = jnp.zeros((latent_dim, 128), f32)
    for n, column in enumerate(halves(sums) + halves(consts)):
        extra = jnp.where(place == n, column, extra)
    extra = jnp.concatenate([extra, jnp.zeros_like(extra)], axis=0).T[:16].astype(bf16)
    piece = rows // n_fsdp
    for f in range(n_fsdp):
        for s in range(sections):
            out_ref[s * n_fsdp + f, :piece] = values[f * piece : (f + 1) * piece]
            out_ref[s * n_fsdp + f, piece:] = extra


def estimate_kernel(sections, width, where_ref, levels_ref, partial_ref, student_ref, noised_ref, group_ref, grad_ref, out_ref):
    piece, latent_dim = student_ref.shape
    count = partial_ref.shape[0] // sections
    estimates = []
    for p in range(sections):
        blocks = [partial_ref[p * count + i].astype(f32) for i in range(count)]

        def column(b, n):
            at = latent_dim + n
            return b[:piece, at : at + 1] + b[:piece, at + 1 : at + 2]

        def line(b, n):
            at = piece + n
            return b[at : at + 1, :latent_dim] + b[at + 1 : at + 2, :latent_dim]

        means = [column(b, 0) for b in blocks]
        mean = sum(means) / count
        linear, spread, shift = 0.0, 0.0, 0.0
        for b, m in zip(blocks, means):
            offset = m - mean
            linear += b[:piece, :latent_dim] + offset * line(b, 0)
            spread += column(b, 2) + (width // count) * (offset * offset)
            shift += line(b, 2)
        velocity = linear * lax.rsqrt(spread / width + 1e-06) + shift
        latent = (student_ref if p == 0 else noised_ref)[...].astype(f32)
        estimates.append(latent - levels_ref[0 if p == 0 else 1] * velocity)
    group_ref[...] = estimates[0]
    teacher = estimates[2] + guidance_scale * (estimates[1] - estimates[2])
    grad = estimates[3] - teacher
    grad_ref[...] = grad
    velocity_grad = -levels_ref[2] * grad
    padded = jnp.concatenate([velocity_grad, jnp.zeros_like(velocity_grad)], axis=1).astype(bf16)
    out_ref[...] = jnp.broadcast_to(padded[None], out_ref.shape)


def gradient_kernel(where_ref, grad_ref, feature_ref, out_ref):
    count, lines, pair = out_ref.shape
    rows = grad_ref.shape[1]
    slot = feature_ref.shape[1] - 2 * rows
    latent_dim, half = pair // 2, slot // 2
    grads = grad_ref[...].reshape(-1, grad_ref.shape[2])
    joined = jnp.concatenate(
        [
            dot(feature_ref[:, at : at + rows].reshape(count * rows, -1), grads, ((0,), (0,)))[:, :latent_dim]
            for at in (slot, slot + rows)
        ],
        axis=0,
    )
    spare = jnp.zeros((lines - half, pair), f32)
    for i in range(count):
        at = i * slot
        block = jnp.concatenate([joined[at : at + half], joined[at + half : at + slot]], axis=1)
        out_ref[i] = jnp.concatenate([block, spare], axis=0).astype(bf16)


def sum_kernel(where_ref, part_ref, out_ref):
    latent_dim, slot = out_ref.shape
    total = part_ref[0].astype(f32)
    for i in range(1, part_ref.shape[0]):
        total += part_ref[i].astype(f32)
    half = slot // 2
    out_ref[...] = jnp.concatenate([total[:half, :latent_dim], total[:half, latent_dim:]], axis=0).T


def per_device(
    student_input,
    previous_latent,
    score_noise,
    timesteps,
    modulation,
    in_weight,
    qkv_weight,
    out_weight,
    head_weight,
    kv_cache,
    saved_features,
):
    section, me_seq, me_fsdp = (lax.axis_index(a) for a in ("section", "seq", "fsdp"))
    sections, n_seq, n_fsdp = (lax.axis_size(a) for a in ("section", "seq", "fsdp"))
    model_index = section - (section >= 2).astype(jnp.int32)
    where = jnp.concatenate([jnp.stack([model_index, me_seq, me_fsdp, section]).astype(jnp.int32), timesteps])
    levels = noise_levels(timesteps)
    rows, latent_dim = student_input.shape
    width = in_weight.shape[2]
    depth, feat = qkv_weight.shape[1], qkv_weight.shape[3]
    heads = feat // HEAD_DIM
    piece = rows // n_fsdp
    shifts = modulation.transpose(1, 0, 2)
    slot = depth // n_fsdp

    lines = 2 * rows + 4 * latent_dim
    own, plain = run(
        prepare_kernel,
        where,
        [((lines, feat), bf16), ((latent_dim, rows), bf16)],
        in_weight,
        qkv_weight.transpose(0, 2, 1, 3),
        shifts,
        student_input.T,
        previous_latent.T,
        score_noise.T,
        kv_cache[0].transpose(1, 0, 2).reshape(2 * rows, feat),
        picked=(0, 1),
        raw=(2, 3, 4, 5, 6),
        scratch=[
            pltpu.VMEM(shifts.shape, f32),
            pltpu.VMEM((latent_dim, rows), bf16),
            pltpu.VMEM((latent_dim, rows), bf16),
            pltpu.VMEM((latent_dim, rows), bf16),
            pltpu.SemaphoreType.DMA((5,)),
        ],
    )
    cut = run(aside_kernel, together(where, own), [((n_fsdp, slot + 2 * piece, feat), bf16)], out_weight, saved_features, picked=(0,))
    aside = exchange(cut, "fsdp")
    embed_here, head_here, shifts_here = run(
        columns_kernel,
        together(where, own),
        [((latent_dim, depth), bf16), ((latent_dim, depth), bf16), ((shifts.shape[0], 1, depth), f32)],
        in_weight,
        head_weight.transpose(0, 2, 1),
        shifts,
        picked=(0, 1),
    )
    around = Ring(own, "seq", n_seq, 0)
    around.step()
    around.step()
    block, *_ = lax.optimization_barrier((aside[:, :slot],) + around.ends())
    weights = Ring(block, "seq", n_seq, 0)
    around.step()
    weights.step()
    around.finish()
    weights.step()
    blocks = around.blocks()
    attended = run(
        functools.partial(attention_kernel, heads, latent_dim),
        together(where, embed_here, *weights.ends()),
        [((n_fsdp, rows, feat), bf16)],
        *blocks,
        scratch=[
            pltpu.VMEM((n_seq, lines, feat), bf16),
            pltpu.VMEM((n_seq, 2 * rows, feat), bf16),
            pltpu.SemaphoreType.DMA((2 * len(blocks),)),
        ],
        raw=range(len(blocks)),
        cost=pl.CostEstimate(flops=11 * 10**9, bytes_accessed=20 * 10**6, transcendentals=3 * 10**6),
    )
    weights.step()
    attended = exchange(together(attended, *weights.ends()), "fsdp")
    weights.finish()
    partials = run(
        functools.partial(head_kernel, sections),
        where,
        [((sections * n_fsdp, piece + 16, 128), bf16)],
        plain,
        embed_here,
        shifts_here,
        head_here,
        attended,
        *weights.blocks(),
    )
    partials = exchange(partials, ("section", "fsdp"))

    noised = (
        (1.0 - levels[1]) * previous_latent.astype(f32) + levels[1] * score_noise.astype(f32)
    ).astype(bf16)
    own_student = lax.dynamic_slice_in_dim(student_input, me_fsdp * piece, piece, 0)
    own_noised = lax.dynamic_slice_in_dim(noised, me_fsdp * piece, piece, 0)
    student_group, dmd_grad, grads = run(
        functools.partial(estimate_kernel, sections, width),
        where,
        [((piece, latent_dim), f32), ((piece, latent_dim), f32), ((n_fsdp, piece, 2 * latent_dim), bf16)],
        levels,
        partials,
        own_student,
        own_noised,
    )
    grads = exchange(grads, "fsdp")
    partial_grad = run(
        gradient_kernel, where, [((n_seq, (slot // 2 + 15) // 16 * 16, 2 * latent_dim), bf16)], grads, aside
    )
    head_grad = run(sum_kernel, where, [((latent_dim, slot), f32)], exchange(partial_grad, "seq")).T
    return (student_group, dmd_grad, head_grad)


def solution(mesh):
    placed = (
        P("seq", None),
        P("seq", None),
        P("seq", None),
        P(),
        P("section", None, None),
        P(),
        P(None, "seq", None, "fsdp"),
        P(None, "seq", "fsdp"),
        P(),
        P("section", "seq", None, "fsdp"),
        P(("seq", "fsdp"), None),
    )
    return jax.shard_map(
        per_device,
        mesh=mesh,
        in_specs=placed,
        out_specs=(P(("seq", "fsdp"), None), P(("seq", "fsdp"), None), P(("seq", "fsdp"), None)),
        check_vma=False,
    )
```

```python
import functools

import jax
import jax.numpy as jnp
from jax import lax
from jax.experimental import pallas as pl
from jax.experimental.pallas import tpu as pltpu
from jax.sharding import PartitionSpec as P

HEAD_DIM = 128
LOG2E = 1.4426950408889634
guidance_scale = 5.0
bf16 = jnp.bfloat16
f32 = jnp.float32


def run(kernel, where, outs, *operands, picked=(), scratch=(), raw=(), cost=None):
    def spec(shape, pick=False):
        zeros = (0,) * (len(shape) - 1)
        if pick:
            return pl.BlockSpec((1,) + tuple(shape[1:]), lambda i, w: (w[0],) + zeros)
        return pl.BlockSpec(tuple(shape), lambda i, w: (0,) + zeros)

    in_specs = [
        pl.BlockSpec(memory_space=pltpu.SMEM)
        if x.ndim == 1
        else pl.BlockSpec(memory_space=pltpu.HBM)
        if n in raw
        else spec(x.shape, n in picked)
        for n, x in enumerate(operands)
    ]
    result = pl.pallas_call(
        kernel,
        grid_spec=pltpu.PrefetchScalarGridSpec(
            num_scalar_prefetch=1,
            grid=(1,),
            in_specs=in_specs,
            out_specs=tuple(spec(shape) for shape, _ in outs),
            scratch_shapes=list(scratch),
        ),
        out_shape=tuple(jax.ShapeDtypeStruct(shape, dtype) for shape, dtype in outs),
        compiler_params=pltpu.CompilerParams(vmem_limit_bytes=52 * 1024 * 1024),
        cost_estimate=cost,
    )(where, *operands)
    return result[0] if len(outs) == 1 else result


def together(value, *others):
    return lax.optimization_barrier((value,) + others)[0]


def noise_levels(steps):
    remain = 1.0 - steps.astype(f32) / 1000.0
    return 5.0 * remain / (1.0 + 4.0 * remain)


def select_model(stacked, model_index):
    return lax.dynamic_index_in_dim(stacked, model_index, 0, keepdims=False)


def exchange(blocks, axis):
    return lax.all_to_all(blocks, axis, 0, 0, tiled=True)


class Ring:
    def __init__(self, block, axis, count, split, split_at=None):
        self.split_at = split_at
        self.axis, self.split, self.half = axis, split, count // 2
        self.up = [(i, (i + 1) % count) for i in range(count)]
        self.down = [(i, (i - 1) % count) for i in range(count)]
        self.behind, self.ahead, self.last = [block], [block], []

    def step(self):
        self.behind.append(lax.ppermute(self.behind[-1], self.axis, self.up))
        self.ahead.append(lax.ppermute(self.ahead[-1], self.axis, self.down))

    def ends(self):
        return self.behind[-1], self.ahead[-1]

    def after(self, other):
        self.behind[-1], self.ahead[-1], *_ = lax.optimization_barrier(self.ends() + other.ends())

    def finish(self):
        while len(self.behind) < self.half:
            self.step()
        total = self.behind[0].shape[self.split]
        size = total // 2 if self.split_at is None else self.split_at
        first = lax.slice_in_dim(self.behind[-1], 0, size, axis=self.split)
        second = lax.slice_in_dim(self.ahead[-1], size, total, axis=self.split)
        self.last = [lax.ppermute(first, self.axis, self.up), lax.ppermute(second, self.axis, self.down)]

    def blocks(self):
        return self.behind + self.ahead[1:] + self.last


def dot(a, b, over):
    return lax.dot_general(a, b, ((over[0], over[1]), ((), ())), preferred_element_type=f32)


def prepare_kernel(
    where_ref, embed_ref, weight_ref, shifts_hbm, student_hbm, previous_hbm, noise_hbm, context_hbm, *refs
):
    out_ref, plain_ref, shifts_ref, student_ref, previous_ref, noise_ref, sems = refs
    latent_dim, width = embed_ref.shape[1:]
    parts, depth, feat = weight_ref.shape[1:]
    rows = student_ref.shape[1]
    sources = (shifts_hbm, student_hbm, previous_hbm, noise_hbm, context_hbm)
    targets = (shifts_ref, student_ref, previous_ref, noise_ref, out_ref.at[pl.ds(0, 2 * rows)])
    copies = [pltpu.make_async_copy(a, b, sems.at[n]) for n, (a, b) in enumerate(zip(sources, targets))]
    for copy in copies:
        copy.start()
    for copy in copies:
        copy.wait()
    level = noise_levels(jnp.full((1, rows), where_ref[5], jnp.int32))
    noised = (1.0 - level) * previous_ref[...].astype(f32) + level * noise_ref[...].astype(f32)
    latents = jnp.where(where_ref[3] == 0, student_ref[...].astype(f32), noised.astype(bf16).astype(f32))

    step = 1024
    row_sum = jnp.zeros((latent_dim, 1), f32)
    for first in range(0, width, step):
        row_sum += jnp.sum(embed_ref[0, :, first : first + step].astype(f32), axis=1, keepdims=True)
    row_mean = row_sum / width

    here = pl.ds(pl.multiple_of(where_ref[1] * depth, 128), depth)
    centred = (embed_ref[0, :, here].astype(f32) - row_mean) * (1.0 + shifts_ref[1, :, here])
    shift = jnp.broadcast_to(shifts_ref[0, :, here], (16, depth))
    folded = jnp.concatenate([centred, shift], axis=0).astype(bf16)
    tail = 2 * rows + parts * latent_dim
    lines = []
    for i in range(parts):
        table = dot(folded, weight_ref[0, i], ((1,), (0,)))
        at = 2 * rows + i * latent_dim
        out_ref[at : at + latent_dim] = table[:latent_dim].astype(bf16)
        lines += [table[latent_dim : latent_dim + 1, n : n + 128] for n in range(0, feat, 128)]

    mean = jnp.sum(row_mean * latents, axis=0, keepdims=True)
    plain = latents.astype(bf16)
    spread = jnp.zeros((1, rows), f32)
    for first in range(0, width, step):
        hidden = dot(embed_ref[0, :, first : first + step], plain, ((0,), (0,))) - mean
        spread += jnp.sum(hidden * hidden, axis=0, keepdims=True)
    inverse = lax.rsqrt(spread / width + 1e-06)
    out_ref[tail:, :rows] = (latents * inverse).astype(bf16)
    plain_ref[...] = plain
    spare = jnp.zeros((latent_dim - len(lines), 128), f32)
    out_ref[tail:, rows:] = jnp.concatenate(lines + [spare], axis=0).astype(bf16)


def aside_kernel(where_ref, weight_ref, feature_ref, out_ref):
    count, lines, feat = out_ref.shape
    rows, width = feature_ref.shape
    slot = weight_ref.shape[1] // count
    part = width // count
    out_ref[:, :slot] = weight_ref[0].reshape(count, slot, feat)
    spare = jnp.zeros((rows, 2 * feat - part), bf16)
    for j in range(count):
        pieces = [feature_ref[:, s * part + j * slot : s * part + (j + 1) * slot] for s in range(count)]
        joined = jnp.concatenate(pieces + [spare], axis=1)
        out_ref[j, slot : slot + rows] = joined[:, :feat]
        out_ref[j, slot + rows :] = joined[:, feat:]


def columns_kernel(where_ref, embed_ref, head_ref, shifts_ref, embed_out, head_out, shifts_out):
    count = 8
    part = embed_ref.shape[2] // count
    slot = part // count
    half = count // 2
    order = [0] + [count - d for d in range(1, half)] + list(range(1, half + 1))
    for f in range(count):

        @pl.when(where_ref[2] == f)
        def _(f=f):
            sources = [(embed_ref.at[0], embed_out), (head_ref.at[0], head_out)]
            sources += [(shifts_ref.at[i], shifts_out.at[i]) for i in range(shifts_ref.shape[0])]
            for source, target in sources:
                pieces = []
                for d in order:
                    owner = lax.rem(where_ref[1] + d, count)
                    block = source[:, pl.ds(pl.multiple_of(owner * part, 128), part)]
                    pieces.append(block[:, f * slot : (f + 1) * slot])
                target[...] = jnp.concatenate(pieces, axis=1)


def fold_keys(heads, carry, queries, keys, values):
    scores = [dot(keys(h), queries[:, h * HEAD_DIM : (h + 1) * HEAD_DIM], ((1,), (1,))) for h in range(heads)]
    new = []
    for h in range(heads):
        top, total, weighted = carry[h]
        new_top = jnp.maximum(top, jnp.max(scores[h], axis=0, keepdims=True))
        weights = jnp.exp2(scores[h] - new_top)
        keep = jnp.exp2(top - new_top)
        total = total * keep + jnp.sum(weights, axis=0, keepdims=True)
        weighted = weighted * keep + dot(values(h), weights.astype(bf16), ((0,), (0,)))
        new.append((new_top, total, weighted))
    return tuple(new)


def attention_kernel(heads, latent_dim, where_ref, *refs):
    n_blocks = len(refs) - 4
    block_refs, (out_ref, all_ref, held_ref, sems) = refs[:n_blocks], refs[n_blocks:]
    count, lines, feat = all_ref.shape
    rows = out_ref.shape[1]
    at = [(n, 0, ref.shape[0]) for n, ref in enumerate(block_refs[:-1])]
    at.append((count - 1, block_refs[-2].shape[0], block_refs[-1].shape[0]))
    early, late = [], []
    for ref, (n, place, size) in zip(block_refs, at):
        for first, last, group in ((0, 2 * rows, late), (2 * rows, lines, early)):
            first, last = max(first, place), min(last, place + size)
            if first < last:
                copies = len(early) + len(late)
                group.append(
                    pltpu.make_async_copy(
                        ref.at[pl.ds(first - place, last - first)],
                        all_ref.at[n, pl.ds(first, last - first)],
                        sems.at[copies],
                    )
                )
    for copy in early + late:
        copy.start()
    for copy in early:
        copy.wait()

    tail = 2 * rows + 3 * latent_dim
    parts = [slice(2 * rows + i * latent_dim, 2 * rows + (i + 1) * latent_dim) for i in range(3)]
    tables = [sum(all_ref[n, at].astype(f32) for n in range(count)).astype(bf16) for at in parts]
    shift = sum(all_ref[n, tail : tail + 16, rows:].astype(f32) for n in range(count))
    shifts = [
        jnp.concatenate([shift[i * heads + h : i * heads + h + 1] for h in range(heads)], axis=1) for i in range(3)
    ]

    def project(n, which):
        latents = all_ref[n, tail : tail + latent_dim, :rows]
        return [dot(latents, tables[i], ((0,), (0,))) + shifts[i] for i in which]

    queries = (project(0, (0,))[0] * (HEAD_DIM ** (-0.5) * LOG2E)).astype(bf16)

    def fill(n, _):
        keys, values = project(n, (1, 2))
        held_ref[n, :rows] = keys.astype(bf16)
        held_ref[n, rows:] = values.astype(bf16)
        return 0

    lax.fori_loop(0, count, fill, 0, unroll=4)
    carry = tuple(
        (jnp.full((1, rows), -1e30, f32), jnp.zeros((1, rows), f32), jnp.zeros((HEAD_DIM, rows), f32))
        for _ in range(heads)
    )

    def four(ref, i, carry):
        def both(first, h):
            cols = slice(h * HEAD_DIM, (h + 1) * HEAD_DIM)
            return jnp.concatenate([ref[4 * i + n, first : first + rows, cols] for n in range(4)], axis=0)

        return fold_keys(heads, carry, queries, lambda h: both(0, h), lambda h: both(rows, h))

    carry = lax.fori_loop(0, count // 4, lambda i, c: four(held_ref, i, c), carry, unroll=2)
    for copy in late:
        copy.wait()
    carry = lax.fori_loop(0, count // 4, lambda i, c: four(all_ref, i, c), carry, unroll=2)
    for h in range(heads):
        _, total, weighted = carry[h]
        attended = (weighted / total).T.astype(bf16)
        out_ref[:, :, h * HEAD_DIM : (h + 1) * HEAD_DIM] = jnp.broadcast_to(
            attended[None], (out_ref.shape[0], rows, HEAD_DIM)
        )


def halves(value):
    high = value.astype(bf16).astype(f32)
    return high, value - high


def head_kernel(sections, where_ref, own_ref, embed_ref, shifts_ref, head_ref, att_ref, *refs):
    weight_refs, out_ref = refs[:-1], refs[-1]
    n_fsdp, rows = att_ref.shape[:2]
    latent_dim = embed_ref.shape[0]
    mixed = None
    for f in range(n_fsdp):
        whole = [ref[f] for ref in weight_refs[:-2]]
        whole.append(weight_refs[-2][f] if f < n_fsdp // 2 else weight_refs[-1][f - n_fsdp // 2])
        part = dot(att_ref[f], jnp.concatenate(whole, axis=0), ((1,), (1,)))
        mixed = part if mixed is None else mixed + part
    residual = dot(own_ref[...], embed_ref[...], ((0,), (0,))) + shifts_ref[2] * mixed
    centre = jnp.mean(residual, axis=1, keepdims=True)
    residual = residual - centre
    spread = jnp.sum(residual * residual, axis=1, keepdims=True)
    plain_head = head_ref[...].astype(f32)
    head = (plain_head * (1.0 + shifts_ref[4])).astype(bf16)
    padded = jnp.concatenate([head, jnp.zeros_like(head)], axis=0)
    values = dot(residual.astype(bf16), padded, ((1,), (1,)))
    lanes = lax.broadcasted_iota(jnp.int32, values.shape, 1)
    for n, column in enumerate(halves(centre) + halves(spread)):
        values = jnp.where(lanes == latent_dim + n, column, values)
    values = values.astype(bf16)
    sums = jnp.sum(head.astype(f32), axis=1, keepdims=True)
    consts = jnp.sum(plain_head * shifts_ref[3], axis=1, keepdims=True)
    place = lax.broadcasted_iota(jnp.int32, (latent_dim, 128), 1)
    extra = jnp.zeros((latent_dim, 128), f32)
    for n, column in enumerate(halves(sums) + halves(consts)):
        extra = jnp.where(place == n, column, extra)
    extra = jnp.concatenate([extra, jnp.zeros_like(extra)], axis=0).T[:16].astype(bf16)
    piece = rows // n_fsdp
    for f in range(n_fsdp):
        for s in range(sections):
            out_ref[s * n_fsdp + f, :piece] = values[f * piece : (f + 1) * piece]
            out_ref[s * n_fsdp + f, piece:] = extra


def estimate_kernel(sections, width, where_ref, levels_ref, partial_ref, student_ref, noised_ref, group_ref, grad_ref, out_ref):
    piece, latent_dim = student_ref.shape
    count = partial_ref.shape[0] // sections
    estimates = []
    for p in range(sections):
        blocks = [partial_ref[p * count + i].astype(f32) for i in range(count)]

        def column(b, n):
            at = latent_dim + n
            return b[:piece, at : at + 1] + b[:piece, at + 1 : at + 2]

        def line(b, n):
            at = piece + n
            return b[at : at + 1, :latent_dim] + b[at + 1 : at + 2, :latent_dim]

        means = [column(b, 0) for b in blocks]
        mean = sum(means) / count
        linear, spread, shift = 0.0, 0.0, 0.0
        for b, m in zip(blocks, means):
            offset = m - mean
            linear += b[:piece, :latent_dim] + offset * line(b, 0)
            spread += column(b, 2) + (width // count) * (offset * offset)
            shift += line(b, 2)
        velocity = linear * lax.rsqrt(spread / width + 1e-06) + shift
        latent = (student_ref if p == 0 else noised_ref)[...].astype(f32)
        estimates.append(latent - levels_ref[0 if p == 0 else 1] * velocity)
    group_ref[...] = estimates[0]
    teacher = estimates[2] + guidance_scale * (estimates[1] - estimates[2])
    grad = estimates[3] - teacher
    grad_ref[...] = grad
    velocity_grad = -levels_ref[2] * grad
    padded = jnp.concatenate([velocity_grad, jnp.zeros_like(velocity_grad)], axis=1).astype(bf16)
    out_ref[...] = jnp.broadcast_to(padded[None], out_ref.shape)


def gradient_kernel(where_ref, grad_ref, feature_ref, out_ref):
    count, lines, pair = out_ref.shape
    rows = grad_ref.shape[1]
    slot = feature_ref.shape[1] - 2 * rows
    latent_dim, half = pair // 2, slot // 2
    grads = grad_ref[...].reshape(-1, grad_ref.shape[2])
    joined = jnp.concatenate(
        [
            dot(feature_ref[:, at : at + rows].reshape(count * rows, -1), grads, ((0,), (0,)))[:, :latent_dim]
            for at in (slot, slot + rows)
        ],
        axis=0,
    )
    spare = jnp.zeros((lines - half, pair), f32)
    for i in range(count):
        at = i * slot
        block = jnp.concatenate([joined[at : at + half], joined[at + half : at + slot]], axis=1)
        out_ref[i] = jnp.concatenate([block, spare], axis=0).astype(bf16)


def sum_kernel(where_ref, part_ref, out_ref):
    latent_dim, slot = out_ref.shape
    total = part_ref[0].astype(f32)
    for i in range(1, part_ref.shape[0]):
        total += part_ref[i].astype(f32)
    half = slot // 2
    out_ref[...] = jnp.concatenate([total[:half, :latent_dim], total[:half, latent_dim:]], axis=0).T


def per_device(
    student_input,
    previous_latent,
    score_noise,
    timesteps,
    modulation,
    in_weight,
    qkv_weight,
    out_weight,
    head_weight,
    kv_cache,
    saved_features,
):
    section, me_seq, me_fsdp = (lax.axis_index(a) for a in ("section", "seq", "fsdp"))
    sections, n_seq, n_fsdp = (lax.axis_size(a) for a in ("section", "seq", "fsdp"))
    model_index = section - (section >= 2).astype(jnp.int32)
    where = jnp.concatenate([jnp.stack([model_index, me_seq, me_fsdp, section]).astype(jnp.int32), timesteps])
    levels = noise_levels(timesteps)
    rows, latent_dim = student_input.shape
    width = in_weight.shape[2]
    depth, feat = qkv_weight.shape[1], qkv_weight.shape[3]
    heads = feat // HEAD_DIM
    piece = rows // n_fsdp
    shifts = modulation.transpose(1, 0, 2)
    slot = depth // n_fsdp

    lines = 2 * rows + 4 * latent_dim
    own, plain = run(
        prepare_kernel,
        where,
        [((lines, feat), bf16), ((latent_dim, rows), bf16)],
        in_weight,
        qkv_weight.transpose(0, 2, 1, 3),
        shifts,
        student_input.T,
        previous_latent.T,
        score_noise.T,
        kv_cache[0].transpose(1, 0, 2).reshape(2 * rows, feat),
        picked=(0, 1),
        raw=(2, 3, 4, 5, 6),
        scratch=[
            pltpu.VMEM(shifts.shape, f32),
            pltpu.VMEM((latent_dim, rows), bf16),
            pltpu.VMEM((latent_dim, rows), bf16),
            pltpu.VMEM((latent_dim, rows), bf16),
            pltpu.SemaphoreType.DMA((5,)),
        ],
    )
    cut = run(aside_kernel, together(where, own), [((n_fsdp, slot + 2 * piece, feat), bf16)], out_weight, saved_features, picked=(0,))
    aside = exchange(cut, "fsdp")
    embed_here, head_here, shifts_here = run(
        columns_kernel,
        together(where, own),
        [((latent_dim, depth), bf16), ((latent_dim, depth), bf16), ((shifts.shape[0], 1, depth), f32)],
        in_weight,
        head_weight.transpose(0, 2, 1),
        shifts,
        picked=(0, 1),
    )
    around = Ring(own, "seq", n_seq, 0)
    around.step()
    block, *_ = lax.optimization_barrier((aside[:, :slot],) + around.ends())
    weights = Ring(block, "seq", n_seq, 0)
    weights.step()
    around.step()
    around.step()
    weights.after(around)
    around.finish()
    weights.step()
    blocks = around.blocks()
    attended = run(
        functools.partial(attention_kernel, heads, latent_dim),
        together(where, embed_here),
        [((n_fsdp, rows, feat), bf16)],
        *blocks,
        scratch=[
            pltpu.VMEM((n_seq, lines, feat), bf16),
            pltpu.VMEM((n_seq, 2 * rows, feat), bf16),
            pltpu.SemaphoreType.DMA((2 * len(blocks),)),
        ],
        raw=range(len(blocks)),
        cost=pl.CostEstimate(flops=11 * 10**9, bytes_accessed=20 * 10**6, transcendentals=3 * 10**6),
    )
    attended = exchange(together(attended, *weights.ends()), "fsdp")
    weights.finish()
    partials = run(
        functools.partial(head_kernel, sections),
        where,
        [((sections * n_fsdp, piece + 16, 128), bf16)],
        plain,
        embed_here,
        shifts_here,
        head_here,
        attended,
        *weights.blocks(),
    )
    partials = exchange(partials, ("section", "fsdp"))

    noised = (
        (1.0 - levels[1]) * previous_latent.astype(f32) + levels[1] * score_noise.astype(f32)
    ).astype(bf16)
    own_student = lax.dynamic_slice_in_dim(student_input, me_fsdp * piece, piece, 0)
    own_noised = lax.dynamic_slice_in_dim(noised, me_fsdp * piece, piece, 0)
    student_group, dmd_grad, grads = run(
        functools.partial(estimate_kernel, sections, width),
        where,
        [((piece, latent_dim), f32), ((piece, latent_dim), f32), ((n_fsdp, piece, 2 * latent_dim), bf16)],
        levels,
        partials,
        own_student,
        own_noised,
    )
    grads = exchange(grads, "fsdp")
    partial_grad = run(
        gradient_kernel, where, [((n_seq, (slot // 2 + 15) // 16 * 16, 2 * latent_dim), bf16)], grads, aside
    )
    head_grad = run(sum_kernel, where, [((latent_dim, slot), f32)], exchange(partial_grad, "seq")).T
    return (student_group, dmd_grad, head_grad)


def solution(mesh):
    placed = (
        P("seq", None),
        P("seq", None),
        P("seq", None),
        P(),
        P("section", None, None),
        P(),
        P(None, "seq", None, "fsdp"),
        P(None, "seq", "fsdp"),
        P(),
        P("section", "seq", None, "fsdp"),
        P(("seq", "fsdp"), None),
    )
    return jax.shard_map(
        per_device,
        mesh=mesh,
        in_specs=placed,
        out_specs=(P(("seq", "fsdp"), None), P(("seq", "fsdp"), None), P(("seq", "fsdp"), None)),
        check_vma=False,
    )
```

```python
import functools

import jax
import jax.numpy as jnp
from jax import lax
from jax.experimental import pallas as pl
from jax.experimental.pallas import tpu as pltpu
from jax.sharding import PartitionSpec as P

HEAD_DIM = 128
LOG2E = 1.4426950408889634
guidance_scale = 5.0
bf16 = jnp.bfloat16
f32 = jnp.float32


def run(kernel, where, outs, *operands, picked=(), scratch=(), raw=(), inside=(), held=False, cost=None, room=52):
    def spec(shape, pick=False):
        zeros = (0,) * (len(shape) - 1)
        if pick:
            return pl.BlockSpec((1,) + tuple(shape[1:]), lambda i, w: (w[0],) + zeros)
        return pl.BlockSpec(tuple(shape), lambda i, w: (0,) + zeros)

    in_specs = [
        pl.BlockSpec(memory_space=pltpu.SMEM)
        if x.ndim == 1
        else pl.BlockSpec(memory_space=pltpu.VMEM)
        if n in inside
        else pl.BlockSpec(memory_space=pltpu.HBM)
        if n in raw
        else spec(x.shape, n in picked)
        for n, x in enumerate(operands)
    ]
    result = pl.pallas_call(
        kernel,
        grid_spec=pltpu.PrefetchScalarGridSpec(
            num_scalar_prefetch=1,
            grid=(1,),
            in_specs=in_specs,
            out_specs=tuple(pl.BlockSpec(memory_space=pltpu.VMEM) if held else spec(shape) for shape, _ in outs),
            scratch_shapes=list(scratch),
        ),
        out_shape=tuple(jax.ShapeDtypeStruct(shape, dtype) for shape, dtype in outs),
        compiler_params=pltpu.CompilerParams(vmem_limit_bytes=room * 1024 * 1024),
        cost_estimate=cost,
    )(where, *operands)
    return result[0] if len(outs) == 1 else result


def together(value, *others):
    return lax.optimization_barrier((value,) + others)[0]


def noise_levels(steps):
    remain = 1.0 - steps.astype(f32) / 1000.0
    return 5.0 * remain / (1.0 + 4.0 * remain)


def select_model(stacked, model_index):
    return lax.dynamic_index_in_dim(stacked, model_index, 0, keepdims=False)


def exchange(blocks, axis):
    return lax.all_to_all(blocks, axis, 0, 0, tiled=True)


class Ring:
    def __init__(self, block, axis, count, split, split_at=None):
        self.split_at = split_at
        self.axis, self.split, self.half = axis, split, count // 2
        self.up = [(i, (i + 1) % count) for i in range(count)]
        self.down = [(i, (i - 1) % count) for i in range(count)]
        self.behind, self.ahead, self.last = [block], [block], []

    def step(self):
        self.behind.append(lax.ppermute(self.behind[-1], self.axis, self.up))
        self.ahead.append(lax.ppermute(self.ahead[-1], self.axis, self.down))

    def ends(self):
        return self.behind[-1], self.ahead[-1]

    def after(self, other):
        self.behind[-1], self.ahead[-1], *_ = lax.optimization_barrier(self.ends() + other.ends())

    def finish(self):
        while len(self.behind) < self.half:
            self.step()
        total = self.behind[0].shape[self.split]
        size = total // 2 if self.split_at is None else self.split_at
        first = lax.slice_in_dim(self.behind[-1], 0, size, axis=self.split)
        second = lax.slice_in_dim(self.ahead[-1], size, total, axis=self.split)
        self.last = [lax.ppermute(first, self.axis, self.up), lax.ppermute(second, self.axis, self.down)]

    def blocks(self):
        return self.behind + self.ahead[1:] + self.last


def dot(a, b, over):
    return lax.dot_general(a, b, ((over[0], over[1]), ((), ())), preferred_element_type=f32)


def prepare_kernel(
    where_ref, embed_hbm, weight_hbm, shifts_hbm, student_hbm, previous_hbm, noise_hbm, context_hbm, *refs
):
    out_ref, plain_ref, embed_ref, weight_ref, shifts_ref, student_ref, previous_ref, noise_ref, context_ref, sems = refs
    latent_dim, width = embed_ref.shape[1:]
    parts, depth, feat = weight_ref.shape[1:]
    rows = student_ref.shape[1]
    model = pl.ds(where_ref[0], 1)
    sources = (embed_hbm.at[model], shifts_hbm, student_hbm, previous_hbm, noise_hbm, weight_hbm.at[model], context_hbm)
    targets = (embed_ref, shifts_ref, student_ref, previous_ref, noise_ref, weight_ref, context_ref)
    copies = [pltpu.make_async_copy(a, b, sems.at[n]) for n, (a, b) in enumerate(zip(sources, targets))]
    for copy in copies:
        copy.start()
    for copy in copies[:5]:
        copy.wait()
    level = noise_levels(jnp.full((1, rows), where_ref[5], jnp.int32))
    noised = (1.0 - level) * previous_ref[...].astype(f32) + level * noise_ref[...].astype(f32)
    latents = jnp.where(where_ref[3] == 0, student_ref[...].astype(f32), noised.astype(bf16).astype(f32))

    step = 1024
    row_sum = jnp.zeros((latent_dim, 1), f32)
    for first in range(0, width, step):
        row_sum += jnp.sum(embed_ref[0, :, first : first + step].astype(f32), axis=1, keepdims=True)
    row_mean = row_sum / width

    mean = jnp.sum(row_mean * latents, axis=0, keepdims=True)
    plain = latents.astype(bf16)
    spread = jnp.zeros((1, rows), f32)
    for first in range(0, width, step):
        hidden = dot(embed_ref[0, :, first : first + step], plain, ((0,), (0,))) - mean
        spread += jnp.sum(hidden * hidden, axis=0, keepdims=True)
    inverse = lax.rsqrt(spread / width + 1e-06)
    heads = feat // HEAD_DIM
    scaled = (latents * inverse).astype(bf16)
    tail = (2 * rows + parts * latent_dim) * heads
    for n in range(rows // 128):
        out_ref[tail + n * latent_dim : tail + (n + 1) * latent_dim] = scaled[:, n * 128 : (n + 1) * 128]
    plain_ref[...] = plain
    for copy in copies[5:]:
        copy.wait()
    here = pl.ds(pl.multiple_of(where_ref[1] * depth, 128), depth)
    centred = (embed_ref[0, :, here].astype(f32) - row_mean) * (1.0 + shifts_ref[1, :, here])
    shift = jnp.broadcast_to(shifts_ref[0, :, here], (16, depth))
    folded = jnp.concatenate([centred, shift], axis=0).astype(bf16)
    lines = []
    for i in range(parts):
        table = dot(folded, weight_ref[0, i], ((1,), (0,)))
        for h in range(heads):
            at = 2 * rows * heads + (i * heads + h) * latent_dim
            out_ref[at : at + latent_dim] = table[:latent_dim, h * 128 : (h + 1) * 128].astype(bf16)
        lines += [table[latent_dim : latent_dim + 1, n : n + 128] for n in range(0, feat, 128)]
    spare = jnp.zeros((16 - len(lines), 128), f32)
    out_ref[tail + rows // 128 * latent_dim :] = jnp.concatenate(lines + [spare], axis=0).astype(bf16)
    for h in range(heads):
        cols = slice(h * 128, (h + 1) * 128)
        out_ref[h * rows : (h + 1) * rows] = context_ref[:rows, cols]
        values = context_ref[rows:, cols].astype(f32).T.astype(bf16)
        for n in range(rows // 128):
            at = heads * rows + h * rows + n * 128
            out_ref[at : at + 128] = values[:, n * 128 : (n + 1) * 128]


def aside_kernel(where_ref, weight_ref, feature_ref, out_ref):
    count, lines, feat = out_ref.shape
    rows, width = feature_ref.shape
    slot = weight_ref.shape[1] // count
    part = width // count
    out_ref[:, :slot] = weight_ref[0].reshape(count, slot, feat)
    spare = jnp.zeros((rows, 2 * feat - part), bf16)
    for j in range(count):
        pieces = [feature_ref[:, s * part + j * slot : s * part + (j + 1) * slot] for s in range(count)]
        joined = jnp.concatenate(pieces + [spare], axis=1)
        out_ref[j, slot : slot + rows] = joined[:, :feat]
        out_ref[j, slot + rows :] = joined[:, feat:]


def columns_kernel(where_ref, embed_ref, head_ref, shifts_ref, embed_out, head_out, shifts_out):
    count = 8
    part = embed_ref.shape[2] // count
    slot = part // count
    half = count // 2
    order = [0] + [count - d for d in range(1, half)] + list(range(1, half + 1))
    for f in range(count):

        @pl.when(where_ref[2] == f)
        def _(f=f):
            sources = [(embed_ref.at[0], embed_out), (head_ref.at[0], head_out)]
            sources += [(shifts_ref.at[i], shifts_out.at[i]) for i in range(shifts_ref.shape[0])]
            for source, target in sources:
                pieces = []
                for d in order:
                    owner = lax.rem(where_ref[1] + d, count)
                    block = source[:, pl.ds(pl.multiple_of(owner * part, 128), part)]
                    pieces.append(block[:, f * slot : (f + 1) * slot])
                target[...] = jnp.concatenate(pieces, axis=1)


def fold_keys(heads, carry, queries, keys, values):
    scores = [dot(keys(h), queries[h], ((1,), (0,))) for h in range(heads)]
    new = []
    for h in range(heads):
        top, total, weighted = carry[h]
        new_top = jnp.maximum(top, jnp.max(scores[h], axis=0, keepdims=True))
        weights = jnp.exp2(scores[h] - new_top)
        keep = jnp.exp2(top - new_top)
        total = total * keep + jnp.sum(weights, axis=0, keepdims=True)
        weighted = weighted * keep + dot(values(h), weights.astype(bf16), ((1,), (0,)))
        new.append((new_top, total, weighted))
    return tuple(new)


def attention_kernel(heads, latent_dim, where_ref, *refs):
    block_refs, (out_ref, all_ref, key_ref, value_ref, sems) = refs[:-5], refs[-5:]
    count, lines, _ = all_ref.shape
    rows = out_ref.shape[2]
    size = heads * rows
    at = [(n, 0, ref.shape[0]) for n, ref in enumerate(block_refs[:-1])]
    at.append((count - 1, block_refs[-2].shape[0], block_refs[-1].shape[0]))
    early, late = [], []
    for ref, (n, place, length) in zip(block_refs, at):
        for first, last, group in ((0, 2 * size, late), (2 * size, lines, early)):
            first, last = max(first, place), min(last, place + length)
            if first < last:
                group.append(
                    pltpu.make_async_copy(
                        ref.at[pl.ds(first - place, last - first)],
                        all_ref.at[n, pl.ds(first, last - first)],
                        sems.at[len(early) + len(late)],
                    )
                )
    for copy in early + late:
        copy.start()
    for copy in early:
        copy.wait()

    tables, base = [], 2 * size
    for i in range(3):
        at = slice(base + i * heads * latent_dim, base + (i + 1) * heads * latent_dim)
        total = sum(all_ref[n, at].astype(f32) for n in range(count)).astype(bf16)
        tables.append([total[h * latent_dim : (h + 1) * latent_dim] for h in range(heads)])
    tail = base + 3 * heads * latent_dim
    ends = tail + rows // 128 * latent_dim
    shift = sum(all_ref[n, ends:].astype(f32) for n in range(count))
    columns = jnp.concatenate([shift, jnp.zeros((112, 128), f32)], axis=0).T
    latents = jnp.concatenate(
        [
            all_ref[n, tail + i * latent_dim : tail + (i + 1) * latent_dim]
            for n in range(count)
            for i in range(rows // 128)
        ],
        axis=1,
    )
    scale = HEAD_DIM ** (-0.5) * LOG2E
    queries = [
        ((dot(tables[0][h], latents[:, :rows], ((0,), (0,))) + columns[:, h : h + 1]) * scale).astype(bf16)
        for h in range(heads)
    ]
    for h in range(heads):
        at = heads + h
        key_ref[h] = (dot(latents, tables[1][h], ((0,), (0,))) + shift[at : at + 1]).astype(bf16)
        at = 2 * heads + h
        value_ref[h] = (dot(tables[2][h], latents, ((0,), (0,))) + columns[:, at : at + 1]).astype(bf16)
    carry = tuple(
        (jnp.full((1, rows), -1e30, f32), jnp.zeros((1, rows), f32), jnp.zeros((HEAD_DIM, rows), f32))
        for _ in range(heads)
    )
    step = 4 * rows
    for i in range(count // 4):
        at = slice(i * step, (i + 1) * step)
        carry = fold_keys(heads, carry, queries, lambda h: key_ref[h, at], lambda h: value_ref[h, :, at])
    for copy in late:
        copy.wait()
    for i in range(count // 4):
        here = range(4 * i, 4 * i + 4)
        carry = fold_keys(
            heads,
            carry,
            queries,
            lambda h: jnp.concatenate([all_ref[n, h * rows : (h + 1) * rows] for n in here], axis=0),
            lambda h: jnp.concatenate(
                [
                    all_ref[n, size + h * rows + j : size + h * rows + j + 128]
                    for n in here
                    for j in range(0, rows, 128)
                ],
                axis=1,
            ),
        )
    for h in range(heads):
        _, total, weighted = carry[h]
        attended = (weighted / total).astype(bf16)
        out_ref[:, h * HEAD_DIM : (h + 1) * HEAD_DIM] = jnp.broadcast_to(
            attended[None], (out_ref.shape[0], HEAD_DIM, rows)
        )


def halves(value):
    high = value.astype(bf16).astype(f32)
    return high, value - high


def head_kernel(sections, where_ref, own_ref, embed_ref, shifts_ref, head_ref, att_ref, *refs):
    weight_refs, out_ref = refs[:-1], refs[-1]
    n_fsdp, _, rows = att_ref.shape
    latent_dim = embed_ref.shape[0]
    mixed = None
    for f in range(n_fsdp):
        whole = [ref[f] for ref in weight_refs[:-2]]
        whole.append(weight_refs[-2][f] if f < n_fsdp // 2 else weight_refs[-1][f - n_fsdp // 2])
        part = dot(jnp.concatenate(whole, axis=0), att_ref[f], ((1,), (0,)))
        mixed = part if mixed is None else mixed + part
    gate = jnp.broadcast_to(shifts_ref[2], (8, embed_ref.shape[1])).T[:, :1]
    residual = dot(embed_ref[...], own_ref[...], ((0,), (0,))) + gate * mixed
    centre = jnp.mean(residual, axis=0, keepdims=True)
    residual = residual - centre
    spread = jnp.sum(residual * residual, axis=0, keepdims=True)
    plain_head = head_ref[...].astype(f32)
    head = (plain_head * (1.0 + shifts_ref[4])).astype(bf16)
    values = dot(head, residual.astype(bf16), ((1,), (0,)))
    spare = jnp.zeros((latent_dim - 4, rows), f32)
    values = jnp.concatenate([values, *halves(centre), *halves(spread), spare], axis=0).T.astype(bf16)
    sums = jnp.sum(head.astype(f32), axis=1, keepdims=True)
    consts = jnp.sum(plain_head * shifts_ref[3], axis=1, keepdims=True)
    place = lax.broadcasted_iota(jnp.int32, (latent_dim, 128), 1)
    extra = jnp.zeros((latent_dim, 128), f32)
    for n, column in enumerate(halves(sums) + halves(consts)):
        extra = jnp.where(place == n, column, extra)
    extra = jnp.concatenate([extra, jnp.zeros_like(extra)], axis=0).T[:16].astype(bf16)
    piece = rows // n_fsdp
    for f in range(n_fsdp):
        for s in range(sections):
            out_ref[s * n_fsdp + f, :piece] = values[f * piece : (f + 1) * piece]
            out_ref[s * n_fsdp + f, piece:] = extra


def estimate_kernel(sections, width, where_ref, levels_ref, partial_ref, student_ref, noised_ref, group_ref, grad_ref, out_ref):
    piece, latent_dim = student_ref.shape
    count = partial_ref.shape[0] // sections
    estimates = []
    for p in range(sections):
        blocks = [partial_ref[p * count + i].astype(f32) for i in range(count)]

        def column(b, n):
            at = latent_dim + n
            return b[:piece, at : at + 1] + b[:piece, at + 1 : at + 2]

        def line(b, n):
            at = piece + n
            return b[at : at + 1, :latent_dim] + b[at + 1 : at + 2, :latent_dim]

        means = [column(b, 0) for b in blocks]
        mean = sum(means) / count
        linear, spread, shift = 0.0, 0.0, 0.0
        for b, m in zip(blocks, means):
            offset = m - mean
            linear += b[:piece, :latent_dim] + offset * line(b, 0)
            spread += column(b, 2) + (width // count) * (offset * offset)
            shift += line(b, 2)
        velocity = linear * lax.rsqrt(spread / width + 1e-06) + shift
        latent = (student_ref if p == 0 else noised_ref)[...].astype(f32)
        estimates.append(latent - levels_ref[0 if p == 0 else 1] * velocity)
    group_ref[...] = estimates[0]
    teacher = estimates[2] + guidance_scale * (estimates[1] - estimates[2])
    grad = estimates[3] - teacher
    grad_ref[...] = grad
    velocity_grad = -levels_ref[2] * grad
    padded = jnp.concatenate([velocity_grad, jnp.zeros_like(velocity_grad)], axis=1).astype(bf16)
    out_ref[...] = jnp.broadcast_to(padded[None], out_ref.shape)


def gradient_kernel(where_ref, grad_ref, feature_ref, out_ref):
    count, lines, pair = out_ref.shape
    rows = grad_ref.shape[1]
    slot = feature_ref.shape[1] - 2 * rows
    latent_dim, half = pair // 2, slot // 2
    grads = grad_ref[...].reshape(-1, grad_ref.shape[2])
    joined = jnp.concatenate(
        [
            dot(feature_ref[:, at : at + rows].reshape(count * rows, -1), grads, ((0,), (0,)))[:, :latent_dim]
            for at in (slot, slot + rows)
        ],
        axis=0,
    )
    spare = jnp.zeros((lines - half, pair), f32)
    for i in range(count):
        at = i * slot
        block = jnp.concatenate([joined[at : at + half], joined[at + half : at + slot]], axis=1)
        out_ref[i] = jnp.concatenate([block, spare], axis=0).astype(bf16)


def sum_kernel(where_ref, part_ref, out_ref):
    latent_dim, slot = out_ref.shape
    total = part_ref[0].astype(f32)
    for i in range(1, part_ref.shape[0]):
        total += part_ref[i].astype(f32)
    half = slot // 2
    out_ref[...] = jnp.concatenate([total[:half, :latent_dim], total[:half, latent_dim:]], axis=0).T


def per_device(
    student_input,
    previous_latent,
    score_noise,
    timesteps,
    modulation,
    in_weight,
    qkv_weight,
    out_weight,
    head_weight,
    kv_cache,
    saved_features,
):
    section, me_seq, me_fsdp = (lax.axis_index(a) for a in ("section", "seq", "fsdp"))
    sections, n_seq, n_fsdp = (lax.axis_size(a) for a in ("section", "seq", "fsdp"))
    model_index = section - (section >= 2).astype(jnp.int32)
    where = jnp.concatenate([jnp.stack([model_index, me_seq, me_fsdp, section]).astype(jnp.int32), timesteps])
    levels = noise_levels(timesteps)
    rows, latent_dim = student_input.shape
    width = in_weight.shape[2]
    depth, feat = qkv_weight.shape[1], qkv_weight.shape[3]
    heads = feat // HEAD_DIM
    piece = rows // n_fsdp
    shifts = modulation.transpose(1, 0, 2)
    slot = depth // n_fsdp

    lines = (2 * rows + 3 * latent_dim) * heads + rows // 128 * latent_dim + 16
    own, plain = run(
        prepare_kernel,
        where,
        [((lines, HEAD_DIM), bf16), ((latent_dim, rows), bf16)],
        in_weight,
        qkv_weight.transpose(0, 2, 1, 3),
        shifts,
        student_input.T,
        previous_latent.T,
        score_noise.T,
        kv_cache[0].transpose(1, 0, 2).reshape(2 * rows, feat),
        raw=range(7),
        scratch=[
            pltpu.VMEM((1, latent_dim, width), bf16),
            pltpu.VMEM((1, 3, depth, feat), bf16),
            pltpu.VMEM(shifts.shape, f32),
            pltpu.VMEM((latent_dim, rows), bf16),
            pltpu.VMEM((latent_dim, rows), bf16),
            pltpu.VMEM((latent_dim, rows), bf16),
            pltpu.VMEM((2 * rows, feat), bf16),
            pltpu.SemaphoreType.DMA((7,)),
        ],
        room=60,
    )
    cut = run(aside_kernel, together(where, own), [((n_fsdp, slot + 2 * piece, feat), bf16)], out_weight, saved_features, picked=(0,))
    aside = exchange(cut, "fsdp")
    embed_here, head_here, shifts_here = run(
        columns_kernel,
        together(where, own),
        [((latent_dim, depth), bf16), ((latent_dim, depth), bf16), ((shifts.shape[0], 1, depth), f32)],
        in_weight,
        head_weight.transpose(0, 2, 1),
        shifts,
        picked=(0, 1),
    )
    around = Ring(own, "seq", n_seq, 0, lines // 32 * 16)
    around.step()
    block, *_ = lax.optimization_barrier((aside[:, :slot],) + around.ends())
    weights = Ring(block, "seq", n_seq, 0)
    weights.step()
    around.step()
    around.step()
    weights.after(around)
    around.finish()
    weights.step()
    blocks = around.blocks()
    attended = run(
        functools.partial(attention_kernel, heads, latent_dim),
        together(where, embed_here),
        [((n_fsdp, feat, rows), bf16)],
        *blocks,
        scratch=[
            pltpu.VMEM((n_seq, lines, HEAD_DIM), bf16),
            pltpu.VMEM((heads, n_seq * rows, HEAD_DIM), bf16),
            pltpu.VMEM((heads, HEAD_DIM, n_seq * rows), bf16),
            pltpu.SemaphoreType.DMA((2 * len(blocks),)),
        ],
        raw=range(len(blocks)),
        cost=pl.CostEstimate(flops=11 * 10**9, bytes_accessed=20 * 10**6, transcendentals=3 * 10**6),
    )
    attended = exchange(together(attended, *weights.ends()), "fsdp")
    weights.finish()
    partials = run(
        functools.partial(head_kernel, sections),
        where,
        [((sections * n_fsdp, piece + 16, 128), bf16)],
        plain,
        embed_here,
        shifts_here,
        head_here,
        attended,
        *weights.blocks(),
    )
    partials = exchange(partials, ("section", "fsdp"))

    noised = (
        (1.0 - levels[1]) * previous_latent.astype(f32) + levels[1] * score_noise.astype(f32)
    ).astype(bf16)
    own_student = lax.dynamic_slice_in_dim(student_input, me_fsdp * piece, piece, 0)
    own_noised = lax.dynamic_slice_in_dim(noised, me_fsdp * piece, piece, 0)
    student_group, dmd_grad, grads = run(
        functools.partial(estimate_kernel, sections, width),
        where,
        [((piece, latent_dim), f32), ((piece, latent_dim), f32), ((n_fsdp, piece, 2 * latent_dim), bf16)],
        levels,
        partials,
        own_student,
        own_noised,
    )
    grads = exchange(grads, "fsdp")
    partial_grad = run(
        gradient_kernel, where, [((n_seq, (slot // 2 + 15) // 16 * 16, 2 * latent_dim), bf16)], grads, aside
    )
    head_grad = run(sum_kernel, where, [((latent_dim, slot), f32)], exchange(partial_grad, "seq")).T
    return (student_group, dmd_grad, head_grad)


def solution(mesh):
    placed = (
        P("seq", None),
        P("seq", None),
        P("seq", None),
        P(),
        P("section", None, None),
        P(),
        P(None, "seq", None, "fsdp"),
        P(None, "seq", "fsdp"),
        P(),
        P("section", "seq", None, "fsdp"),
        P(("seq", "fsdp"), None),
    )
    return jax.shard_map(
        per_device,
        mesh=mesh,
        in_specs=placed,
        out_specs=(P(("seq", "fsdp"), None), P(("seq", "fsdp"), None), P(("seq", "fsdp"), None)),
        check_vma=False,
    )
```

```python
import functools

import jax
import jax.numpy as jnp
from jax import lax
from jax.experimental import pallas as pl
from jax.experimental.pallas import tpu as pltpu
from jax.sharding import PartitionSpec as P

HEAD_DIM = 128
LOG2E = 1.4426950408889634
guidance_scale = 5.0
bf16 = jnp.bfloat16
f32 = jnp.float32


def run(kernel, where, outs, *operands, picked=(), scratch=(), raw=(), inside=(), held=False, cost=None, room=52):
    def spec(shape, pick=False):
        zeros = (0,) * (len(shape) - 1)
        if pick:
            return pl.BlockSpec((1,) + tuple(shape[1:]), lambda i, w: (w[0],) + zeros)
        return pl.BlockSpec(tuple(shape), lambda i, w: (0,) + zeros)

    in_specs = [
        pl.BlockSpec(memory_space=pltpu.SMEM)
        if x.ndim == 1
        else pl.BlockSpec(memory_space=pltpu.VMEM)
        if n in inside
        else pl.BlockSpec(memory_space=pltpu.HBM)
        if n in raw
        else spec(x.shape, n in picked)
        for n, x in enumerate(operands)
    ]
    result = pl.pallas_call(
        kernel,
        grid_spec=pltpu.PrefetchScalarGridSpec(
            num_scalar_prefetch=1,
            grid=(1,),
            in_specs=in_specs,
            out_specs=tuple(pl.BlockSpec(memory_space=pltpu.VMEM) if held else spec(shape) for shape, _ in outs),
            scratch_shapes=list(scratch),
        ),
        out_shape=tuple(jax.ShapeDtypeStruct(shape, dtype) for shape, dtype in outs),
        compiler_params=pltpu.CompilerParams(vmem_limit_bytes=room * 1024 * 1024),
        cost_estimate=cost,
    )(where, *operands)
    return result[0] if len(outs) == 1 else result


def together(value, *others):
    return lax.optimization_barrier((value,) + others)[0]


def noise_levels(steps):
    remain = 1.0 - steps.astype(f32) / 1000.0
    return 5.0 * remain / (1.0 + 4.0 * remain)


def exchange(blocks, axis):
    return lax.all_to_all(blocks, axis, 0, 0, tiled=True)


class Ring:
    def __init__(self, block, axis, count, split, split_at=None):
        self.split_at = split_at
        self.axis, self.split, self.half = axis, split, count // 2
        self.up = [(i, (i + 1) % count) for i in range(count)]
        self.down = [(i, (i - 1) % count) for i in range(count)]
        self.behind, self.ahead, self.last = [block], [block], []

    def step(self):
        self.behind.append(lax.ppermute(self.behind[-1], self.axis, self.up))
        self.ahead.append(lax.ppermute(self.ahead[-1], self.axis, self.down))

    def ends(self):
        return self.behind[-1], self.ahead[-1]

    def after(self, other):
        self.behind[-1], self.ahead[-1], *_ = lax.optimization_barrier(self.ends() + other.ends())

    def finish(self):
        while len(self.behind) < self.half:
            self.step()
        total = self.behind[0].shape[self.split]
        size = total // 2 if self.split_at is None else self.split_at
        first = lax.slice_in_dim(self.behind[-1], 0, size, axis=self.split)
        second = lax.slice_in_dim(self.ahead[-1], size, total, axis=self.split)
        self.last = [lax.ppermute(first, self.axis, self.up), lax.ppermute(second, self.axis, self.down)]

    def blocks(self):
        return self.behind + self.ahead[1:] + self.last


def dot(a, b, over):
    return lax.dot_general(a, b, ((over[0], over[1]), ((), ())), preferred_element_type=f32)


def prepare_kernel(
    steps_ref, embed_hbm, weight_hbm, shifts_hbm, student_hbm, previous_hbm, noise_hbm, context_hbm, *refs
):
    out_ref, plain_ref, embed_ref, weight_ref, shifts_ref, student_ref, previous_ref, noise_ref, context_ref, sems = refs
    latent_dim, width = embed_ref.shape[1:]
    parts, depth, feat = weight_ref.shape[1:]
    rows = student_ref.shape[1]
    section, me_seq = lax.axis_index("section"), lax.axis_index("seq")
    model = pl.ds(jnp.where(section >= 2, section - 1, section), 1)
    sources = (embed_hbm.at[model], shifts_hbm, student_hbm, previous_hbm, noise_hbm, weight_hbm.at[model], context_hbm)
    targets = (embed_ref, shifts_ref, student_ref, previous_ref, noise_ref, weight_ref, context_ref)
    copies = [pltpu.make_async_copy(a, b, sems.at[n]) for n, (a, b) in enumerate(zip(sources, targets))]
    for copy in copies:
        copy.start()
    for copy in copies[:5]:
        copy.wait()
    level = noise_levels(jnp.full((1, rows), steps_ref[1], jnp.int32))
    noised = (1.0 - level) * previous_ref[...].astype(f32) + level * noise_ref[...].astype(f32)
    latents = jnp.where(section == 0, student_ref[...].astype(f32), noised.astype(bf16).astype(f32))

    step = 1024
    row_sum = jnp.zeros((latent_dim, 1), f32)
    for first in range(0, width, step):
        row_sum += jnp.sum(embed_ref[0, :, first : first + step].astype(f32), axis=1, keepdims=True)
    row_mean = row_sum / width

    mean = jnp.sum(row_mean * latents, axis=0, keepdims=True)
    plain = latents.astype(bf16)
    spread = jnp.zeros((1, rows), f32)
    for first in range(0, width, step):
        hidden = dot(embed_ref[0, :, first : first + step], plain, ((0,), (0,))) - mean
        spread += jnp.sum(hidden * hidden, axis=0, keepdims=True)
    inverse = lax.rsqrt(spread / width + 1e-06)
    heads = feat // HEAD_DIM
    scaled = (latents * inverse).astype(bf16)
    tail = (2 * rows + parts * latent_dim) * heads
    for n in range(rows // 128):
        out_ref[tail + n * latent_dim : tail + (n + 1) * latent_dim] = scaled[:, n * 128 : (n + 1) * 128]
    plain_ref[...] = plain
    for copy in copies[5:]:
        copy.wait()
    here = pl.ds(pl.multiple_of(me_seq * depth, 128), depth)
    centred = (embed_ref[0, :, here].astype(f32) - row_mean) * (1.0 + shifts_ref[1, :, here])
    shift = jnp.broadcast_to(shifts_ref[0, :, here], (16, depth))
    folded = jnp.concatenate([centred, shift], axis=0).astype(bf16)
    lines = []
    for i in range(parts):
        table = dot(folded, weight_ref[0, i], ((1,), (0,)))
        for h in range(heads):
            at = 2 * rows * heads + (i * heads + h) * latent_dim
            out_ref[at : at + latent_dim] = table[:latent_dim, h * 128 : (h + 1) * 128].astype(bf16)
        lines += [table[latent_dim : latent_dim + 1, n : n + 128] for n in range(0, feat, 128)]
    spare = jnp.zeros((16 - len(lines), 128), f32)
    out_ref[tail + rows // 128 * latent_dim :] = jnp.concatenate(lines + [spare], axis=0).astype(bf16)
    for h in range(heads):
        cols = slice(h * 128, (h + 1) * 128)
        out_ref[h * rows : (h + 1) * rows] = context_ref[:, 0, cols]
        values = context_ref[:, 1, cols].astype(f32).T.astype(bf16)
        for n in range(rows // 128):
            at = heads * rows + h * rows + n * 128
            out_ref[at : at + 128] = values[:, n * 128 : (n + 1) * 128]


def aside_kernel(where_ref, weight_ref, feature_ref, out_ref):
    count, lines, feat = out_ref.shape
    rows, width = feature_ref.shape
    slot = weight_ref.shape[1] // count
    part = width // count
    out_ref[:, :slot] = weight_ref[0].reshape(count, slot, feat)
    spare = jnp.zeros((rows, 2 * feat - part), bf16)
    for j in range(count):
        pieces = [feature_ref[:, s * part + j * slot : s * part + (j + 1) * slot] for s in range(count)]
        joined = jnp.concatenate(pieces + [spare], axis=1)
        out_ref[j, slot : slot + rows] = joined[:, :feat]
        out_ref[j, slot + rows :] = joined[:, feat:]


def columns_kernel(where_ref, embed_ref, head_ref, shifts_ref, embed_out, head_out, shifts_out):
    count = 8
    part = embed_ref.shape[2] // count
    slot = part // count
    half = count // 2
    order = [0] + [count - d for d in range(1, half)] + list(range(1, half + 1))
    for f in range(count):

        @pl.when(where_ref[2] == f)
        def _(f=f):
            sources = [(embed_ref.at[0], embed_out), (head_ref.at[0], head_out)]
            sources += [(shifts_ref.at[i], shifts_out.at[i]) for i in range(shifts_ref.shape[0])]
            for source, target in sources:
                pieces = []
                for d in order:
                    owner = lax.rem(where_ref[1] + d, count)
                    block = source[:, pl.ds(pl.multiple_of(owner * part, 128), part)]
                    pieces.append(block[:, f * slot : (f + 1) * slot])
                target[...] = jnp.concatenate(pieces, axis=1)


def fold_keys(heads, carry, queries, keys, values):
    scores = [dot(keys(h), queries[h], ((1,), (0,))) for h in range(heads)]
    new = []
    for h in range(heads):
        top, total, weighted = carry[h]
        new_top = jnp.maximum(top, jnp.max(scores[h], axis=0, keepdims=True))
        weights = jnp.exp2(scores[h] - new_top)
        keep = jnp.exp2(top - new_top)
        total = total * keep + jnp.sum(weights, axis=0, keepdims=True)
        weighted = weighted * keep + dot(values(h), weights.astype(bf16), ((1,), (0,)))
        new.append((new_top, total, weighted))
    return tuple(new)


def attention_kernel(heads, latent_dim, where_ref, *refs):
    block_refs, (out_ref, all_ref, key_ref, value_ref, sems) = refs[:-5], refs[-5:]
    count, lines, _ = all_ref.shape
    rows = out_ref.shape[2]
    size = heads * rows
    at = [(n, 0, ref.shape[0]) for n, ref in enumerate(block_refs[:-1])]
    at.append((count - 1, block_refs[-2].shape[0], block_refs[-1].shape[0]))
    early, late = [], []
    for ref, (n, place, length) in zip(block_refs, at):
        for first, last, group in ((0, 2 * size, late), (2 * size, lines, early)):
            first, last = max(first, place), min(last, place + length)
            if first < last:
                group.append(
                    pltpu.make_async_copy(
                        ref.at[pl.ds(first - place, last - first)],
                        all_ref.at[n, pl.ds(first, last - first)],
                        sems.at[len(early) + len(late)],
                    )
                )
    for copy in early + late:
        copy.start()
    for copy in early:
        copy.wait()

    tables, base = [], 2 * size
    for i in range(3):
        at = slice(base + i * heads * latent_dim, base + (i + 1) * heads * latent_dim)
        total = sum(all_ref[n, at].astype(f32) for n in range(count)).astype(bf16)
        tables.append([total[h * latent_dim : (h + 1) * latent_dim] for h in range(heads)])
    tail = base + 3 * heads * latent_dim
    ends = tail + rows // 128 * latent_dim
    shift = sum(all_ref[n, ends:].astype(f32) for n in range(count))
    columns = jnp.concatenate([shift, jnp.zeros((112, 128), f32)], axis=0).T
    latents = jnp.concatenate(
        [
            all_ref[n, tail + i * latent_dim : tail + (i + 1) * latent_dim]
            for n in range(count)
            for i in range(rows // 128)
        ],
        axis=1,
    )
    scale = HEAD_DIM ** (-0.5) * LOG2E
    queries = [
        ((dot(tables[0][h], latents[:, :rows], ((0,), (0,))) + columns[:, h : h + 1]) * scale).astype(bf16)
        for h in range(heads)
    ]
    for h in range(heads):
        at = heads + h
        key_ref[h] = (dot(latents, tables[1][h], ((0,), (0,))) + shift[at : at + 1]).astype(bf16)
        at = 2 * heads + h
        value_ref[h] = (dot(tables[2][h], latents, ((0,), (0,))) + columns[:, at : at + 1]).astype(bf16)
    carry = tuple(
        (jnp.full((1, rows), -1e30, f32), jnp.zeros((1, rows), f32), jnp.zeros((HEAD_DIM, rows), f32))
        for _ in range(heads)
    )
    step = 4 * rows
    for i in range(count // 4):
        at = slice(i * step, (i + 1) * step)
        carry = fold_keys(heads, carry, queries, lambda h: key_ref[h, at], lambda h: value_ref[h, :, at])
    for copy in late:
        copy.wait()
    for i in range(count // 4):
        here = range(4 * i, 4 * i + 4)
        carry = fold_keys(
            heads,
            carry,
            queries,
            lambda h: jnp.concatenate([all_ref[n, h * rows : (h + 1) * rows] for n in here], axis=0),
            lambda h: jnp.concatenate(
                [
                    all_ref[n, size + h * rows + j : size + h * rows + j + 128]
                    for n in here
                    for j in range(0, rows, 128)
                ],
                axis=1,
            ),
        )
    for h in range(heads):
        _, total, weighted = carry[h]
        attended = (weighted / total).astype(bf16)
        out_ref[:, h * HEAD_DIM : (h + 1) * HEAD_DIM] = jnp.broadcast_to(
            attended[None], (out_ref.shape[0], HEAD_DIM, rows)
        )


def halves(value):
    high = value.astype(bf16).astype(f32)
    return high, value - high


def head_kernel(sections, where_ref, own_ref, embed_ref, shifts_ref, head_ref, att_ref, *refs):
    weight_refs, out_ref = refs[:-1], refs[-1]
    n_fsdp, _, rows = att_ref.shape
    latent_dim = embed_ref.shape[0]
    mixed = None
    for f in range(n_fsdp):
        whole = [ref[f] for ref in weight_refs[:-2]]
        whole.append(weight_refs[-2][f] if f < n_fsdp // 2 else weight_refs[-1][f - n_fsdp // 2])
        part = dot(jnp.concatenate(whole, axis=0), att_ref[f], ((1,), (0,)))
        mixed = part if mixed is None else mixed + part
    gate = jnp.broadcast_to(shifts_ref[2], (8, embed_ref.shape[1])).T[:, :1]
    residual = dot(embed_ref[...], own_ref[...], ((0,), (0,))) + gate * mixed
    centre = jnp.mean(residual, axis=0, keepdims=True)
    residual = residual - centre
    spread = jnp.sum(residual * residual, axis=0, keepdims=True)
    plain_head = head_ref[...].astype(f32)
    head = (plain_head * (1.0 + shifts_ref[4])).astype(bf16)
    values = dot(head, residual.astype(bf16), ((1,), (0,)))
    spare = jnp.zeros((latent_dim - 4, rows), f32)
    values = jnp.concatenate([values, *halves(centre), *halves(spread), spare], axis=0).T.astype(bf16)
    sums = jnp.sum(head.astype(f32), axis=1, keepdims=True)
    consts = jnp.sum(plain_head * shifts_ref[3], axis=1, keepdims=True)
    place = lax.broadcasted_iota(jnp.int32, (latent_dim, 128), 1)
    extra = jnp.zeros((latent_dim, 128), f32)
    for n, column in enumerate(halves(sums) + halves(consts)):
        extra = jnp.where(place == n, column, extra)
    extra = jnp.concatenate([extra, jnp.zeros_like(extra)], axis=0).T[:16].astype(bf16)
    piece = rows // n_fsdp
    for f in range(n_fsdp):
        for s in range(sections):
            out_ref[s * n_fsdp + f, :piece] = values[f * piece : (f + 1) * piece]
            out_ref[s * n_fsdp + f, piece:] = extra


def estimate_kernel(sections, width, where_ref, levels_ref, partial_ref, student_ref, noised_ref, group_ref, grad_ref, out_ref):
    piece, latent_dim = student_ref.shape
    count = partial_ref.shape[0] // sections
    estimates = []
    for p in range(sections):
        blocks = [partial_ref[p * count + i].astype(f32) for i in range(count)]

        def column(b, n):
            at = latent_dim + n
            return b[:piece, at : at + 1] + b[:piece, at + 1 : at + 2]

        def line(b, n):
            at = piece + n
            return b[at : at + 1, :latent_dim] + b[at + 1 : at + 2, :latent_dim]

        means = [column(b, 0) for b in blocks]
        mean = sum(means) / count
        linear, spread, shift = 0.0, 0.0, 0.0
        for b, m in zip(blocks, means):
            offset = m - mean
            linear += b[:piece, :latent_dim] + offset * line(b, 0)
            spread += column(b, 2) + (width // count) * (offset * offset)
            shift += line(b, 2)
        velocity = linear * lax.rsqrt(spread / width + 1e-06) + shift
        latent = (student_ref if p == 0 else noised_ref)[...].astype(f32)
        estimates.append(latent - levels_ref[0 if p == 0 else 1] * velocity)
    group_ref[...] = estimates[0]
    teacher = estimates[2] + guidance_scale * (estimates[1] - estimates[2])
    grad = estimates[3] - teacher
    grad_ref[...] = grad
    velocity_grad = -levels_ref[2] * grad
    padded = jnp.concatenate([velocity_grad, jnp.zeros_like(velocity_grad)], axis=1).astype(bf16)
    out_ref[...] = jnp.broadcast_to(padded[None], out_ref.shape)


def gradient_kernel(where_ref, grad_ref, feature_ref, out_ref):
    count, lines, pair = out_ref.shape
    rows = grad_ref.shape[1]
    slot = feature_ref.shape[1] - 2 * rows
    latent_dim, half = pair // 2, slot // 2
    grads = grad_ref[...].reshape(-1, grad_ref.shape[2])
    joined = jnp.concatenate(
        [
            dot(feature_ref[:, at : at + rows].reshape(count * rows, -1), grads, ((0,), (0,)))[:, :latent_dim]
            for at in (slot, slot + rows)
        ],
        axis=0,
    )
    spare = jnp.zeros((lines - half, pair), f32)
    for i in range(count):
        at = i * slot
        block = jnp.concatenate([joined[at : at + half], joined[at + half : at + slot]], axis=1)
        out_ref[i] = jnp.concatenate([block, spare], axis=0).astype(bf16)


def sum_kernel(where_ref, part_ref, out_ref):
    latent_dim, slot = out_ref.shape
    total = part_ref[0].astype(f32)
    for i in range(1, part_ref.shape[0]):
        total += part_ref[i].astype(f32)
    half = slot // 2
    out_ref[...] = jnp.concatenate([total[:half, :latent_dim], total[:half, latent_dim:]], axis=0).T


def per_device(
    student_input,
    previous_latent,
    score_noise,
    timesteps,
    modulation,
    in_weight,
    qkv_weight,
    out_weight,
    head_weight,
    kv_cache,
    saved_features,
):
    section, me_seq, me_fsdp = (lax.axis_index(a) for a in ("section", "seq", "fsdp"))
    sections, n_seq, n_fsdp = (lax.axis_size(a) for a in ("section", "seq", "fsdp"))
    model_index = section - (section >= 2).astype(jnp.int32)
    where = jnp.concatenate([jnp.stack([model_index, me_seq, me_fsdp, section]).astype(jnp.int32), timesteps])
    levels = noise_levels(timesteps)
    rows, latent_dim = student_input.shape
    width = in_weight.shape[2]
    depth, feat = qkv_weight.shape[1], qkv_weight.shape[3]
    heads = feat // HEAD_DIM
    piece = rows // n_fsdp
    shifts = modulation.transpose(1, 0, 2)
    slot = depth // n_fsdp

    lines = (2 * rows + 3 * latent_dim) * heads + rows // 128 * latent_dim + 16
    own, plain = run(
        prepare_kernel,
        timesteps,
        [((lines, HEAD_DIM), bf16), ((latent_dim, rows), bf16)],
        in_weight,
        qkv_weight.transpose(0, 2, 1, 3),
        shifts,
        student_input.T,
        previous_latent.T,
        score_noise.T,
        kv_cache[0],
        raw=range(7),
        scratch=[
            pltpu.VMEM((1, latent_dim, width), bf16),
            pltpu.VMEM((1, 3, depth, feat), bf16),
            pltpu.VMEM(shifts.shape, f32),
            pltpu.VMEM((latent_dim, rows), bf16),
            pltpu.VMEM((latent_dim, rows), bf16),
            pltpu.VMEM((latent_dim, rows), bf16),
            pltpu.VMEM((rows, 2, feat), bf16),
            pltpu.SemaphoreType.DMA((7,)),
        ],
        room=60,
    )
    cut = run(aside_kernel, together(where, own), [((n_fsdp, slot + 2 * piece, feat), bf16)], out_weight, saved_features, picked=(0,))
    aside = exchange(cut, "fsdp")
    embed_here, head_here, shifts_here = run(
        columns_kernel,
        together(where, own),
        [((latent_dim, depth), bf16), ((latent_dim, depth), bf16), ((shifts.shape[0], 1, depth), f32)],
        in_weight,
        head_weight.transpose(0, 2, 1),
        shifts,
        picked=(0, 1),
    )
    around = Ring(own, "seq", n_seq, 0, lines // 32 * 16)
    around.step()
    block, *_ = lax.optimization_barrier((aside[:, :slot],) + around.ends())
    weights = Ring(block, "seq", n_seq, 0)
    weights.step()
    around.step()
    around.step()
    weights.after(around)
    around.finish()
    weights.step()
    blocks = around.blocks()
    attended = run(
        functools.partial(attention_kernel, heads, latent_dim),
        together(where, embed_here),
        [((n_fsdp, feat, rows), bf16)],
        *blocks,
        scratch=[
            pltpu.VMEM((n_seq, lines, HEAD_DIM), bf16),
            pltpu.VMEM((heads, n_seq * rows, HEAD_DIM), bf16),
            pltpu.VMEM((heads, HEAD_DIM, n_seq * rows), bf16),
            pltpu.SemaphoreType.DMA((2 * len(blocks),)),
        ],
        raw=range(len(blocks)),
        cost=pl.CostEstimate(flops=11 * 10**9, bytes_accessed=20 * 10**6, transcendentals=3 * 10**6),
    )
    attended = exchange(together(attended, *weights.ends()), "fsdp")
    weights.finish()
    partials = run(
        functools.partial(head_kernel, sections),
        where,
        [((sections * n_fsdp, piece + 16, 128), bf16)],
        plain,
        embed_here,
        shifts_here,
        head_here,
        attended,
        *weights.blocks(),
    )
    partials = exchange(partials, ("section", "fsdp"))

    noised = (
        (1.0 - levels[1]) * previous_latent.astype(f32) + levels[1] * score_noise.astype(f32)
    ).astype(bf16)
    own_student = lax.dynamic_slice_in_dim(student_input, me_fsdp * piece, piece, 0)
    own_noised = lax.dynamic_slice_in_dim(noised, me_fsdp * piece, piece, 0)
    student_group, dmd_grad, grads = run(
        functools.partial(estimate_kernel, sections, width),
        where,
        [((piece, latent_dim), f32), ((piece, latent_dim), f32), ((n_fsdp, piece, 2 * latent_dim), bf16)],
        levels,
        partials,
        own_student,
        own_noised,
    )
    grads = exchange(grads, "fsdp")
    partial_grad = run(
        gradient_kernel, where, [((n_seq, (slot // 2 + 15) // 16 * 16, 2 * latent_dim), bf16)], grads, aside
    )
    head_grad = run(sum_kernel, where, [((latent_dim, slot), f32)], exchange(partial_grad, "seq")).T
    return (student_group, dmd_grad, head_grad)


def solution(mesh):
    placed = (
        P("seq", None),
        P("seq", None),
        P("seq", None),
        P(),
        P("section", None, None),
        P(),
        P(None, "seq", None, "fsdp"),
        P(None, "seq", "fsdp"),
        P(),
        P("section", "seq", None, "fsdp"),
        P(("seq", "fsdp"), None),
    )
    return jax.shard_map(
        per_device,
        mesh=mesh,
        in_specs=placed,
        out_specs=(P(("seq", "fsdp"), None), P(("seq", "fsdp"), None), P(("seq", "fsdp"), None)),
        check_vma=False,
    )
```

```python
import functools

import jax
import jax.numpy as jnp
from jax import lax
from jax.experimental import pallas as pl
from jax.experimental.pallas import tpu as pltpu
from jax.sharding import PartitionSpec as P

HEAD_DIM = 128
LOG2E = 1.4426950408889634
guidance_scale = 5.0
bf16 = jnp.bfloat16
f32 = jnp.float32


def run(kernel, where, outs, *operands, picked=(), scratch=(), raw=(), inside=(), held=False, cost=None, room=52):
    def spec(shape, pick=False):
        zeros = (0,) * (len(shape) - 1)
        if pick:
            return pl.BlockSpec((1,) + tuple(shape[1:]), lambda i, w: (w[0],) + zeros)
        return pl.BlockSpec(tuple(shape), lambda i, w: (0,) + zeros)

    in_specs = [
        pl.BlockSpec(memory_space=pltpu.SMEM)
        if x.ndim == 1
        else pl.BlockSpec(memory_space=pltpu.VMEM)
        if n in inside
        else pl.BlockSpec(memory_space=pltpu.HBM)
        if n in raw
        else spec(x.shape, n in picked)
        for n, x in enumerate(operands)
    ]
    result = pl.pallas_call(
        kernel,
        grid_spec=pltpu.PrefetchScalarGridSpec(
            num_scalar_prefetch=1,
            grid=(1,),
            in_specs=in_specs,
            out_specs=tuple(pl.BlockSpec(memory_space=pltpu.VMEM) if held else spec(shape) for shape, _ in outs),
            scratch_shapes=list(scratch),
        ),
        out_shape=tuple(jax.ShapeDtypeStruct(shape, dtype) for shape, dtype in outs),
        compiler_params=pltpu.CompilerParams(vmem_limit_bytes=room * 1024 * 1024),
        cost_estimate=cost,
    )(where, *operands)
    return result[0] if len(outs) == 1 else result


def together(value, *others):
    return lax.optimization_barrier((value,) + others)[0]


def noise_levels(steps):
    remain = 1.0 - steps.astype(f32) / 1000.0
    return 5.0 * remain / (1.0 + 4.0 * remain)


def exchange(blocks, axis):
    return lax.all_to_all(blocks, axis, 0, 0, tiled=True)


class Ring:
    def __init__(self, block, axis, count, split, split_at=None):
        self.split_at = split_at
        self.axis, self.split, self.half = axis, split, count // 2
        self.up = [(i, (i + 1) % count) for i in range(count)]
        self.down = [(i, (i - 1) % count) for i in range(count)]
        self.behind, self.ahead, self.last = [block], [block], []

    def step(self):
        self.behind.append(lax.ppermute(self.behind[-1], self.axis, self.up))
        self.ahead.append(lax.ppermute(self.ahead[-1], self.axis, self.down))

    def ends(self):
        return self.behind[-1], self.ahead[-1]

    def after(self, other):
        self.behind[-1], self.ahead[-1], *_ = lax.optimization_barrier(self.ends() + other.ends())

    def finish(self):
        while len(self.behind) < self.half:
            self.step()
        total = self.behind[0].shape[self.split]
        size = total // 2 if self.split_at is None else self.split_at
        first = lax.slice_in_dim(self.behind[-1], 0, size, axis=self.split)
        second = lax.slice_in_dim(self.ahead[-1], size, total, axis=self.split)
        self.last = [lax.ppermute(first, self.axis, self.up), lax.ppermute(second, self.axis, self.down)]

    def blocks(self):
        return self.behind + self.ahead[1:] + self.last


def dot(a, b, over):
    return lax.dot_general(a, b, ((over[0], over[1]), ((), ())), preferred_element_type=f32)


def prepare_kernel(
    steps_ref, embed_hbm, weight_hbm, shifts_hbm, student_hbm, previous_hbm, noise_hbm, context_hbm, *refs
):
    out_ref, plain_ref, embed_ref, weight_ref, shifts_ref, student_ref, previous_ref, noise_ref, context_ref, sems = refs
    latent_dim, width = embed_ref.shape[1:]
    parts, depth, feat = weight_ref.shape[1:]
    rows = student_ref.shape[1]
    section, me_seq = lax.axis_index("section"), lax.axis_index("seq")
    model = pl.ds(jnp.where(section >= 2, section - 1, section), 1)
    sources = (embed_hbm.at[model], shifts_hbm, student_hbm, previous_hbm, noise_hbm, weight_hbm.at[model], context_hbm)
    targets = (embed_ref, shifts_ref, student_ref, previous_ref, noise_ref, weight_ref, context_ref)
    copies = [pltpu.make_async_copy(a, b, sems.at[n]) for n, (a, b) in enumerate(zip(sources, targets))]
    for copy in copies:
        copy.start()
    for copy in copies[:5]:
        copy.wait()
    level = noise_levels(jnp.full((1, rows), steps_ref[1], jnp.int32))
    noised = (1.0 - level) * previous_ref[...].astype(f32) + level * noise_ref[...].astype(f32)
    latents = jnp.where(section == 0, student_ref[...].astype(f32), noised.astype(bf16).astype(f32))

    step = 1024
    row_sum = jnp.zeros((latent_dim, 1), f32)
    for first in range(0, width, step):
        row_sum += jnp.sum(embed_ref[0, :, first : first + step].astype(f32), axis=1, keepdims=True)
    row_mean = row_sum / width

    mean = jnp.sum(row_mean * latents, axis=0, keepdims=True)
    plain = latents.astype(bf16)
    spread = jnp.zeros((1, rows), f32)
    for first in range(0, width, step):
        hidden = dot(embed_ref[0, :, first : first + step], plain, ((0,), (0,))) - mean
        spread += jnp.sum(hidden * hidden, axis=0, keepdims=True)
    inverse = lax.rsqrt(spread / width + 1e-06)
    heads = feat // HEAD_DIM
    scaled = (latents * inverse).astype(bf16)
    tail = (2 * rows + parts * latent_dim) * heads
    for n in range(rows // 128):
        out_ref[tail + n * latent_dim : tail + (n + 1) * latent_dim] = scaled[:, n * 128 : (n + 1) * 128]
    plain_ref[...] = plain
    for copy in copies[5:]:
        copy.wait()
    here = pl.ds(pl.multiple_of(me_seq * depth, 128), depth)
    centred = (embed_ref[0, :, here].astype(f32) - row_mean) * (1.0 + shifts_ref[1, :, here])
    shift = jnp.broadcast_to(shifts_ref[0, :, here], (16, depth))
    folded = jnp.concatenate([centred, shift], axis=0).astype(bf16)
    lines = []
    for i in range(parts):
        table = dot(folded, weight_ref[0, i], ((1,), (0,)))
        for h in range(heads):
            at = 2 * rows * heads + (i * heads + h) * latent_dim
            out_ref[at : at + latent_dim] = table[:latent_dim, h * 128 : (h + 1) * 128].astype(bf16)
        lines += [table[latent_dim : latent_dim + 1, n : n + 128] for n in range(0, feat, 128)]
    spare = jnp.zeros((16 - len(lines), 128), f32)
    out_ref[tail + rows // 128 * latent_dim :] = jnp.concatenate(lines + [spare], axis=0).astype(bf16)
    for h in range(heads):
        cols = slice(h * 128, (h + 1) * 128)
        out_ref[h * rows : (h + 1) * rows] = context_ref[:, 0, cols]
        values = context_ref[:, 1, cols].astype(f32).T.astype(bf16)
        for n in range(rows // 128):
            at = heads * rows + h * rows + n * 128
            out_ref[at : at + 128] = values[:, n * 128 : (n + 1) * 128]


def aside_kernel(where_ref, weight_ref, feature_ref, out_ref):
    count, lines, feat = out_ref.shape
    rows, width = feature_ref.shape
    slot = weight_ref.shape[1] // count
    part = width // count
    out_ref[:, :slot] = weight_ref[0].reshape(count, slot, feat)
    spare = jnp.zeros((rows, 2 * feat - part), bf16)
    for j in range(count):
        pieces = [feature_ref[:, s * part + j * slot : s * part + (j + 1) * slot] for s in range(count)]
        joined = jnp.concatenate(pieces + [spare], axis=1)
        out_ref[j, slot : slot + rows] = joined[:, :feat]
        out_ref[j, slot + rows :] = joined[:, feat:]


def columns_kernel(where_ref, embed_ref, head_ref, shifts_ref, plain_ref, *refs):
    hidden_out, gate_out, scaled_out, extra_out, embed_out, head_out, shifts_out = refs
    count = 8
    part = embed_ref.shape[2] // count
    slot = part // count
    half = count // 2
    order = [0] + [count - d for d in range(1, half)] + list(range(1, half + 1))
    for f in range(count):

        @pl.when(where_ref[2] == f)
        def _(f=f):
            sources = [(embed_ref.at[0], embed_out), (head_ref.at[0], head_out)]
            sources += [(shifts_ref.at[i], shifts_out.at[i]) for i in range(shifts_ref.shape[0])]
            for source, target in sources:
                pieces = []
                for d in order:
                    owner = lax.rem(where_ref[1] + d, count)
                    block = source[:, pl.ds(pl.multiple_of(owner * part, 128), part)]
                    pieces.append(block[:, f * slot : (f + 1) * slot])
                target[...] = jnp.concatenate(pieces, axis=1)

    latent_dim = embed_out.shape[0]
    hidden_out[...] = dot(embed_out[...], plain_ref[...], ((0,), (0,)))
    gate_out[...] = jnp.broadcast_to(shifts_out[2], (128, shifts_out.shape[2])).T
    plain_head = head_out[...].astype(f32)
    head = (plain_head * (1.0 + shifts_out[4])).astype(bf16)
    scaled_out[...] = head
    sums = jnp.sum(head.astype(f32), axis=1, keepdims=True)
    consts = jnp.sum(plain_head * shifts_out[3], axis=1, keepdims=True)
    place = lax.broadcasted_iota(jnp.int32, (latent_dim, 128), 1)
    extra = jnp.zeros((latent_dim, 128), f32)
    for n, column in enumerate(halves(sums) + halves(consts)):
        extra = jnp.where(place == n, column, extra)
    extra = jnp.concatenate([extra, jnp.zeros_like(extra)], axis=0).T
    extra_out[...] = extra[:16].astype(bf16)


def fold_keys(heads, carry, queries, keys, values):
    scores = [dot(keys(h), queries[h], ((1,), (0,))) for h in range(heads)]
    new = []
    for h in range(heads):
        top, total, weighted = carry[h]
        new_top = jnp.maximum(top, jnp.max(scores[h], axis=0, keepdims=True))
        weights = jnp.exp2(scores[h] - new_top)
        keep = jnp.exp2(top - new_top)
        total = total * keep + jnp.sum(weights, axis=0, keepdims=True)
        weighted = weighted * keep + dot(values(h), weights.astype(bf16), ((1,), (0,)))
        new.append((new_top, total, weighted))
    return tuple(new)


def attention_kernel(heads, latent_dim, where_ref, *refs):
    block_refs, (out_ref, all_ref, key_ref, value_ref, sems) = refs[:-5], refs[-5:]
    count, lines, _ = all_ref.shape
    rows = out_ref.shape[2]
    size = heads * rows
    at = [(n, 0, ref.shape[0]) for n, ref in enumerate(block_refs[:-1])]
    at.append((count - 1, block_refs[-2].shape[0], block_refs[-1].shape[0]))
    early, late = [], []
    for ref, (n, place, length) in zip(block_refs, at):
        for first, last, group in ((0, 2 * size, late), (2 * size, lines, early)):
            first, last = max(first, place), min(last, place + length)
            if first < last:
                group.append(
                    pltpu.make_async_copy(
                        ref.at[pl.ds(first - place, last - first)],
                        all_ref.at[n, pl.ds(first, last - first)],
                        sems.at[len(early) + len(late)],
                    )
                )
    for copy in early + late:
        copy.start()
    for copy in early:
        copy.wait()

    tables, base = [], 2 * size
    for i in range(3):
        at = slice(base + i * heads * latent_dim, base + (i + 1) * heads * latent_dim)
        total = sum(all_ref[n, at].astype(f32) for n in range(count)).astype(bf16)
        tables.append([total[h * latent_dim : (h + 1) * latent_dim] for h in range(heads)])
    tail = base + 3 * heads * latent_dim
    ends = tail + rows // 128 * latent_dim
    shift = sum(all_ref[n, ends:].astype(f32) for n in range(count))
    columns = jnp.concatenate([shift, jnp.zeros((112, 128), f32)], axis=0).T
    latents = jnp.concatenate(
        [
            all_ref[n, tail + i * latent_dim : tail + (i + 1) * latent_dim]
            for n in range(count)
            for i in range(rows // 128)
        ],
        axis=1,
    )
    scale = HEAD_DIM ** (-0.5) * LOG2E
    queries = [
        ((dot(tables[0][h], latents[:, :rows], ((0,), (0,))) + columns[:, h : h + 1]) * scale).astype(bf16)
        for h in range(heads)
    ]
    for h in range(heads):
        at = heads + h
        key_ref[h] = (dot(latents, tables[1][h], ((0,), (0,))) + shift[at : at + 1]).astype(bf16)
        at = 2 * heads + h
        value_ref[h] = (dot(tables[2][h], latents, ((0,), (0,))) + columns[:, at : at + 1]).astype(bf16)
    carry = tuple(
        (jnp.full((1, rows), -1e30, f32), jnp.zeros((1, rows), f32), jnp.zeros((HEAD_DIM, rows), f32))
        for _ in range(heads)
    )
    step = 4 * rows
    for i in range(count // 4):
        at = slice(i * step, (i + 1) * step)
        carry = fold_keys(heads, carry, queries, lambda h: key_ref[h, at], lambda h: value_ref[h, :, at])
    for copy in late:
        copy.wait()
    for i in range(count // 4):
        here = range(4 * i, 4 * i + 4)
        carry = fold_keys(
            heads,
            carry,
            queries,
            lambda h: jnp.concatenate([all_ref[n, h * rows : (h + 1) * rows] for n in here], axis=0),
            lambda h: jnp.concatenate(
                [
                    all_ref[n, size + h * rows + j : size + h * rows + j + 128]
                    for n in here
                    for j in range(0, rows, 128)
                ],
                axis=1,
            ),
        )
    for h in range(heads):
        _, total, weighted = carry[h]
        attended = (weighted / total).astype(bf16)
        out_ref[:, h * HEAD_DIM : (h + 1) * HEAD_DIM] = jnp.broadcast_to(
            attended[None], (out_ref.shape[0], HEAD_DIM, rows)
        )


def halves(value):
    high = value.astype(bf16).astype(f32)
    return high, value - high


def head_kernel(sections, where_ref, hidden_ref, gate_ref, head_ref, extra_ref, att_ref, *refs):
    weight_refs, out_ref = refs[:-1], refs[-1]
    n_fsdp, _, rows = att_ref.shape
    latent_dim = head_ref.shape[0]
    mixed = None
    for f in range(n_fsdp):
        whole = [ref[f] for ref in weight_refs[:-2]]
        whole.append(weight_refs[-2][f] if f < n_fsdp // 2 else weight_refs[-1][f - n_fsdp // 2])
        part = dot(jnp.concatenate(whole, axis=0), att_ref[f], ((1,), (0,)))
        mixed = part if mixed is None else mixed + part
    residual = hidden_ref[...] + gate_ref[:, :1] * mixed
    centre = jnp.mean(residual, axis=0, keepdims=True)
    residual = residual - centre
    spread = jnp.sum(residual * residual, axis=0, keepdims=True)
    values = dot(head_ref[...], residual.astype(bf16), ((1,), (0,)))
    spare = jnp.zeros((latent_dim - 4, rows), f32)
    values = jnp.concatenate([values, *halves(centre), *halves(spread), spare], axis=0).T.astype(bf16)
    extra = extra_ref[...]
    piece = rows // n_fsdp
    for f in range(n_fsdp):
        for s in range(sections):
            out_ref[s * n_fsdp + f, :piece] = values[f * piece : (f + 1) * piece]
            out_ref[s * n_fsdp + f, piece:] = extra


def estimate_kernel(sections, width, where_ref, levels_ref, partial_ref, student_ref, noised_ref, group_ref, grad_ref, out_ref):
    piece, latent_dim = student_ref.shape
    count = partial_ref.shape[0] // sections
    estimates = []
    for p in range(sections):
        blocks = [partial_ref[p * count + i].astype(f32) for i in range(count)]

        def column(b, n):
            at = latent_dim + n
            return b[:piece, at : at + 1] + b[:piece, at + 1 : at + 2]

        def line(b, n):
            at = piece + n
            return b[at : at + 1, :latent_dim] + b[at + 1 : at + 2, :latent_dim]

        means = [column(b, 0) for b in blocks]
        mean = sum(means) / count
        linear, spread, shift = 0.0, 0.0, 0.0
        for b, m in zip(blocks, means):
            offset = m - mean
            linear += b[:piece, :latent_dim] + offset * line(b, 0)
            spread += column(b, 2) + (width // count) * (offset * offset)
            shift += line(b, 2)
        velocity = linear * lax.rsqrt(spread / width + 1e-06) + shift
        latent = (student_ref if p == 0 else noised_ref)[...].astype(f32)
        estimates.append(latent - levels_ref[0 if p == 0 else 1] * velocity)
    group_ref[...] = estimates[0]
    teacher = estimates[2] + guidance_scale * (estimates[1] - estimates[2])
    grad = estimates[3] - teacher
    grad_ref[...] = grad
    velocity_grad = -levels_ref[2] * grad
    padded = jnp.concatenate([velocity_grad, jnp.zeros_like(velocity_grad)], axis=1).astype(bf16)
    out_ref[...] = jnp.broadcast_to(padded[None], out_ref.shape)


def gradient_kernel(where_ref, grad_ref, feature_ref, out_ref):
    count, lines, pair = out_ref.shape
    rows = grad_ref.shape[1]
    slot = feature_ref.shape[1] - 2 * rows
    latent_dim, half = pair // 2, slot // 2
    grads = grad_ref[...].reshape(-1, grad_ref.shape[2])
    joined = jnp.concatenate(
        [
            dot(feature_ref[:, at : at + rows].reshape(count * rows, -1), grads, ((0,), (0,)))[:, :latent_dim]
            for at in (slot, slot + rows)
        ],
        axis=0,
    )
    spare = jnp.zeros((lines - half, pair), f32)
    for i in range(count):
        at = i * slot
        block = jnp.concatenate([joined[at : at + half], joined[at + half : at + slot]], axis=1)
        out_ref[i] = jnp.concatenate([block, spare], axis=0).astype(bf16)


def sum_kernel(where_ref, part_ref, out_ref):
    latent_dim, slot = out_ref.shape
    total = part_ref[0].astype(f32)
    for i in range(1, part_ref.shape[0]):
        total += part_ref[i].astype(f32)
    half = slot // 2
    out_ref[...] = jnp.concatenate([total[:half, :latent_dim], total[:half, latent_dim:]], axis=0).T


def per_device(
    student_input,
    previous_latent,
    score_noise,
    timesteps,
    modulation,
    in_weight,
    qkv_weight,
    out_weight,
    head_weight,
    kv_cache,
    saved_features,
):
    section, me_seq, me_fsdp = (lax.axis_index(a) for a in ("section", "seq", "fsdp"))
    sections, n_seq, n_fsdp = (lax.axis_size(a) for a in ("section", "seq", "fsdp"))
    model_index = section - (section >= 2).astype(jnp.int32)
    where = jnp.concatenate([jnp.stack([model_index, me_seq, me_fsdp, section]).astype(jnp.int32), timesteps])
    levels = noise_levels(timesteps)
    rows, latent_dim = student_input.shape
    width = in_weight.shape[2]
    depth, feat = qkv_weight.shape[1], qkv_weight.shape[3]
    heads = feat // HEAD_DIM
    piece = rows // n_fsdp
    shifts = modulation.transpose(1, 0, 2)
    slot = depth // n_fsdp

    lines = (2 * rows + 3 * latent_dim) * heads + rows // 128 * latent_dim + 16
    own, plain = run(
        prepare_kernel,
        timesteps,
        [((lines, HEAD_DIM), bf16), ((latent_dim, rows), bf16)],
        in_weight,
        qkv_weight.transpose(0, 2, 1, 3),
        shifts,
        student_input.T,
        previous_latent.T,
        score_noise.T,
        kv_cache[0],
        raw=range(7),
        scratch=[
            pltpu.VMEM((1, latent_dim, width), bf16),
            pltpu.VMEM((1, 3, depth, feat), bf16),
            pltpu.VMEM(shifts.shape, f32),
            pltpu.VMEM((latent_dim, rows), bf16),
            pltpu.VMEM((latent_dim, rows), bf16),
            pltpu.VMEM((latent_dim, rows), bf16),
            pltpu.VMEM((rows, 2, feat), bf16),
            pltpu.SemaphoreType.DMA((7,)),
        ],
        room=60,
    )
    cut = run(aside_kernel, together(where, own), [((n_fsdp, slot + 2 * piece, feat), bf16)], out_weight, saved_features, picked=(0,))
    aside = exchange(cut, "fsdp")
    hidden, gate, head_here, extra = run(
        columns_kernel,
        together(where, own),
        [
            ((depth, rows), f32),
            ((depth, 128), f32),
            ((latent_dim, depth), bf16),
            ((16, 128), bf16),
        ],
        in_weight,
        head_weight.transpose(0, 2, 1),
        shifts,
        plain,
        picked=(0, 1),
        scratch=[
            pltpu.VMEM((latent_dim, depth), bf16),
            pltpu.VMEM((latent_dim, depth), bf16),
            pltpu.VMEM((shifts.shape[0], 1, depth), f32),
        ],
    )
    around = Ring(own, "seq", n_seq, 0, lines // 32 * 16)
    around.step()
    block, *_ = lax.optimization_barrier((aside[:, :slot],) + around.ends())
    weights = Ring(block, "seq", n_seq, 0)
    weights.step()
    around.step()
    around.step()
    weights.after(around)
    around.finish()
    weights.step()
    blocks = around.blocks()
    attended = run(
        functools.partial(attention_kernel, heads, latent_dim),
        together(where, hidden),
        [((n_fsdp, feat, rows), bf16)],
        *blocks,
        scratch=[
            pltpu.VMEM((n_seq, lines, HEAD_DIM), bf16),
            pltpu.VMEM((heads, n_seq * rows, HEAD_DIM), bf16),
            pltpu.VMEM((heads, HEAD_DIM, n_seq * rows), bf16),
            pltpu.SemaphoreType.DMA((2 * len(blocks),)),
        ],
        raw=range(len(blocks)),
        cost=pl.CostEstimate(flops=11 * 10**9, bytes_accessed=20 * 10**6, transcendentals=3 * 10**6),
    )
    attended = exchange(together(attended, *weights.ends()), "fsdp")
    weights.finish()
    partials = run(
        functools.partial(head_kernel, sections),
        where,
        [((sections * n_fsdp, piece + 16, 128), bf16)],
        hidden,
        gate,
        head_here,
        extra,
        attended,
        *weights.blocks(),
    )
    partials = exchange(partials, ("section", "fsdp"))

    noised = (
        (1.0 - levels[1]) * previous_latent.astype(f32) + levels[1] * score_noise.astype(f32)
    ).astype(bf16)
    own_student = lax.dynamic_slice_in_dim(student_input, me_fsdp * piece, piece, 0)
    own_noised = lax.dynamic_slice_in_dim(noised, me_fsdp * piece, piece, 0)
    student_group, dmd_grad, grads = run(
        functools.partial(estimate_kernel, sections, width),
        where,
        [((piece, latent_dim), f32), ((piece, latent_dim), f32), ((n_fsdp, piece, 2 * latent_dim), bf16)],
        levels,
        partials,
        own_student,
        own_noised,
    )
    grads = exchange(grads, "fsdp")
    partial_grad = run(
        gradient_kernel, where, [((n_seq, (slot // 2 + 15) // 16 * 16, 2 * latent_dim), bf16)], grads, aside
    )
    head_grad = run(sum_kernel, where, [((latent_dim, slot), f32)], exchange(partial_grad, "seq")).T
    return (student_group, dmd_grad, head_grad)


def solution(mesh):
    placed = (
        P("seq", None),
        P("seq", None),
        P("seq", None),
        P(),
        P("section", None, None),
        P(),
        P(None, "seq", None, "fsdp"),
        P(None, "seq", "fsdp"),
        P(),
        P("section", "seq", None, "fsdp"),
        P(("seq", "fsdp"), None),
    )
    return jax.shard_map(
        per_device,
        mesh=mesh,
        in_specs=placed,
        out_specs=(P(("seq", "fsdp"), None), P(("seq", "fsdp"), None), P(("seq", "fsdp"), None)),
        check_vma=False,
    )
```
